32 devices in a mesh: dp: 8 (over z, x), mp: 4 (over y, core).
Axes of the slice: x: 2, y: 2, z: 4, core: 2. Of those that a mesh axis runs over, the one named last changes fastest.
Arguments:
- inputs: bfloat16 [24, 2048, 256], P('dp', 'mp'), may hold values from -6 to 6
- segments: int32 [24, 2048], P('dp', 'mp'), may hold values from 0 to 512, as said below
- w_qkv: bfloat16 [3, 256, 256], P(None, None, 'mp'), may hold values from -0.375 to 0.375
- b_qv: bfloat16 [2, 256], P(None, 'mp'), may hold values from -3 to 3
- w_out: bfloat16 [256, 256], P('mp'), may hold values from -2 to 2
- b_out: bfloat16 [256], replicated, may hold values from -3 to 3
- gain_one: float32 [256], replicated, may hold values from 0.1 to 1.9
- shift_one: float32 [256], replicated, may hold values from -2 to 2
- w_in: bfloat16 [256, 512], P(None, 'mp'), may hold values from -0.375 to 0.375
- b_in: bfloat16 [512], P('mp'), may hold values from -3 to 3
- w_back: bfloat16 [512, 256], P('mp'), may hold values from -0.375 to 0.375
- b_back: bfloat16 [256], replicated, may hold values from -3 to 3
- gain_two: float32 [256], replicated, may hold values from 0.1 to 1.9
- shift_two: float32 [256], replicated, may hold values from -2 to 2
- cotangent: bfloat16 [24, 2048, 256], P('dp', 'mp'), may hold values from -6 to 6
Outputs:
- result: bfloat16 [24, 2048, 256], P('dp', 'mp')
- grad_inputs: float32 [24, 2048, 256], P('dp', 'mp')
- grad_qkv: float32 [3, 256, 256], P(None, None, 'mp')
- grad_bias_qv: float32 [2, 256], P(None, 'mp')
- grad_w_out: float32 [256, 256], P('mp')
- grad_b_out: float32 [256], replicated
- grad_gain_one: float32 [256], replicated
- grad_shift_one: float32 [256], replicated
- grad_w_in: float32 [256, 512], P(None, 'mp')
- grad_b_in: float32 [512], P('mp')
- grad_w_back: float32 [512, 256], P('mp')
- grad_b_back: float32 [256], replicated
- grad_gain_two: float32 [256], replicated
- grad_shift_two: float32 [256], replicated
The draws below stay inside these ranges and needn't reach their ends.
Inputs may be any that keep to these rules, and one draw needn't show every extreme that they name: `segments`: cell numbers start at 0 in every row and never fall along it; in every row one cell covers positions 256 to 1791.
All inputs are finite; a program needn't handle non-finite values.
Results may differ from the reference program's by a relative error of at most 0.017.
Values may be sent and summed in bfloat16 or wider, within the bound.
No kernel may reach another device: no remote copies, remote signals or barrier semaphores. Data moves between devices by JAX's collectives and lax.ppermute only.
A program may use at most 128 MiB of HBM per device.

```python
import jax
import jax.numpy as jnp
from jax import lax

D = 256
HEADS = 4
FF = 512
LENGTH = 2048
ROWS = 24


def draw_segments(key, part):
    key = jax.random.fold_in(key, 11)
    key_start, key_end, key_flag, key_pick = jax.random.split(key, 4)
    chosen = jax.random.randint(key_pick, (), 0, ROWS)
    row_ids = jnp.arange(ROWS, dtype=jnp.int32)[:, None]
    picked = row_ids == chosen
    start = jax.random.randint(key_start, (ROWS, 1), 0, LENGTH // 8 + 1)
    finish = jax.random.randint(key_end, (ROWS, 1), 7 * LENGTH // 8, LENGTH + 1)
    start = jnp.where(picked, LENGTH // 8, start)
    finish = jnp.where(picked, 7 * LENGTH // 8, finish)
    flags = (jax.random.randint(key_flag, (ROWS, LENGTH), 0, 48) == 0).astype(jnp.int32)
    place = jnp.arange(LENGTH, dtype=jnp.int32)[None, :]
    inside = (place > start) & (place < finish)
    flags = jnp.where(picked, 1, flags)
    flags = jnp.where(inside, 0, flags)
    flags = jnp.where((place == start) | (place == finish), 1, flags)
    flags = jnp.where(place == 0, 0, flags)
    return jnp.cumsum(flags, axis=1).astype(jnp.int32)


def levels(own_key, shape, pieces, low, high):
    loudness = 1.0
    for dim, shards_of in pieces:
        steps = jax.random.uniform(jax.random.fold_in(jax.random.fold_in(own_key, 6), dim), (shards_of,), jnp.float32, low / len(pieces), high / len(pieces))
        loudness = loudness * jnp.repeat(jnp.exp(steps), shape[dim] // shards_of).reshape((-1,) + (1,) * (len(shape) - 1 - dim))
    return loudness


def noise(stream_key, dims, scale, reach, cuts=(), kind=jnp.bfloat16):
    result = scale * jax.random.normal(stream_key, dims, jnp.float32)
    if cuts:
        result = result * levels(stream_key, dims, cuts, -0.22, 0.18)
    return jnp.clip(result, -reach, reach).astype(kind)


def setup_inputs(seed: int = 0) -> dict:
    streams_of = jax.random.split(jax.random.key(seed), 16)
    inputs = noise(streams_of[0], (ROWS, LENGTH, D), 1.0, 6.0, ((0, 8), (1, 4)))
    segments = draw_segments(jax.random.fold_in(streams_of[15], 71), 0)
    w_qkv = noise(streams_of[2], (3, D, D), D ** -0.5, 0.375, ((2, 4),))
    b_qv = noise(streams_of[3], (2, D), 0.5, 3.0, ((1, 4),))
    w_out = noise(streams_of[4], (D, D), (D // 32) ** -0.5, 2.0, ((0, 4),))
    b_out = noise(streams_of[5], (D,), 0.5, 3.0)
    gain_one = jnp.clip(1.0 + 0.18 * jax.random.normal(streams_of[6], (D,), jnp.float32), 0.1, 1.9)
    shift_one = noise(streams_of[7], (D,), 0.3, 2.0, (), jnp.float32)
    w_in = noise(streams_of[8], (D, FF), D ** -0.5, 0.375, ((1, 4),))
    b_in = noise(streams_of[9], (FF,), 0.5, 3.0, ((0, 4),))
    w_back = noise(streams_of[10], (FF, D), (FF // 2) ** -0.5, 0.375, ((0, 4),))
    b_back = noise(streams_of[11], (D,), 0.5, 3.0)
    gain_two = jnp.clip(1.0 + 0.18 * jax.random.normal(streams_of[12], (D,), jnp.float32), 0.1, 1.9)
    shift_two = noise(streams_of[13], (D,), 0.3, 2.0, (), jnp.float32)
    cotangent = noise(streams_of[14], (ROWS, LENGTH, D), 1.0, 6.0, ((0, 8), (1, 4)))
    return dict(inputs=inputs, segments=segments, w_qkv=w_qkv, b_qv=b_qv, w_out=w_out, b_out=b_out, gain_one=gain_one, shift_one=shift_one, w_in=w_in, b_in=b_in, w_back=w_back, b_back=b_back, gain_two=gain_two, shift_two=shift_two, cotangent=cotangent)


eps = 1e-06
HIGH = lax.Precision.HIGHEST

@jax.custom_vjp
def low(v):
    return lax.optimization_barrier(v.astype(jnp.bfloat16)).astype(jnp.float32)

@jax.custom_vjp
def low_back(v):
    return v

def low_keep(v):
    return (low(v), None)

def low_pass(kept, grad):
    return (grad,)

def back_keep(v):
    return (v, None)

def back_low(kept, grad):
    return (low(grad),)
low.defvjp(low_keep, low_pass)
low_back.defvjp(back_keep, back_low)

def layer_norm(hidden, gain, shift):
    centre = hidden - lax.optimization_barrier(jnp.mean(hidden, axis=-1, keepdims=True))
    spread = lax.optimization_barrier(jnp.mean(centre * centre, axis=-1, keepdims=True))
    return centre * lax.rsqrt(spread + eps) * gain + shift

def attend(keys, values, cells, query_block, cell_block):
    scale = query_block.shape[-1] ** (-0.5)
    scores = jnp.einsum('qhd,khd->hqk', query_block, keys, precision=HIGH) * scale
    scores = low_back(scores)
    same = (cell_block[:, None] == cells[None, :])[None]
    scores = jnp.where(same, scores, -1e+30)
    probs = jax.nn.softmax(scores, axis=-1)
    return jnp.einsum('hqk,khd->qhd', low(probs), values, precision=HIGH)

def forward(rowin, cells, w_qkv, b_qv, w_out, b_out, gain_one, shift_one, w_in, b_in, w_back, b_back, gain_two, shift_two):
    length, width = rowin.shape
    head_dim = width // HEADS
    proj = jnp.einsum('td,cde->cte', rowin, w_qkv, precision=HIGH)
    query = low(low_back(proj[0] + b_qv[0])).reshape(length, HEADS, head_dim)
    keys = low(low_back(proj[1])).reshape(length, HEADS, head_dim)
    values = low(low_back(proj[2] + b_qv[1])).reshape(length, HEADS, head_dim)
    block = min(512, length)
    count = length // block
    q_blocks = query.reshape(count, block, HEADS, head_dim)
    c_blocks = cells.reshape(count, block)

    def one_block(args):
        return jax.checkpoint(attend)(keys, values, cells, args[0], args[1])
    attended = lax.map(one_block, (q_blocks, c_blocks)).reshape(length, width)
    attended = low(low_back(attended))
    branch = low_back(jnp.dot(attended, w_out, precision=HIGH))
    hidden_one = rowin + branch + b_out
    normed = layer_norm(hidden_one, gain_one, shift_one)
    pre = low_back(jnp.dot(low(normed), w_in, precision=HIGH) + b_in)
    act = low(jax.nn.gelu(pre, approximate=True))
    feed = low_back(jnp.dot(act, w_back, precision=HIGH))
    hidden_two = normed + feed + b_back
    return layer_norm(hidden_two, gain_two, shift_two)

def reference(inputs, segments, w_qkv, b_qv, w_out, b_out, gain_one, shift_one, w_in, b_in, w_back, b_back, gain_two, shift_two, cotangent):
    params = tuple((p.astype(jnp.float32) for p in (w_qkv, b_qv, w_out, b_out, gain_one, shift_one, w_in, b_in, w_back, b_back, gain_two, shift_two)))

    def one_row(carry, row):
        rowin, cells, cot = row

        def apply(xx, *pp):
            return forward(xx, cells, *pp)
        out, pull = jax.vjp(apply, rowin.astype(jnp.float32), *params)
        grads = pull(cot.astype(jnp.float32))
        carry = tuple((a + b for a, b in zip(carry, grads[1:])))
        return (carry, (out.astype(jnp.bfloat16), grads[0]))
    zeros = tuple((jnp.zeros(p.shape, jnp.float32) for p in params))
    sums, (outs, grad_in) = lax.scan(one_row, zeros, (inputs, segments, cotangent))
    return (outs, grad_in, sums[0], sums[1], sums[2], sums[3], sums[4], sums[5], sums[6], sums[7], sums[8], sums[9], sums[10], sums[11])
```

```python
import functools

import jax
import jax.numpy as jnp
from jax import lax
from jax.experimental import pallas as pl
from jax.experimental.pallas import tpu as pltpu
from jax.sharding import PartitionSpec as P

HEADS = 4
EPS = 1e-06
FAR = -(2.0**99)
GELU_C = 0.7978845608028654
GELU_A = 0.044715

BF = jnp.bfloat16
F32 = jnp.float32

NN = (((1,), (0,)), ((), ()))
NT = (((1,), (1,)), ((), ()))
TN = (((0,), (0,)), ((), ()))

MB = 2**20


def mm(left, right, dims):
    return lax.dot_general(left, right, dims, preferred_element_type=F32)


def vmem():
    return pl.BlockSpec(memory_space=pltpu.VMEM)


def params(limit):
    return pltpu.CompilerParams(vmem_limit_bytes=limit * MB)


def pack_kernel(w_qkv, b_qv, w_out, w_in, b_in, w_back, one, two):
    width = w_qkv.shape[2]
    units = w_in.shape[1]
    for c in range(3):
        one[c * width : (c + 1) * width, :] = w_qkv[c].astype(F32).T.astype(BF)
    one[3 * width :, :] = jnp.zeros((16, one.shape[1]), BF)
    one[3 * width : 3 * width + 1, 0:width] = b_qv[0:1, :]
    one[3 * width : 3 * width + 1, width : 2 * width] = b_qv[1:2, :]
    two[0:width, :] = w_out[...]
    two[width : width + units, :] = w_in[...].astype(F32).T.astype(BF)
    two[width + units : width + 2 * units, :] = w_back[...]
    two[width + 2 * units :, :] = jnp.zeros((16, two.shape[1]), BF)
    two[width + 2 * units : width + 2 * units + 1, 0:units] = b_in[...]


def pack(w_qkv, b_qv, w_out, w_in, b_in, w_back):
    width, units, model = w_qkv.shape[2], w_in.shape[1], w_in.shape[0]
    return pl.pallas_call(
        pack_kernel,
        out_shape=[
            jax.ShapeDtypeStruct((3 * width + 16, model), BF),
            jax.ShapeDtypeStruct((width + 2 * units + 16, model), BF),
        ],
        in_specs=[vmem()] * 6,
        out_specs=[vmem()] * 2,
        name="pack",
    )(w_qkv, b_qv, w_out, w_in, b_in.reshape(1, units), w_back)


def forward_kernel(parts, *refs):
    xs, segs, ws = refs[:parts], refs[parts : 2 * parts], refs[2 * parts : 3 * parts]
    e_out, kt_out, vt_out, qt_out, o_out, stack, feats, qfeat = refs[3 * parts :]
    head = pl.program_id(0)
    here = xs[0].shape[1]
    hd = qt_out.shape[1]

    @pl.when(head == 0)
    def _():
        for b in range(parts):
            stack[b] = ws[b][...]
            seg = segs[b][0]
            lane = lax.broadcasted_iota(jnp.int32, (hd, here), 0)
            digit = jnp.where(lane < 32, jnp.bitwise_and(seg, 31), jnp.right_shift(seg, 5) + 32)
            same = lane == digit
            feats[:, b * here : (b + 1) * here] = jnp.where(same, 0.0, FAR).astype(BF)
            if b == 0:
                qfeat[...] = same.astype(F32)

    w = stack[head]
    bias = w[3 * hd : 3 * hd + 1, 0 : 2 * hd].astype(F32)
    bias = jnp.broadcast_to(bias, (2 * hd, 2 * hd)).T[:, 0:1]
    kt_out[0, hd:, :] = feats[...]
    rows = lax.broadcasted_iota(jnp.int32, (hd, vt_out.shape[2]), 0)
    vt_out[0, hd:, :] = (rows < 2).astype(F32).astype(BF)
    for b in range(parts):
        cols = slice(b * here, (b + 1) * here)
        if b == 0:
            proj = mm(w[: 3 * hd], xs[b][0], NT)
            qt = (proj[:hd] + bias[:hd]).astype(BF).astype(F32) * (hd**-0.5)
            qt_out[0] = qt.astype(BF)
            proj = proj[hd:]
        else:
            proj = mm(w[hd : 3 * hd], xs[b][0], NT)
        kt_out[0, :hd, cols] = proj[:hd].astype(BF)
        vt_out[0, :hd, cols] = (proj[hd:] + bias[hd:]).astype(BF)
    q = jnp.concatenate([qt, qfeat[...]], axis=0).T.astype(BF)
    chunk = here // 2
    for c in range(2):
        rows = slice(c * chunk, (c + 1) * chunk)
        scores = mm(q[rows], kt_out[0], NN)
        top = jnp.max(scores, axis=-1, keepdims=True)
        expo = jnp.exp(scores - top).astype(BF)
        e_out[0, rows, :] = expo
        o_out[0, rows, :] = mm(expo, vt_out[0], NT)


def attend_forward(blocks, segs, ws, heads):
    parts = len(blocks)
    here, model = blocks[0][0].shape[1:]
    length = parts * here
    hd = model // heads

    def row_spec(arr, r):
        return pl.BlockSpec((1,) + arr.shape[1:], lambda h, r=r: (r, 0, 0))

    flops = heads * (4 * here * length * 2 * hd + 4 * length * hd * model)
    return pl.pallas_call(
        functools.partial(forward_kernel, parts),
        grid=(heads,),
        out_shape=[
            jax.ShapeDtypeStruct((heads, here, length), BF),
            jax.ShapeDtypeStruct((heads, 2 * hd, length), BF),
            jax.ShapeDtypeStruct((heads, 2 * hd, length), BF),
            jax.ShapeDtypeStruct((heads, hd, here), BF),
            jax.ShapeDtypeStruct((heads, here, 2 * hd), F32),
        ],
        in_specs=[row_spec(a, r) for a, r in blocks]
        + [row_spec(a, r) for a, r in segs]
        + [pl.BlockSpec(w.shape, lambda h: (0, 0)) for w in ws],
        out_specs=[
            pl.BlockSpec((1, here, length), lambda h: (h, 0, 0)),
            pl.BlockSpec((1, 2 * hd, length), lambda h: (h, 0, 0)),
            pl.BlockSpec((1, 2 * hd, length), lambda h: (h, 0, 0)),
            pl.BlockSpec((1, hd, here), lambda h: (h, 0, 0)),
            pl.BlockSpec((1, here, 2 * hd), lambda h: (h, 0, 0)),
        ],
        scratch_shapes=[
            pltpu.VMEM((parts,) + ws[0].shape, BF),
            pltpu.VMEM((hd, length), BF),
            pltpu.VMEM((hd, here), F32),
        ],
        compiler_params=params(48),
        cost_estimate=pl.CostEstimate(
            flops=flops, bytes_accessed=14 * MB, transcendentals=heads * here * length
        ),
        name="attend_forward",
    )(*[a for a, _ in blocks], *[a for a, _ in segs], *ws)


def middle_kernel(parts, heads, *refs):
    o_in, x_in, cot_in = refs[:3]
    ws = refs[3 : 3 + parts]
    b_out, g_one, e_one, b_back, g_two, e_two, grads_in, sums_in = refs[3 + parts : 11 + parts]
    result_out, dh1_out, do_out, grads_out, sums_out = refs[11 + parts : 16 + parts]
    w_out, w_pad, w_in, w_back = refs[16 + parts :]
    model = x_in.shape[2]
    hd = model // heads
    per = w_out.shape[0] // parts
    units = w_in.shape[0] // parts
    w_pad[...] = jnp.zeros(w_pad.shape, BF)
    bias = []
    for b in range(parts):
        w_out[b * per : (b + 1) * per, :] = ws[b][0:per, :]
        w_pad[b * 2 * per : b * 2 * per + per, :] = ws[b][0:per, :]
        w_in[b * units : (b + 1) * units, :] = ws[b][per : per + units, :]
        w_back[b * units : (b + 1) * units, :] = ws[b][per + units : per + 2 * units, :]
        bias.append(ws[b][per + 2 * units : per + 2 * units + 1, 0:units].astype(F32))
    b_in = jnp.concatenate(bias, axis=1)

    lane = lax.broadcasted_iota(jnp.int32, o_in.shape[1:], 1)
    inv = [1.0 / o_in[h][:, hd : hd + 1] for h in range(heads)]
    normal = [o_in[h] * inv[h] for h in range(heads)]
    tiles = [
        jnp.where(lane < hd, normal[h], pltpu.roll(normal[h + 1], hd, 1))
        for h in range(0, heads, 2)
    ]
    att = jnp.concatenate(tiles, axis=1).astype(BF)
    x = x_in[0].astype(F32)
    h1 = x + mm(att, w_out[...], NN) + b_out[...].astype(F32)

    def norm(h):
        centre = h - jnp.mean(h, axis=-1, keepdims=True)
        rstd = lax.rsqrt(jnp.mean(centre * centre, axis=-1, keepdims=True) + EPS)
        return centre * rstd, rstd

    def norm_back(dy, gain, unit, rstd):
        dn = dy * gain
        mean = jnp.mean(dn, axis=-1, keepdims=True)
        along = jnp.mean(dn * unit, axis=-1, keepdims=True)
        return rstd * (dn - mean - unit * along)

    def down(v):
        return jnp.sum(v, axis=0, keepdims=True)

    n1, rstd1 = norm(h1)
    y1 = n1 * g_one[...] + e_one[...]
    y1b = y1.astype(BF)
    pre = mm(y1b, w_in[...], NT) + b_in
    square = pre * pre
    th = jnp.tanh(GELU_C * pre * (1.0 + GELU_A * square))
    half = 0.5 * (1.0 + th)
    act = (pre * half).astype(BF)
    slope = half + 0.5 * pre * (1.0 - th * th) * (GELU_C * (1.0 + 3.0 * GELU_A * square))
    h2 = y1 + mm(act, w_back[...], NN) + b_back[...].astype(F32)
    n2, rstd2 = norm(h2)
    result_out[0] = (n2 * g_two[...] + e_two[...]).astype(BF)
    cot = cot_in[0].astype(F32)
    dh2 = norm_back(cot, g_two[...], n2, rstd2)
    dz = dh2.astype(BF)
    dact = mm(dz, w_back[...], NT)
    dpre = (dact * slope).astype(BF)
    dw_back = mm(act, dz, TN)
    dw_in = mm(dpre, y1b, TN)
    db_in = down(dpre.astype(F32))
    dy1 = mm(dpre, w_in[...], NN) + dh2
    dh1 = norm_back(dy1, g_one[...], n1, rstd1)
    dh1_out[0] = dh1
    da = dh1.astype(BF)
    dw_out = mm(att, da, TN)
    dwide = mm(da, w_pad[...], NT)
    for h in range(heads):
        grad = (dwide[:, 2 * hd * h : 2 * hd * (h + 1)] * inv[h]).astype(BF)
        wide = grad.astype(F32)
        inner = jnp.sum(wide * normal[h], axis=-1, keepdims=True)
        high = inner.astype(BF).astype(F32)
        rest = inner - high
        wide = jnp.where(lane == hd, -high, jnp.where(lane == hd + 1, -rest, wide))
        do_out[h] = wide.astype(BF)
    for b in range(parts):
        grads_out[b, 0:per, :] = grads_in[b, 0:per, :] + dw_out[b * per : (b + 1) * per]
        here = slice(per, per + units)
        grads_out[b, here, :] = grads_in[b, here, :] + dw_in[b * units : (b + 1) * units]
        here = slice(per + units, per + 2 * units)
        grads_out[b, here, :] = grads_in[b, here, :] + dw_back[b * units : (b + 1) * units]
        grads_out[b, per + 2 * units :, :] = grads_in[b, per + 2 * units :, :]
        here = slice(per + 2 * units, per + 2 * units + 1)
        grads_out[b, here, 0:units] = (
            grads_in[b, here, 0:units] + db_in[:, b * units : (b + 1) * units]
        )
    rows = [down(dh1), down(dy1 * n1), down(dy1), down(dh2), down(cot * n2), down(cot)]
    for i, row in enumerate(rows):
        sums_out[i : i + 1, :] = sums_in[i : i + 1, :] + row
    sums_out[len(rows) :, :] = jnp.zeros((8 - len(rows), model), F32)


def middle(r, o, inputs, cotangent, ws, vectors, grads, sums, heads):
    parts = len(ws)
    here, model = inputs.shape[1:]
    per = grads.shape[1] - 16
    width = model // parts
    units = (per - width) // 2
    row = pl.BlockSpec((1, here, model), lambda i, r=r: (r, 0, 0))
    out_row = pl.BlockSpec((1, here, model), lambda i: (0, 0, 0))

    def whole(a):
        return pl.BlockSpec(a.shape, lambda i, n=len(a.shape): (0,) * n)

    do_shape = jax.ShapeDtypeStruct((heads, here, 2 * (model // heads)), BF)
    return pl.pallas_call(
        functools.partial(middle_kernel, parts, heads),
        grid=(1,),
        out_shape=[
            jax.ShapeDtypeStruct((1, here, model), BF),
            jax.ShapeDtypeStruct((1, here, model), F32),
            do_shape,
            jax.ShapeDtypeStruct(grads.shape, F32),
            jax.ShapeDtypeStruct(sums.shape, F32),
        ],
        in_specs=[whole(o), row, row]
        + [whole(a) for a in ws]
        + [whole(a) for a in vectors]
        + [whole(grads), whole(sums)],
        out_specs=[out_row, out_row, whole(do_shape), whole(grads), whole(sums)],
        scratch_shapes=[
            pltpu.VMEM((parts * width, model), BF),
            pltpu.VMEM((2 * parts * width, model), BF),
            pltpu.VMEM((parts * units, model), BF),
            pltpu.VMEM((parts * units, model), BF),
        ],
        compiler_params=params(48),
        cost_estimate=pl.CostEstimate(
            flops=6 * here * model * (2 * model + 2 * parts * units),
            bytes_accessed=8 * MB,
            transcendentals=here * parts * units,
        ),
        name="middle",
    )(o, inputs, cotangent, *ws, *vectors, grads, sums)


def backward_kernel(parts, heads, *refs):
    e_in, kt_in, vt_in, qt_in, do_in, dh1_in, grads_in = refs[:7]
    xs, ws = refs[7 : 7 + parts], refs[7 + parts : 7 + 2 * parts]
    dxs = refs[7 + 2 * parts : 7 + 3 * parts]
    grads_out, ds, dkv, dq, w_kv, w_q = refs[7 + 3 * parts :]
    head = pl.program_id(0)
    hd = qt_in.shape[1]
    here = do_in.shape[1]
    chunk = here // 2
    for c in range(2):
        rows = slice(c * chunk, (c + 1) * chunk)
        dp = mm(do_in[0, rows, :], vt_in[0], NN)
        ds[rows, :] = (dp * e_in[0, rows, :].astype(F32)).astype(BF)
    dkv[head, hd:, :] = mm(do_in[0], e_in[0], TN)[:hd].astype(BF)
    dkv[head, :hd, :] = mm(qt_in[0], ds[...], NN).astype(BF)
    dq[head] = (mm(kt_in[0, :hd, :], ds[...], NT) * (hd**-0.5)).astype(BF)

    @pl.when(head == heads - 1)
    def _():
        for b in range(parts):
            w_q[b * hd : (b + 1) * hd, :] = ws[b][0:hd, :]
            w_kv[b * 2 * hd : (b + 1) * 2 * hd, :] = ws[b][hd : 3 * hd, :]
        dq_all = dq[...].reshape(heads * hd, here)
        dkv_all = dkv[...].reshape(heads * 2 * hd, parts * here)
        gkv = jnp.zeros((heads * 2 * hd, xs[0].shape[2]), F32)
        for b in range(parts):
            part = dkv_all[:, b * here : (b + 1) * here]
            dx = mm(part, w_kv[...], TN)
            gkv = gkv + mm(part, xs[b][0], NN)
            if b == 0:
                dx = dx + mm(dq_all, w_q[...], TN) + dh1_in[0]
                dxs[b][...] = dx
            else:
                dxs[b][...] = dx.astype(BF)
        gq = mm(dq_all, xs[0][0], NN)
        bq = mm(jnp.ones((8, here), BF), dq_all, NT)
        bkv = mm(jnp.ones((8, parts * here), BF), dkv_all, NT)
        for b in range(parts):
            grads_out[b, 0:hd, :] = grads_in[b, 0:hd, :] + gq[b * hd : (b + 1) * hd]
            grads_out[b, hd : 3 * hd, :] = (
                grads_in[b, hd : 3 * hd, :] + gkv[b * 2 * hd : (b + 1) * 2 * hd]
            )
            grads_out[b, 3 * hd :, :] = grads_in[b, 3 * hd :, :]
            line = slice(3 * hd, 3 * hd + 1)
            grads_out[b, line, 0:hd] = grads_in[b, line, 0:hd] + bq[0:1, b * hd : (b + 1) * hd]
            grads_out[b, line, hd : 2 * hd] = (
                grads_in[b, line, hd : 2 * hd]
                + bkv[0:1, b * 2 * hd + hd : (b + 1) * 2 * hd]
            )


def attend_backward(saved, dh1, grads, blocks, ws, heads):
    e, kt, vt, qt, do = saved
    parts = len(blocks)
    here, model = blocks[0][0].shape[1:]
    hd = model // heads
    length = parts * here

    def per_head(a):
        return pl.BlockSpec((1,) + a.shape[1:], lambda h: (h, 0, 0))

    def whole(a):
        return pl.BlockSpec(a.shape, lambda h, n=len(a.shape): (0,) * n)

    def row_spec(arr, r):
        return pl.BlockSpec((1,) + arr.shape[1:], lambda h, r=r: (r, 0, 0))

    out_shape = [
        jax.ShapeDtypeStruct((here, model), F32 if b == 0 else BF) for b in range(parts)
    ] + [jax.ShapeDtypeStruct(grads.shape, F32)]
    return pl.pallas_call(
        functools.partial(backward_kernel, parts, heads),
        grid=(heads,),
        out_shape=out_shape,
        in_specs=[per_head(a) for a in saved]
        + [whole(dh1), whole(grads)]
        + [row_spec(a, r) for a, r in blocks]
        + [whole(w) for w in ws],
        out_specs=[whole(s) for s in out_shape],
        scratch_shapes=[
            pltpu.VMEM((here, length), BF),
            pltpu.VMEM((heads, 2 * hd, length), BF),
            pltpu.VMEM((heads, hd, here), BF),
            pltpu.VMEM((heads * 2 * hd, model), BF),
            pltpu.VMEM((heads * hd, model), BF),
        ],
        compiler_params=params(48),
        cost_estimate=pl.CostEstimate(
            flops=heads * (8 * here * length * 2 * hd),
            bytes_accessed=16 * MB,
            transcendentals=0,
        ),
        name="attend_backward",
    )(*saved, dh1, grads, *[a for a, _ in blocks], *ws)


def swap(value, axis, size, bit):
    return lax.ppermute(value, axis, [(i, i ^ bit) for i in range(size)])


def bits_of(size):
    return [1 << k for k in range(size.bit_length() - 1)]


def layer(mesh_sizes, *args):
    (inputs, segments, w_qkv, b_qv, w_out, b_out, gain_one, shift_one) = args[:8]
    (w_in, b_in, w_back, b_back, gain_two, shift_two, cotangent) = args[8:]
    dp, mp = mesh_sizes
    rows, here, model = inputs.shape
    heads = HEADS
    width = w_qkv.shape[2]

    def gather(value):
        got = [value]
        for bit in reversed(bits_of(mp)):
            got = got + [swap(g, "mp", mp, bit) for g in got]
        order = [0]
        for bit in reversed(bits_of(mp)):
            order = order + [o ^ bit for o in order]
        return [got[order.index(i)] for i in range(mp)]

    one, two = pack(w_qkv, b_qv, w_out, w_in, b_in, w_back)
    seg_parts = gather(segments.reshape(rows, 1, here))
    w_one = gather(one)
    first = gather(inputs[0:1])
    w_two = gather(two)
    later = gather(inputs[1:]) if rows > 1 else None

    def block_of(r):
        if r == 0:
            return [(inputs, 0)] + [(a, 0) for a in first[1:]]
        return [(inputs, r)] + [(a, r - 1) for a in later[1:]]

    vectors = [
        v.reshape(1, model) for v in (b_out, gain_one, shift_one, b_back, gain_two, shift_two)
    ]
    saved = [
        attend_forward(block_of(r), [(a, r) for a in seg_parts], w_one, heads) for r in range(rows)
    ]
    grads_two = jnp.zeros((mp,) + two.shape, F32)
    sums = jnp.zeros((8, model), F32)
    results, dh1s, dos = [], [], []
    for r in range(rows):
        res, dh1, do, grads_two, sums = middle(
            r, saved[r][4], inputs, cotangent, w_two, vectors, grads_two, sums, heads
        )
        results.append(res)
        dh1s.append(dh1)
        dos.append(do)

    def halve(pieces, bit_list):
        pieces = list(pieces)
        for bit in bit_list:
            keep = {i: p for i, p in pieces_items(pieces) if not i & bit}
            send = {i: p for i, p in pieces_items(pieces) if i & bit}
            for i in keep:
                got = swap(send[i | bit].astype(BF), "mp", mp, bit)
                keep[i] = keep[i].astype(F32) + got.astype(F32)
            pieces = [keep.get(i) for i in range(mp)]
        return pieces[0]

    def pieces_items(pieces):
        return [(i, p) for i, p in enumerate(pieces) if p is not None]

    def over_dp(value):
        for bit in bits_of(dp):
            near = value.astype(BF)
            value = near.astype(F32) + swap(near, "dp", dp, bit).astype(F32)
        return value

    def everywhere(value):
        for bit in bits_of(mp):
            value = value + swap(value, "mp", mp, bit)
        for bit in bits_of(dp):
            value = value + swap(value, "dp", dp, bit)
        return value

    total_two = over_dp(halve([grads_two[i] for i in range(mp)], bits_of(mp)))
    total_sums = everywhere(sums)

    grads_one = jnp.zeros((mp,) + one.shape, F32)
    outs = []
    for r in range(rows):
        out = attend_backward(
            list(saved[r][:4]) + [dos[r]], dh1s[r], grads_one, block_of(r), w_one, heads
        )
        grads_one = out[-1]
        outs.append(halve(out[:-1], bits_of(mp)))
    total_one = over_dp(halve([grads_one[i] for i in range(mp)], bits_of(mp)))

    units = w_in.shape[1]
    return (
        jnp.concatenate(results, axis=0),
        jnp.stack(outs),
        total_one[: 3 * width].reshape(3, width, model).transpose(0, 2, 1),
        total_one[3 * width, : 2 * width].reshape(2, width),
        total_two[:width],
        total_sums[0],
        total_sums[1],
        total_sums[2],
        total_two[width : width + units].T,
        total_two[width + 2 * units, :units],
        total_two[width + units : width + 2 * units],
        total_sums[3],
        total_sums[4],
        total_sums[5],
    )


def solution(mesh):
    in_specs = (
        P("dp", "mp", None),
        P("dp", "mp"),
        P(None, None, "mp"),
        P(None, "mp"),
        P("mp", None),
        P(),
        P(),
        P(),
        P(None, "mp"),
        P("mp"),
        P("mp", None),
        P(),
        P(),
        P(),
        P("dp", "mp", None),
    )
    out_specs = (
        P("dp", "mp", None),
        P("dp", "mp", None),
        P(None, None, "mp"),
        P(None, "mp"),
        P("mp", None),
        P(),
        P(),
        P(),
        P(None, "mp"),
        P("mp"),
        P("mp", None),
        P(),
        P(),
        P(),
    )
    sizes = (mesh.shape["dp"], mesh.shape["mp"])
    return jax.shard_map(
        functools.partial(layer, sizes),
        mesh=mesh,
        in_specs=in_specs,
        out_specs=out_specs,
        check_vma=False,
    )
```

```python
import functools

import jax
import jax.numpy as jnp
from jax import lax
from jax.experimental import pallas as pl
from jax.experimental.pallas import tpu as pltpu
from jax.sharding import PartitionSpec as P

HEADS = 4
EPS = 1e-06
FAR = -(2.0**99)
GELU_C = 0.7978845608028654
GELU_A = 0.044715

BF = jnp.bfloat16
F32 = jnp.float32

NN = (((1,), (0,)), ((), ()))
NT = (((1,), (1,)), ((), ()))
TN = (((0,), (0,)), ((), ()))

MB = 2**20
LIMITS = (14, 16, 10, 10)


def mm(left, right, dims):
    return lax.dot_general(left, right, dims, preferred_element_type=F32)


def call(kernel, name, args, outs, scratch=(), flops=0, limit=20):
    whole = pl.BlockSpec(memory_space=pltpu.VMEM)
    return pl.pallas_call(
        kernel,
        out_shape=[jax.ShapeDtypeStruct(shape, kind) for shape, kind in outs],
        in_specs=[whole] * len(args),
        out_specs=[whole] * len(outs),
        scratch_shapes=[pltpu.VMEM(shape, kind) for shape, kind in scratch],
        compiler_params=pltpu.CompilerParams(vmem_limit_bytes=limit * MB),
        cost_estimate=pl.CostEstimate(flops=flops // 20, bytes_accessed=0, transcendentals=0),
        name=name,
    )(*args)


def pack_kernel(rows, *refs):
    w_qkv, b_qv, w_out, w_in, b_in, w_back, segs, x = refs[:8]
    xs = refs[8:]
    width, model = w_qkv.shape[1:]
    units = w_in.shape[1]
    half = model // 2
    here = x.shape[1]
    for r in range(rows):
        out = xs[r]
        out[0:here, :] = x[r]
        out[here : here + 16, :] = jnp.zeros((16, model), BF)
        seg = segs[r : r + 1, :]
        at = here
        for digit in (jnp.bitwise_and(seg, 31), jnp.right_shift(seg, 5)):
            digit = digit.astype(F32).astype(BF)
            for start in range(0, here, model):
                out[at : at + 1, :] = digit[:, start : start + model]
                at += 1
    out = xs[0]
    at = here + 16
    for c in range(3):
        out[at : at + width, :] = w_qkv[c]
        at += width
    out[at : at + 16, :] = jnp.zeros((16, model), BF)
    out[at : at + 1, 0:width] = b_qv[0:1, :]
    out[at : at + 1, width : 2 * width] = b_qv[1:2, :]
    out = xs[-1]
    at = out.shape[0] - width - half - units - 16
    out[at : at + width, :] = w_out[...]
    at += width
    out[at : at + half, 0:units] = w_in[0:half, :]
    out[at : at + half, units : 2 * units] = w_in[half:, :]
    at += half
    out[at : at + units, :] = w_back[...]
    at += units
    out[at : at + 16, :] = jnp.zeros((16, model), BF)
    out[at : at + 1, 0:units] = b_in[...]


def pack(w_qkv, b_qv, w_out, w_in, b_in, w_back, segments, inputs):
    width, units, model = w_qkv.shape[2], w_in.shape[1], w_in.shape[0]
    rows, here = segments.shape
    sizes = [here + 16] * rows
    sizes[0] += 3 * width + 16
    sizes[-1] += width + model // 2 + units + 16
    args = (
        w_qkv.transpose(0, 2, 1),
        b_qv,
        w_out,
        w_in,
        b_in.reshape(1, units),
        w_back,
        segments,
        inputs,
    )
    return call(
        functools.partial(pack_kernel, rows),
        "pack",
        [pltpu.with_memory_space_constraint(a, pltpu.HBM) for a in args],
        [((size, model), BF) for size in sizes],
    )


def forward_kernel(parts, here, hd, *refs):
    xs, ws = refs[:parts], refs[parts : parts + 2]
    e_out, kv_out, qt_out, o_out, w_kv, w_q, feats = refs[parts + 2 :]
    model = xs[0].shape[1]
    length = parts * here
    bias = []
    at = here + 16
    for i in range(2):
        w_q[i * hd : (i + 1) * hd, :] = ws[i][at : at + hd, :]
        w_kv[i * 2 * hd : (i + 1) * 2 * hd, :] = ws[i][at + hd : at + 3 * hd, :]
        line = ws[i][at + 3 * hd : at + 3 * hd + 1, 0 : 2 * hd].astype(F32)
        bias.append(jnp.broadcast_to(line, (2 * hd, 2 * hd)).T)
    per = here // model
    lane = lax.broadcasted_iota(jnp.int32, (hd, here), 0).astype(F32)
    for b in range(parts):
        low = [xs[b][here + i : here + i + 1, :].astype(F32) for i in range(per)]
        high = [xs[b][here + per + i : here + per + i + 1, :].astype(F32) for i in range(per)]
        low, high = jnp.concatenate(low, axis=1), jnp.concatenate(high, axis=1)
        same = lane == jnp.where(lane < 32, low, high + 32.0)
        feats[:, b * here : (b + 1) * here] = jnp.where(same, 0.0, FAR).astype(BF)
        if b == 0:
            qfeat = same.astype(F32)
    proj_q = mm(w_q[...], xs[0][0:here, :], NT)
    qs = []
    for h in range(2):
        qt = proj_q[h * hd : (h + 1) * hd] + bias[h][:hd, 0:1]
        qt = qt.astype(BF).astype(F32) * (hd**-0.5)
        qt_out[h] = qt.astype(BF)
        qs.append(jnp.concatenate([qt, qfeat], axis=0).T.astype(BF))
    for b in range(parts):
        cols = slice(b * here, (b + 1) * here)
        proj = mm(w_kv[...], xs[b][0:here, :], NT)
        for h in range(2):
            at = 2 * h * hd
            kv_out[at : at + hd, cols] = proj[at : at + hd].astype(BF)
            kv_out[at + hd : at + 2 * hd, cols] = (
                proj[at + hd : at + 2 * hd] + bias[h][hd:, 0:1]
            ).astype(BF)
    ones = value_ones(hd, length)

    def score(h):
        keys = kv_out[2 * h * hd : 2 * h * hd + hd, :]
        scores = mm(qs[h], jnp.concatenate([keys, feats[...]], axis=0), NN)
        return scores, jnp.max(scores, axis=-1, keepdims=True)

    later = score(0)
    for h in range(2):
        scores, top = later
        if h == 0:
            later = score(1)
        expo = jnp.exp(scores - top).astype(BF)
        e_out[h] = expo
        values = kv_out[2 * h * hd + hd : 2 * (h + 1) * hd, :]
        o_out[h] = mm(expo, jnp.concatenate([values, ones], axis=0), NT)


def value_ones(hd, length):
    return (lax.broadcasted_iota(jnp.int32, (hd, length), 0) < 2).astype(F32).astype(BF)


def attend_forward(blocks, ws, heads, here):
    parts = len(blocks)
    model = blocks[0].shape[1]
    length = parts * here
    hd = model // heads
    return call(
        functools.partial(forward_kernel, parts, here, hd),
        "attend_forward",
        (*blocks, *ws),
        [
            ((2, here, length), BF),
            ((4 * hd, length), BF),
            ((2, hd, here), BF),
            ((2, here, 2 * hd), F32),
        ],
        [((4 * hd, model), BF), ((2 * hd, model), BF), ((hd, length), BF)],
        flops=2 * 4 * here * length * 256,
        limit=LIMITS[0],
    )


def middle_kernel(parts, heads, rows, skip, *refs):
    pairs = heads // 2
    os, xs = refs[: rows * pairs], refs[rows * pairs : rows * pairs + rows]
    at = rows * pairs + rows
    cot_in = refs[at]
    ws = refs[at + 1 : at + 1 + parts]
    at += 1 + parts
    b_out, g_one, e_one, b_back, g_two, e_two = refs[at : at + 6]
    at += 6
    result_out, keep_out, send_out = refs[at : at + 3]
    at += 3
    dh1s, dos = refs[at : at + rows], refs[at + rows : at + rows + rows * pairs]
    w_out, w_pad, w_in, w_back = refs[at + rows + rows * pairs :]
    here, model = cot_in.shape[1:]
    hd = model // heads
    per = w_out.shape[0] // parts
    units = w_back.shape[0] // parts
    half_model = model // 2
    w_pad[...] = jnp.zeros(w_pad.shape, BF)
    bias = []
    for b in range(parts):
        at = skip
        w_out[b * per : (b + 1) * per, :] = ws[b][at : at + per, :]
        w_pad[b * 2 * per : b * 2 * per + per, :] = ws[b][at : at + per, :]
        at += per
        cols = slice(b * units, (b + 1) * units)
        w_in[0:half_model, cols] = ws[b][at : at + half_model, 0:units]
        w_in[half_model:, cols] = ws[b][at : at + half_model, units : 2 * units]
        at += half_model
        w_back[b * units : (b + 1) * units, :] = ws[b][at : at + units, :]
        at += units
        bias.append(ws[b][at : at + 1, 0:units].astype(F32))
    b_in = jnp.concatenate(bias, axis=1)
    lane = lax.broadcasted_iota(jnp.int32, os[0].shape[1:], 1)

    def norm(h):
        centre = h - jnp.mean(h, axis=-1, keepdims=True)
        rstd = lax.rsqrt(jnp.mean(centre * centre, axis=-1, keepdims=True) + EPS)
        return centre * rstd, rstd

    def norm_back(dy, gain, unit, rstd):
        dn = dy * gain
        mean = jnp.mean(dn, axis=-1, keepdims=True)
        along = jnp.mean(dn * unit, axis=-1, keepdims=True)
        return rstd * (dn - mean - unit * along)

    def down(v):
        return jnp.sum(v, axis=0, keepdims=True)

    def one_row(r):
        o_in = [os[r * pairs + h // 2][h % 2] for h in range(heads)]
        inv = [1.0 / o[:, hd : hd + 1] for o in o_in]
        normal = [o * i for o, i in zip(o_in, inv)]
        tiles = [
            jnp.where(lane < hd, normal[h], pltpu.roll(normal[h + 1], hd, 1))
            for h in range(0, heads, 2)
        ]
        att = jnp.concatenate(tiles, axis=1).astype(BF)
        h1 = xs[r][0:here, :].astype(F32) + mm(att, w_out[...], NN) + b_out[...].astype(F32)
        n1, rstd1 = norm(h1)
        y1 = n1 * g_one[...] + e_one[...]
        y1b = y1.astype(BF)
        pre = mm(y1b, w_in[...], NN) + b_in
        square = pre * pre
        th = jnp.tanh(GELU_C * pre * (1.0 + GELU_A * square))
        half = 0.5 * (1.0 + th)
        act = (pre * half).astype(BF)
        slope = half + 0.5 * pre * (1.0 - th * th) * (GELU_C * (1.0 + 3.0 * GELU_A * square))
        h2 = y1 + mm(act, w_back[...], NN) + b_back[...].astype(F32)
        n2, rstd2 = norm(h2)
        result_out[r] = (n2 * g_two[...] + e_two[...]).astype(BF)
        cot = cot_in[r].astype(F32)
        dh2 = norm_back(cot, g_two[...], n2, rstd2)
        dz = dh2.astype(BF)
        dact = mm(dz, w_back[...], NT)
        dpre = (dact * slope).astype(BF)
        dw_back = mm(act, dz, TN)
        dw_in = mm(y1b, dpre, TN)
        db_in = down(dpre.astype(F32))
        dy1 = mm(dpre, w_in[...], NT) + dh2
        dh1 = norm_back(dy1, g_one[...], n1, rstd1)
        dh1s[r][...] = dh1
        da = dh1.astype(BF)
        dw_out = mm(att, da, TN)
        dwide = mm(da, w_pad[...], NT)
        for h in range(heads):
            grad = (dwide[:, 2 * hd * h : 2 * hd * (h + 1)] * inv[h]).astype(BF)
            wide = grad.astype(F32)
            inner = jnp.sum(wide * normal[h], axis=-1, keepdims=True)
            high = inner.astype(BF).astype(F32)
            rest = inner - high
            wide = jnp.where(lane == hd, -high, jnp.where(lane == hd + 1, -rest, wide))
            dos[r * pairs + h // 2][h % 2] = wide.astype(BF)
        sums = [down(dh1), down(dy1 * n1), down(dy1), down(dh2), down(cot * n2), down(cot)]
        return [dw_out, dw_in, dw_back, db_in] + sums

    total = one_row(0)
    for r in range(1, rows):
        total = [a + b for a, b in zip(total, one_row(r))]
    dw_out, dw_in, dw_back, db_in = total[:4]
    for b in range(parts):
        out = send_out if b % 2 else keep_out
        kind = out.dtype
        c = b // 2
        cols = slice(b * units, (b + 1) * units)
        at = 0
        out[c, at : at + per, :] = dw_out[b * per : (b + 1) * per].astype(kind)
        at += per
        out[c, at : at + half_model, 0:units] = dw_in[0:half_model, cols].astype(kind)
        out[c, at : at + half_model, units : 2 * units] = dw_in[half_model:, cols].astype(kind)
        at += half_model
        out[c, at : at + units, :] = dw_back[b * units : (b + 1) * units].astype(kind)
        at += units
        out[c, at:, :] = jnp.zeros((16, model), kind)
        out[c, at : at + 1, 0:units] = db_in[:, cols].astype(kind)
        for i, row in enumerate(total[4:]):
            out[c, at + 1 + i : at + 2 + i, :] = row.astype(kind)


def middle(os, xs, cotangent, ws, vectors, heads, skip):
    parts = len(ws)
    rows, here, model = cotangent.shape
    hd = model // heads
    size = ws[0].shape[0] - skip
    width = model // parts
    units = size - 16 - width - model // 2
    return call(
        functools.partial(middle_kernel, parts, heads, rows, skip),
        "middle",
        (*os, *xs, cotangent, *ws, *vectors),
        [
            (cotangent.shape, BF),
            ((parts // 2, size, model), F32),
            ((parts // 2, size, model), BF),
        ]
        + [((here, model), F32)] * rows
        + [((2, here, 2 * hd), BF)] * (rows * heads // 2),
        [
            ((parts * width, model), BF),
            ((2 * parts * width, model), BF),
            ((model, parts * units), BF),
            ((parts * units, model), BF),
        ],
        flops=rows * 6 * here * model * (2 * model + 2 * parts * units),
        limit=LIMITS[1],
    )


def backward_kernel(*refs):
    e_in, kv_in, qt_in, do_in, dkv, dq, ds = refs
    hd = qt_in.shape[1]
    here = qt_in.shape[2]
    length = kv_in.shape[1]
    chunk = here // 2
    ones = value_ones(hd, length)
    for h in range(2):
        keys = kv_in[2 * h * hd : 2 * h * hd + hd, :]
        values = jnp.concatenate([kv_in[2 * h * hd + hd : 2 * (h + 1) * hd, :], ones], axis=0)
        for c in range(2):
            rows = slice(c * chunk, (c + 1) * chunk)
            dp = mm(do_in[h, rows, :], values, NN)
            ds[h, rows, :] = (dp * e_in[h, rows, :].astype(F32)).astype(BF)
        dkv[2 * h * hd + hd : 2 * (h + 1) * hd, :] = mm(do_in[h], e_in[h], TN)[:hd].astype(BF)
        dkv[2 * h * hd : 2 * h * hd + hd, :] = mm(qt_in[h], ds[h], NN).astype(BF)
        dq[h * hd : (h + 1) * hd, :] = (mm(keys, ds[h], NT) * (hd**-0.5)).astype(BF)


def attend_backward(e, kv, qt, do):
    _, hd, here = qt.shape
    length = kv.shape[1]
    return call(
        backward_kernel,
        "attend_backward",
        (e, kv, qt, do),
        [((4 * hd, length), BF), ((2 * hd, here), BF)],
        [((2, here, length), BF)],
        flops=2 * 6 * here * length * 256,
        limit=LIMITS[2],
    )


def inputs_kernel(parts, here, *refs):
    pairs = parts // 2
    dkvs, dqs = refs[:pairs], refs[pairs : 2 * pairs]
    at = 2 * pairs
    dh1_in = refs[at]
    ws = refs[at + 1 : at + 1 + parts]
    dx_own, dx_keep, dx_send, w_kv, w_q = refs[at + 1 + parts :]
    hd = w_q.shape[0] // parts
    at = here + 16
    for b in range(parts):
        w_q[b * hd : (b + 1) * hd, :] = ws[b][at : at + hd, :]
        w_kv[b * 2 * hd : (b + 1) * 2 * hd, :] = ws[b][at + hd : at + 3 * hd, :]
    dq = jnp.concatenate([d[...] for d in dqs], axis=0)
    for b in range(parts):
        cols = slice(b * here, (b + 1) * here)
        part = jnp.concatenate([d[:, cols] for d in dkvs], axis=0)
        dx = mm(part, w_kv[...], TN)
        if b == 0:
            dx_own[...] = dx + mm(dq, w_q[...], TN) + dh1_in[...]
        elif b % 2:
            dx_send[b // 2] = dx.astype(BF)
        else:
            dx_keep[b // 2 - 1] = dx


def input_gradients(dkvs, dqs, dh1, ws):
    parts = len(ws)
    here, model = dh1.shape
    return call(
        functools.partial(inputs_kernel, parts, here),
        "input_gradients",
        (*dkvs, *dqs, dh1, *ws),
        [
            ((here, model), F32),
            ((parts // 2 - 1, here, model), F32),
            ((parts // 2, here, model), BF),
        ],
        [((2 * model, model), BF), ((model, model), BF)],
        flops=4 * parts * here * model * model,
        limit=LIMITS[3],
    )


def weights_kernel(parts, here, first, last, *refs):
    pairs = parts // 2
    dkvs, dqs = refs[:pairs], refs[pairs : 2 * pairs]
    at = 2 * pairs
    xs = refs[at : at + parts]
    at += parts
    if not first:
        grads_in = refs[at]
        at += 1
    outs = refs[at:]
    model = xs[0].shape[1]
    hd = model // parts
    dq = jnp.concatenate([d[...] for d in dqs], axis=0)
    gkv = None
    for b in range(parts):
        cols = slice(b * here, (b + 1) * here)
        part = jnp.concatenate([d[:, cols] for d in dkvs], axis=0)
        term = mm(part, xs[b][0:here, :], NN)
        gkv = term if gkv is None else gkv + term
    gq = mm(dq, xs[0][0:here, :], NN)
    bq = mm(jnp.ones((8, here), BF), dq, NT)[0:1]
    full = jnp.concatenate([d[...] for d in dkvs], axis=0)
    bkv = mm(jnp.ones((8, parts * here), BF), full, NT)[0:1]
    for b in range(parts):
        pieces = [
            (slice(0, hd), slice(0, model), gq[b * hd : (b + 1) * hd]),
            (slice(hd, 3 * hd), slice(0, model), gkv[b * 2 * hd : (b + 1) * 2 * hd]),
            (slice(3 * hd, 3 * hd + 1), slice(0, hd), bq[:, b * hd : (b + 1) * hd]),
            (
                slice(3 * hd, 3 * hd + 1),
                slice(hd, 2 * hd),
                bkv[:, b * 2 * hd + hd : (b + 1) * 2 * hd],
            ),
        ]
        out, c = (outs[b % 2], b // 2) if last else (outs[0], b)
        out[c, 3 * hd :, :] = jnp.zeros((16, model), out.dtype)
        for rows, cols, value in pieces:
            if not first:
                value = value + grads_in[b, rows, cols]
            out[c, rows, cols] = value.astype(out.dtype)


def weight_gradients(dkvs, dqs, grads, blocks, here, first, last):
    parts = len(blocks)
    model = blocks[0].shape[1]
    size = 3 * (model // parts) + 16
    if last:
        outs = [((parts // 2, size, model), F32), ((parts // 2, size, model), BF)]
    else:
        outs = [((parts, size, model), F32)]
    return call(
        functools.partial(weights_kernel, parts, here, first, last),
        "weight_gradients",
        (*dkvs, *dqs, *blocks) + (() if first else (grads,)),
        outs,
        flops=4 * parts * here * model * model,
        limit=LIMITS[3],
    )


def add_kernel(rows, *refs):
    owns, nears, fars = refs[:rows], refs[rows : 2 * rows], refs[2 * rows : 3 * rows]
    out = refs[3 * rows]
    for r in range(rows):
        out[r] = owns[r][...] + nears[r][0].astype(F32) + fars[r][...].astype(F32)


def add_inputs(owns, nears, fars):
    rows = len(owns)
    (out,) = call(
        functools.partial(add_kernel, rows),
        "add_inputs",
        (*owns, *nears, *fars),
        [((rows,) + owns[0].shape, F32)],
        limit=LIMITS[3],
    )
    return out


def finish_one_kernel(a, b, qkv, bias):
    width = qkv.shape[1]
    total = a[...].astype(F32) + b[...].astype(F32)
    for c in range(3):
        qkv[c] = total[c * width : (c + 1) * width]
    line = total[3 * width : 3 * width + 1]
    bias[0:1, :] = line[:, 0:width]
    bias[1:2, :] = line[:, width : 2 * width]


def finish_two_kernel(a, b, w_out, w_in, b_in, w_back, *sums):
    width, model = w_out.shape
    units = w_back.shape[0]
    half = model // 2
    total = a[...].astype(F32) + b[...].astype(F32)
    w_out[...] = total[:width]
    at = width
    w_in[0:half, :] = total[at : at + half, 0:units]
    w_in[half:, :] = total[at : at + half, units : 2 * units]
    at += half
    w_back[...] = total[at : at + units]
    at += units
    b_in[...] = total[at : at + 1, 0:units]
    for i, out in enumerate(sums):
        out[...] = total[at + 1 + i : at + 2 + i]


def swap(value, axis, size, bit):
    return lax.ppermute(value, axis, [(i, i ^ bit) for i in range(size)])


def after(value, *others):
    return lax.optimization_barrier((value, *others))[0]


def layer(mesh_sizes, *args):
    (inputs, segments, w_qkv, b_qv, w_out, b_out, gain_one, shift_one) = args[:8]
    (w_in, b_in, w_back, b_back, gain_two, shift_two, cotangent) = args[8:]
    dp, mp = mesh_sizes
    rows, here, model = inputs.shape
    heads = HEADS
    width = w_qkv.shape[2]
    units = w_in.shape[1]

    def near(value):
        return swap(value, "mp", mp, 1)

    def far(value):
        return swap(value, "mp", mp, 2)

    packs = pack(w_qkv, b_qv, w_out, w_in, b_in, w_back, segments, inputs)
    vectors = [
        v.reshape(1, model) for v in (b_out, gain_one, shift_one, b_back, gain_two, shift_two)
    ]
    fars = [far(packs[0])]
    nears = [near(after(packs[0], *vectors))]
    boths = [near(fars[0])]
    for r in range(1, rows):
        fars.append(far(after(packs[r], fars[0] if r == 1 else boths[0])))
        nears.append(near(packs[r]))
    ones = [packs[0], nears[0], fars[0], boths[0]]
    saved, boths_of = [], []
    pairs = heads // 2
    for r in range(rows):
        saved.append([])
        for pair in range(pairs):
            blocks = [packs[r], nears[r], fars[r], boths[r]]
            out = attend_forward(blocks, ones[2 * pair : 2 * pair + 2], heads, here)
            saved[r].append(out)
            if pair == 0 and r + 1 < rows:
                boths.append(near(after(fars[r + 1], out[2])))
        boths_of.append(blocks)
    skip = packs[-1].shape[0] - width - model // 2 - units - 16
    result, keep_two, send_two, *rest = middle(
        [out[3] for row in saved for out in row],
        packs,
        cotangent,
        boths_of[-1],
        vectors,
        heads,
        skip,
    )
    dh1s, dos = rest[:rows], rest[rows:]

    def chain(keep, send):
        got = near(send)
        mine = keep[0] + got[0].astype(F32)
        other = (keep[1] + got[1].astype(F32)).astype(BF)
        yield other
        value = mine + far(other).astype(F32)
        bit = 1
        while bit < dp:
            sent = value.astype(BF)
            yield sent
            got = swap(sent, "dp", dp, bit)
            value = sent.astype(F32) + got.astype(F32)
            bit *= 2
        yield (sent, got)

    steps = chain(keep_two, send_two)
    total_two = None
    ready = []
    grads = None
    owns, near_got, far_got = [], [], []
    pending = None

    def advance():
        nonlocal total_two, pending
        step = next(steps, None)
        if isinstance(step, tuple):
            total_two = step
        elif step is not None:
            ready.append(step)
        if pending is not None:
            other = (pending[0] + pending[1].astype(F32)).astype(BF)
            far_got.append(far(other))
            ready.append(other)
            pending = None

    for r in range(rows):
        dkvs, dqs = [], []
        for pair in range(pairs):
            e, kv, qt, _ = saved[r][pair]
            if ready:
                e = after(e, *ready)
                ready.clear()
            dkv, dq = attend_backward(e, kv, qt, dos[r * pairs + pair])
            dkvs.append(dkv)
            dqs.append(dq)
            advance()
        last = r == rows - 1
        grads = weight_gradients(dkvs, dqs, grads, boths_of[r], here, r == 0, last)
        if last:
            tail = chain(*grads)
            other = next(tail)
            dkvs = [after(d, grads[1]) for d in dkvs]
        else:
            grads = grads[0]
        own, keep, send = input_gradients(dkvs, dqs, dh1s[r], ones)
        got = near(after(send, other) if last else send)
        owns.append(own)
        near_got.append(got)
        pending = (keep[0], got[1])
    sent = next(tail)
    final = after((pending[0] + pending[1].astype(F32)).astype(BF), sent)
    far_got.append(far(final))
    for step in steps:
        total_two = step
    for step in tail:
        total_one = step
    grad_inputs = add_inputs(owns, near_got, far_got)
    grad_out, grad_in, grad_b_in, grad_back, *sums = call(
        finish_two_kernel,
        "finish_two",
        total_two,
        [
            ((width, model), F32),
            ((model, units), F32),
            ((1, units), F32),
            ((units, model), F32),
        ]
        + [((1, model), F32)] * 6,
    )
    grad_qkv, grad_bias = call(
        finish_one_kernel,
        "finish_one",
        total_one,
        [((3, width, model), F32), ((2, width), F32)],
    )
    sums = [s.reshape(model) for s in sums]
    return (
        result,
        grad_inputs,
        grad_qkv.transpose(0, 2, 1),
        grad_bias,
        grad_out,
        sums[0],
        sums[1],
        sums[2],
        grad_in,
        grad_b_in.reshape(units),
        grad_back,
        sums[3],
        sums[4],
        sums[5],
    )


def solution(mesh):
    in_specs = (
        P("dp", "mp", None),
        P("dp", "mp"),
        P(None, None, "mp"),
        P(None, "mp"),
        P("mp", None),
        P(),
        P(),
        P(),
        P(None, "mp"),
        P("mp"),
        P("mp", None),
        P(),
        P(),
        P(),
        P("dp", "mp", None),
    )
    out_specs = (
        P("dp", "mp", None),
        P("dp", "mp", None),
        P(None, None, "mp"),
        P(None, "mp"),
        P("mp", None),
        P(),
        P(),
        P(),
        P(None, "mp"),
        P("mp"),
        P("mp", None),
        P(),
        P(),
        P(),
    )
    sizes = (mesh.shape["dp"], mesh.shape["mp"])
    return jax.shard_map(
        functools.partial(layer, sizes),
        mesh=mesh,
        in_specs=in_specs,
        out_specs=out_specs,
        check_vma=False,
    )
```

```python
import functools

import jax
import jax.numpy as jnp
from jax import lax
from jax.experimental import pallas as pl
from jax.experimental.pallas import tpu as pltpu
from jax.sharding import PartitionSpec as P

HEADS = 4
EPS = 1e-06
FAR = -(2.0**99)
GELU_C = 0.7978845608028654
GELU_A = 0.044715

BF = jnp.bfloat16
F32 = jnp.float32

NN = (((1,), (0,)), ((), ()))
NT = (((1,), (1,)), ((), ()))
TN = (((0,), (0,)), ((), ()))

MB = 2**20
LIMITS = (20, 20, 12, 12)


def mm(left, right, dims):
    return lax.dot_general(left, right, dims, preferred_element_type=F32)


def call(kernel, name, args, outs, scratch=(), flops=0, limit=20):
    whole = pl.BlockSpec(memory_space=pltpu.VMEM)
    return pl.pallas_call(
        kernel,
        out_shape=[jax.ShapeDtypeStruct(shape, kind) for shape, kind in outs],
        in_specs=[whole] * len(args),
        out_specs=[whole] * len(outs),
        scratch_shapes=[pltpu.VMEM(shape, kind) for shape, kind in scratch],
        compiler_params=pltpu.CompilerParams(vmem_limit_bytes=limit * MB),
        cost_estimate=pl.CostEstimate(flops=flops // 20, bytes_accessed=0, transcendentals=0),
        name=name,
    )(*args)


def pack_kernel(rows, *refs):
    w_qkv, b_qv, w_out, w_in, b_in, w_back, segs, x = refs[:8]
    xs, two = refs[8:-1], refs[-1]
    width, model = w_qkv.shape[1:]
    units = w_in.shape[1]
    half = model // 2
    here = x.shape[1]
    for r in range(rows):
        out = xs[r]
        out[0:here, :] = x[r]
        out[here : here + 16, :] = jnp.zeros((16, model), BF)
        seg = segs[r : r + 1, :]
        at = here
        for digit in (jnp.bitwise_and(seg, 31), jnp.right_shift(seg, 5)):
            digit = digit.astype(F32).astype(BF)
            for start in range(0, here, model):
                out[at : at + 1, :] = digit[:, start : start + model]
                at += 1
    out = xs[0]
    at = here + 16
    for c in range(3):
        out[at : at + width, :] = w_qkv[c]
        at += width
    out[at : at + 16, :] = jnp.zeros((16, model), BF)
    out[at : at + 1, 0:width] = b_qv[0:1, :]
    out[at : at + 1, width : 2 * width] = b_qv[1:2, :]
    two[0:width, :] = w_out[...]
    at = width
    two[at : at + half, 0:units] = w_in[0:half, :]
    two[at : at + half, units : 2 * units] = w_in[half:, :]
    at += half
    two[at : at + units, :] = w_back[...]
    at += units
    two[at : at + 16, :] = jnp.zeros((16, model), BF)
    two[at : at + 1, 0:units] = b_in[...]


def pack(w_qkv, b_qv, w_out, w_in, b_in, w_back, segments, inputs):
    width, units, model = w_qkv.shape[2], w_in.shape[1], w_in.shape[0]
    rows, here = segments.shape
    sizes = [here + 16] * rows
    sizes[0] += 3 * width + 16
    sizes.append(width + model // 2 + units + 16)
    args = (
        w_qkv.transpose(0, 2, 1),
        b_qv,
        w_out,
        w_in,
        b_in.reshape(1, units),
        w_back,
        segments,
        inputs,
    )
    return call(
        functools.partial(pack_kernel, rows),
        "pack",
        [pltpu.with_memory_space_constraint(a, pltpu.HBM) for a in args],
        [((size, model), BF) for size in sizes],
    )


def forward_kernel(parts, here, hd, *refs):
    xs, ws = refs[:parts], refs[parts : 2 * parts]
    e_out, kv_out, qt_out, o_out, w_kv, w_q, bias, feats, qfeat = refs[2 * parts :]
    heads = parts
    length = parts * here
    at = here + 16
    for h in range(heads):
        w_q[h * hd : (h + 1) * hd, :] = ws[h][at : at + hd, :]
        w_kv[h * 2 * hd : (h + 1) * 2 * hd, :] = ws[h][at + hd : at + 3 * hd, :]
        line = ws[h][at + 3 * hd : at + 3 * hd + 1, 0 : 2 * hd].astype(F32)
        bias[h] = jnp.broadcast_to(line, (2 * hd, 2 * hd)).T
    per = here // xs[0].shape[1]
    lane = lax.broadcasted_iota(jnp.int32, (hd, here), 0).astype(F32)
    for b in range(parts):
        low = [xs[b][here + i : here + i + 1, :].astype(F32) for i in range(per)]
        high = [xs[b][here + per + i : here + per + i + 1, :].astype(F32) for i in range(per)]
        low, high = jnp.concatenate(low, axis=1), jnp.concatenate(high, axis=1)
        same = lane == jnp.where(lane < 32, low, high + 32.0)
        feats[:, b * here : (b + 1) * here] = jnp.where(same, 0.0, FAR).astype(BF)
        if b == 0:
            qfeat[...] = same.astype(F32)
    ones = value_ones(hd, length)

    def two_heads(pair, _):
        first = 2 * pair
        proj = mm(w_q[pl.ds(pl.multiple_of(first * hd, 2 * hd), 2 * hd), :], xs[0][0:here, :], NT)
        qs = []
        for i in range(2):
            qt = proj[i * hd : (i + 1) * hd] + bias[first + i, :hd, 0:1]
            qt = qt.astype(BF).astype(F32) * (hd**-0.5)
            qt_out[first + i] = qt.astype(BF)
            qs.append(jnp.concatenate([qt, qfeat[...]], axis=0).T.astype(BF))
        w = w_kv[pl.ds(pl.multiple_of(first * 2 * hd, 4 * hd), 4 * hd), :]
        for b in range(parts):
            cols = slice(b * here, (b + 1) * here)
            proj = mm(w, xs[b][0:here, :], NT)
            for i in range(2):
                at = 2 * i * hd
                kv_out[first + i, 0:hd, cols] = proj[at : at + hd].astype(BF)
                kv_out[first + i, hd:, cols] = (
                    proj[at + hd : at + 2 * hd] + bias[first + i, hd:, 0:1]
                ).astype(BF)

        def score(i):
            keys = jnp.concatenate([kv_out[first + i, 0:hd, :], feats[...]], axis=0)
            scores = mm(qs[i], keys, NN)
            return scores, jnp.max(scores, axis=-1, keepdims=True)

        later = score(0)
        for i in range(2):
            scores, top = later
            if i == 0:
                later = score(1)
            expo = jnp.exp(scores - top).astype(BF)
            e_out[first + i] = expo
            values = jnp.concatenate([kv_out[first + i, hd:, :], ones], axis=0)
            o_out[first + i] = mm(expo, values, NT)
        return 0

    lax.fori_loop(0, heads // 2, two_heads, 0)


def value_ones(hd, length):
    return (lax.broadcasted_iota(jnp.int32, (hd, length), 0) < 2).astype(F32).astype(BF)


def attend_forward(blocks, ws, heads, here):
    parts = len(blocks)
    model = blocks[0].shape[1]
    length = parts * here
    hd = model // heads
    return call(
        functools.partial(forward_kernel, parts, here, hd),
        "attend_forward",
        (*blocks, *ws),
        [
            ((heads, here, length), BF),
            ((heads, 2 * hd, length), BF),
            ((heads, hd, here), BF),
            ((heads, here, 2 * hd), F32),
        ],
        [
            ((heads * 2 * hd, model), BF),
            ((heads * hd, model), BF),
            ((heads, 2 * hd, 2 * hd), F32),
            ((hd, length), BF),
            ((hd, here), F32),
        ],
        flops=heads * 4 * here * length * 256,
        limit=LIMITS[0],
    )


def middle_kernel(parts, heads, rows, *refs):
    os, xs = refs[:rows], refs[rows : 2 * rows]
    cot_in = refs[2 * rows]
    ws = refs[2 * rows + 1 : 2 * rows + 1 + parts]
    at = 2 * rows + 1 + parts
    b_out, g_one, e_one, b_back, g_two, e_two = refs[at : at + 6]
    result_out, keep_out, send_out, dh1_out, do_out = refs[at + 6 : at + 11]
    w_out, w_pad, w_in, w_back, o_all, x_all = refs[at + 11 : at + 17]
    dw_out, dw_in, dw_back, db_in, sums = refs[at + 17 :]
    here, model = cot_in.shape[1:]
    hd = model // heads
    per = w_out.shape[0] // parts
    units = w_back.shape[0] // parts
    half_model = model // 2
    w_pad[...] = jnp.zeros(w_pad.shape, BF)
    bias = []
    for b in range(parts):
        at = 0
        w_out[b * per : (b + 1) * per, :] = ws[b][at : at + per, :]
        w_pad[b * 2 * per : b * 2 * per + per, :] = ws[b][at : at + per, :]
        at += per
        cols = slice(b * units, (b + 1) * units)
        w_in[0:half_model, cols] = ws[b][at : at + half_model, 0:units]
        w_in[half_model:, cols] = ws[b][at : at + half_model, units : 2 * units]
        at += half_model
        w_back[b * units : (b + 1) * units, :] = ws[b][at : at + units, :]
        at += units
        bias.append(ws[b][at : at + 1, 0:units].astype(F32))
    b_in = jnp.concatenate(bias, axis=1)
    lane = lax.broadcasted_iota(jnp.int32, (here, 2 * hd), 1)
    for r in range(rows):
        o_all[r] = os[r][...]
        x_all[r] = xs[r][0:here, :]
    for total in (dw_out, dw_in, dw_back, db_in, sums):
        total[...] = jnp.zeros(total.shape, F32)

    def norm(h):
        centre = h - jnp.mean(h, axis=-1, keepdims=True)
        rstd = lax.rsqrt(jnp.mean(centre * centre, axis=-1, keepdims=True) + EPS)
        return centre * rstd, rstd

    def norm_back(dy, gain, unit, rstd):
        dn = dy * gain
        mean = jnp.mean(dn, axis=-1, keepdims=True)
        along = jnp.mean(dn * unit, axis=-1, keepdims=True)
        return rstd * (dn - mean - unit * along)

    def down(v):
        return jnp.sum(v, axis=0, keepdims=True)

    def one_row(r, _):
        o_in = [o_all[r, h] for h in range(heads)]
        inv = [1.0 / o[:, hd : hd + 1] for o in o_in]
        normal = [o * i for o, i in zip(o_in, inv)]
        tiles = [
            jnp.where(lane < hd, normal[h], pltpu.roll(normal[h + 1], hd, 1))
            for h in range(0, heads, 2)
        ]
        att = jnp.concatenate(tiles, axis=1).astype(BF)
        h1 = x_all[r].astype(F32) + mm(att, w_out[...], NN) + b_out[...].astype(F32)
        n1, rstd1 = norm(h1)
        y1 = n1 * g_one[...] + e_one[...]
        y1b = y1.astype(BF)
        pre = mm(y1b, w_in[...], NN) + b_in
        square = pre * pre
        th = jnp.tanh(GELU_C * pre * (1.0 + GELU_A * square))
        half = 0.5 * (1.0 + th)
        act = (pre * half).astype(BF)
        slope = half + 0.5 * pre * (1.0 - th * th) * (GELU_C * (1.0 + 3.0 * GELU_A * square))
        h2 = y1 + mm(act, w_back[...], NN) + b_back[...].astype(F32)
        n2, rstd2 = norm(h2)
        result_out[r] = (n2 * g_two[...] + e_two[...]).astype(BF)
        cot = cot_in[r].astype(F32)
        dh2 = norm_back(cot, g_two[...], n2, rstd2)
        dz = dh2.astype(BF)
        dact = mm(dz, w_back[...], NT)
        dpre = (dact * slope).astype(BF)
        dw_back[...] += mm(act, dz, TN)
        dw_in[...] += mm(y1b, dpre, TN)
        db_in[...] += down(dpre.astype(F32))
        dy1 = mm(dpre, w_in[...], NT) + dh2
        dh1 = norm_back(dy1, g_one[...], n1, rstd1)
        dh1_out[r] = dh1
        da = dh1.astype(BF)
        dw_out[...] += mm(att, da, TN)
        dwide = mm(da, w_pad[...], NT)
        for h in range(heads):
            grad = (dwide[:, 2 * hd * h : 2 * hd * (h + 1)] * inv[h]).astype(BF)
            wide = grad.astype(F32)
            inner = jnp.sum(wide * normal[h], axis=-1, keepdims=True)
            high = inner.astype(BF).astype(F32)
            rest = inner - high
            wide = jnp.where(lane == hd, -high, jnp.where(lane == hd + 1, -rest, wide))
            do_out[r, h] = wide.astype(BF)
        rows_of = [down(dh1), down(dy1 * n1), down(dy1), down(dh2), down(cot * n2), down(cot)]
        for i, row in enumerate(rows_of):
            sums[i : i + 1, :] += row
        return 0

    lax.fori_loop(0, rows, one_row, 0)
    for b in range(parts):
        out = send_out if b % 2 else keep_out
        kind = out.dtype
        c = b // 2
        cols = slice(b * units, (b + 1) * units)
        at = 0
        out[c, at : at + per, :] = dw_out[b * per : (b + 1) * per, :].astype(kind)
        at += per
        out[c, at : at + half_model, 0:units] = dw_in[0:half_model, cols].astype(kind)
        out[c, at : at + half_model, units : 2 * units] = dw_in[half_model:, cols].astype(kind)
        at += half_model
        out[c, at : at + units, :] = dw_back[b * units : (b + 1) * units, :].astype(kind)
        at += units
        out[c, at:, :] = jnp.zeros((16, model), kind)
        out[c, at : at + 1, 0:units] = db_in[:, cols].astype(kind)
        out[c, at + 1 : at + 7, :] = sums[0:6, :].astype(kind)


def middle(os, xs, cotangent, ws, vectors, heads):
    parts = len(ws)
    rows, here, model = cotangent.shape
    hd = model // heads
    size = ws[0].shape[0]
    width = model // parts
    units = size - 16 - width - model // 2
    return call(
        functools.partial(middle_kernel, parts, heads, rows),
        "middle",
        (*os, *xs, cotangent, *ws, *vectors),
        [
            (cotangent.shape, BF),
            ((parts // 2, size, model), F32),
            ((parts // 2, size, model), BF),
            ((rows, here, model), F32),
            ((rows, heads, here, 2 * hd), BF),
        ],
        [
            ((parts * width, model), BF),
            ((2 * parts * width, model), BF),
            ((model, parts * units), BF),
            ((parts * units, model), BF),
            ((rows, heads, here, 2 * hd), F32),
            ((rows, here, model), BF),
            ((parts * width, model), F32),
            ((model, parts * units), F32),
            ((parts * units, model), F32),
            ((1, parts * units), F32),
            ((8, model), F32),
        ],
        flops=rows * 6 * here * model * (2 * model + 2 * parts * units),
        limit=LIMITS[1],
    )


def backward_kernel(row, first, each, *refs):
    e_in, kv_in, qt_in, do_in, dkv, dq, ds = refs
    hd, here = qt_in.shape[1:]
    length = kv_in.shape[2]
    chunk = here // 2
    ones = value_ones(hd, length)

    def some_heads(step, _):
        for i in range(each):
            o = step * each + i
            h = first + o
            values = jnp.concatenate([kv_in[h, hd:, :], ones], axis=0)
            for c in range(2):
                rows = slice(c * chunk, (c + 1) * chunk)
                dp = mm(do_in[row, h, rows, :], values, NN)
                ds[i, rows, :] = (dp * e_in[h, rows, :].astype(F32)).astype(BF)
            dkv[o, hd:, :] = mm(do_in[row, h], e_in[h], TN)[:hd].astype(BF)
            dkv[o, :hd, :] = mm(qt_in[h], ds[i], NN).astype(BF)
            dq[o] = (mm(kv_in[h, :hd, :], ds[i], NT) * (hd**-0.5)).astype(BF)
        return 0

    lax.fori_loop(0, dq.shape[0] // each, some_heads, 0)


def attend_backward(row, first, count, each, e, kv, qt, do):
    _, hd, here = qt.shape
    length = kv.shape[2]
    return call(
        functools.partial(backward_kernel, row, first, each),
        "attend_backward",
        (e, kv, qt, do),
        [((count, 2 * hd, length), BF), ((count, hd, here), BF)],
        [((each, here, length), BF)],
        flops=count * 6 * here * length * 256,
        limit=LIMITS[2],
    )


def inputs_kernel(parts, here, row, pieces, *refs):
    dkvs, dqs = refs[:pieces], refs[pieces : 2 * pieces]
    at = 2 * pieces
    dh1_in = refs[at]
    ws = refs[at + 1 : at + 1 + parts]
    dx_own, dx_keep, dx_send, w_kv, w_q = refs[at + 1 + parts :]
    hd = w_q.shape[0] // parts
    at = here + 16
    for b in range(parts):
        w_q[b * hd : (b + 1) * hd, :] = ws[b][at : at + hd, :]
        w_kv[b * 2 * hd : (b + 1) * 2 * hd, :] = ws[b][at + hd : at + 3 * hd, :]
    for b in range(parts):
        dx = mm(joined(dkvs, slice(b * here, (b + 1) * here)), w_kv[...], TN)
        if b == 0:
            dx_own[...] = dx + mm(joined(dqs, slice(0, here)), w_q[...], TN) + dh1_in[row]
        elif b % 2:
            dx_send[b // 2] = dx.astype(BF)
        else:
            dx_keep[b // 2 - 1] = dx


def joined(refs, cols):
    return jnp.concatenate([ref[h, :, cols] for ref in refs for h in range(ref.shape[0])], axis=0)


def input_gradients(row, dkvs, dqs, dh1, ws):
    parts = len(ws)
    here, model = dh1.shape[1:]
    return call(
        functools.partial(inputs_kernel, parts, here, row, len(dkvs)),
        "input_gradients",
        (*dkvs, *dqs, dh1, *ws),
        [
            ((here, model), F32),
            ((parts // 2 - 1, here, model), F32),
            ((parts // 2, here, model), BF),
        ],
        [((2 * model, model), BF), ((model, model), BF)],
        flops=4 * parts * here * model * model,
        limit=LIMITS[3],
    )


def weights_kernel(parts, here, first, last, many, *refs):
    dkvs, dqs = refs[:many], refs[many : 2 * many]
    at = 2 * many
    xs = refs[at : at + parts]
    at += parts
    if not first:
        grads_in = refs[at]
        at += 1
    outs = refs[at:]
    model = xs[0].shape[1]
    hd = model // parts
    dq = joined(dqs, slice(0, here))
    gkv = None
    for b in range(parts):
        term = mm(joined(dkvs, slice(b * here, (b + 1) * here)), xs[b][0:here, :], NN)
        gkv = term if gkv is None else gkv + term
    gq = mm(dq, xs[0][0:here, :], NN)
    bq = mm(jnp.ones((8, here), BF), dq, NT)[0:1]
    length = parts * here
    bkv = mm(jnp.ones((8, length), BF), joined(dkvs, slice(0, length)), NT)[0:1]
    for b in range(parts):
        pieces = [
            (slice(0, hd), slice(0, model), gq[b * hd : (b + 1) * hd]),
            (slice(hd, 3 * hd), slice(0, model), gkv[b * 2 * hd : (b + 1) * 2 * hd]),
            (slice(3 * hd, 3 * hd + 1), slice(0, hd), bq[:, b * hd : (b + 1) * hd]),
            (
                slice(3 * hd, 3 * hd + 1),
                slice(hd, 2 * hd),
                bkv[:, b * 2 * hd + hd : (b + 1) * 2 * hd],
            ),
        ]
        out, c = (outs[b % 2], b // 2) if last else (outs[0], b)
        out[c, 3 * hd :, :] = jnp.zeros((16, model), out.dtype)
        for rows, cols, value in pieces:
            if not first:
                value = value + grads_in[b, rows, cols]
            out[c, rows, cols] = value.astype(out.dtype)


def weight_gradients(dkvs, dqs, grads, blocks, here, first, last):
    parts = len(blocks)
    model = blocks[0].shape[1]
    size = 3 * (model // parts) + 16
    if last:
        outs = [((parts // 2, size, model), F32), ((parts // 2, size, model), BF)]
    else:
        outs = [((parts, size, model), F32)]
    return call(
        functools.partial(weights_kernel, parts, here, first, last, len(dkvs)),
        "weight_gradients",
        (*dkvs, *dqs, *blocks) + (() if first else (grads,)),
        outs,
        flops=4 * parts * here * model * model,
        limit=LIMITS[3],
    )


def add_kernel(rows, *refs):
    owns, nears, fars = refs[:rows], refs[rows : 2 * rows], refs[2 * rows : 3 * rows]
    out = refs[3 * rows]
    for r in range(rows):
        out[r] = owns[r][...] + nears[r][0].astype(F32) + fars[r][...].astype(F32)


def add_inputs(owns, nears, fars):
    rows = len(owns)
    (out,) = call(
        functools.partial(add_kernel, rows),
        "add_inputs",
        (*owns, *nears, *fars),
        [((rows,) + owns[0].shape, F32)],
        limit=LIMITS[3],
    )
    return out


def finish_one_kernel(a, b, qkv, bias):
    width = qkv.shape[1]
    total = a[...].astype(F32) + b[...].astype(F32)
    for c in range(3):
        qkv[c] = total[c * width : (c + 1) * width]
    line = total[3 * width : 3 * width + 1]
    bias[0:1, :] = line[:, 0:width]
    bias[1:2, :] = line[:, width : 2 * width]


def finish_two_kernel(a, b, w_out, w_in, b_in, w_back, *sums):
    width, model = w_out.shape
    units = w_back.shape[0]
    half = model // 2
    total = a[...].astype(F32) + b[...].astype(F32)
    w_out[...] = total[:width]
    at = width
    w_in[0:half, :] = total[at : at + half, 0:units]
    w_in[half:, :] = total[at : at + half, units : 2 * units]
    at += half
    w_back[...] = total[at : at + units]
    at += units
    b_in[...] = total[at : at + 1, 0:units]
    for i, out in enumerate(sums):
        out[...] = total[at + 1 + i : at + 2 + i]


def swap(value, axis, size, bit):
    return lax.ppermute(value, axis, [(i, i ^ bit) for i in range(size)])


def after(value, *others):
    return lax.optimization_barrier((value, *others))[0]


def layer(mesh_sizes, *args):
    (inputs, segments, w_qkv, b_qv, w_out, b_out, gain_one, shift_one) = args[:8]
    (w_in, b_in, w_back, b_back, gain_two, shift_two, cotangent) = args[8:]
    dp, mp = mesh_sizes
    rows, here, model = inputs.shape
    heads = HEADS
    width = w_qkv.shape[2]
    units = w_in.shape[1]

    def near(value):
        return swap(value, "mp", mp, 1)

    def far(value):
        return swap(value, "mp", mp, 2)

    *packs, two = pack(w_qkv, b_qv, w_out, w_in, b_in, w_back, segments, inputs)
    vectors = [
        v.reshape(1, model) for v in (b_out, gain_one, shift_one, b_back, gain_two, shift_two)
    ]
    fars = [far(packs[0])]
    nears = [near(after(packs[0], *vectors))]
    for r in range(1, rows):
        fars.append(far(after(packs[r], nears[r - 1])))
        nears.append(near(packs[r]))
    two_far = far(after(two, nears[-1]))
    two_near = near(two)
    boths = [near(fars[0])]
    saved, boths_of = [], []
    for r in range(rows):
        blocks = [packs[r], nears[r], fars[r], boths[r]]
        boths_of.append(blocks)
        out = attend_forward(blocks, boths_of[0], heads, here)
        saved.append(out)
        if r + 1 < rows:
            boths.append(near(after(fars[r + 1], out[2])))
    two_both = near(after(two_far, saved[max(rows - 2, 0)][2]))
    result, keep_two, send_two, dh1s, dos = middle(
        [s[3] for s in saved],
        packs,
        cotangent,
        [two, two_near, two_far, two_both],
        vectors,
        heads,
    )

    def chain(keep, send):
        got = near(send)
        mine = keep[0] + got[0].astype(F32)
        other = (keep[1] + got[1].astype(F32)).astype(BF)
        yield other
        value = mine + far(other).astype(F32)
        bit = 1
        while bit < dp:
            sent = value.astype(BF)
            yield sent
            got = swap(sent, "dp", dp, bit)
            value = sent.astype(F32) + got.astype(F32)
            bit *= 2
        yield (sent, got)

    steps = chain(keep_two, send_two)
    total_two = None
    ready = []
    grads = None
    owns, near_got, far_got = [], [], []
    pending = None

    def advance():
        nonlocal total_two, pending
        step = next(steps, None)
        if isinstance(step, tuple):
            total_two = step
        elif step is not None:
            ready.append(step)
        if pending is not None:
            other = (pending[0] + pending[1].astype(F32)).astype(BF)
            far_got.append(far(other))
            ready.append(other)
            pending = None

    for r in range(rows):
        dkvs, dqs = [], []
        last = r == rows - 1
        splits = [(0, heads, 2)] if r != 1 else [(0, heads // 2, 1), (heads // 2, heads // 2, 1)]
        for first, count, each in splits:
            e, kv, qt, _ = saved[r]
            if ready:
                e = after(e, *ready)
                ready.clear()
            dkv, dq = attend_backward(r, first, count, each, e, kv, qt, dos)
            dkvs.append(dkv)
            dqs.append(dq)
            advance()
        grads = weight_gradients(dkvs, dqs, grads, boths_of[r], here, r == 0, last)
        if last:
            tail = chain(*grads)
            other = next(tail)
            dkvs = [after(d, grads[1]) for d in dkvs]
        else:
            grads = grads[0]
        own, keep, send = input_gradients(r, dkvs, dqs, dh1s, boths_of[0])
        got = near(after(send, other) if last else send)
        owns.append(own)
        near_got.append(got)
        pending = (keep[0], got[1])
    sent = next(tail)
    final = after((pending[0] + pending[1].astype(F32)).astype(BF), sent)
    far_got.append(far(final))
    for step in steps:
        total_two = step
    for step in tail:
        total_one = step
    grad_inputs = add_inputs(owns, near_got, far_got)
    grad_out, grad_in, grad_b_in, grad_back, *sums = call(
        finish_two_kernel,
        "finish_two",
        total_two,
        [
            ((width, model), F32),
            ((model, units), F32),
            ((1, units), F32),
            ((units, model), F32),
        ]
        + [((1, model), F32)] * 6,
    )
    grad_qkv, grad_bias = call(
        finish_one_kernel,
        "finish_one",
        total_one,
        [((3, width, model), F32), ((2, width), F32)],
    )
    sums = [s.reshape(model) for s in sums]
    return (
        result,
        grad_inputs,
        grad_qkv.transpose(0, 2, 1),
        grad_bias,
        grad_out,
        sums[0],
        sums[1],
        sums[2],
        grad_in,
        grad_b_in.reshape(units),
        grad_back,
        sums[3],
        sums[4],
        sums[5],
    )


def solution(mesh):
    in_specs = (
        P("dp", "mp", None),
        P("dp", "mp"),
        P(None, None, "mp"),
        P(None, "mp"),
        P("mp", None),
        P(),
        P(),
        P(),
        P(None, "mp"),
        P("mp"),
        P("mp", None),
        P(),
        P(),
        P(),
        P("dp", "mp", None),
    )
    out_specs = (
        P("dp", "mp", None),
        P("dp", "mp", None),
        P(None, None, "mp"),
        P(None, "mp"),
        P("mp", None),
        P(),
        P(),
        P(),
        P(None, "mp"),
        P("mp"),
        P("mp", None),
        P(),
        P(),
        P(),
    )
    sizes = (mesh.shape["dp"], mesh.shape["mp"])
    return jax.shard_map(
        functools.partial(layer, sizes),
        mesh=mesh,
        in_specs=in_specs,
        out_specs=out_specs,
        check_vma=False,
    )
```

```python
import functools

import jax
import jax.numpy as jnp
from jax import lax
from jax.experimental import pallas as pl
from jax.experimental.pallas import tpu as pltpu
from jax.sharding import PartitionSpec as P

HEADS = 4
EPS = 1e-06
FAR = -(2.0**99)
GELU_C = 0.7978845608028654
GELU_A = 0.044715
LOG2_E = 1.4426950408889634
LN_2 = 0.6931471805599453

BF = jnp.bfloat16
F32 = jnp.float32

NN = (((1,), (0,)), ((), ()))
NT = (((1,), (1,)), ((), ()))
TN = (((0,), (0,)), ((), ()))

MB = 2**20
LIMITS = (10, 16, 8, 8)


def mm(left, right, dims):
    return lax.dot_general(left, right, dims, preferred_element_type=F32)


def call(kernel, name, args, outs, scratch=(), flops=0, limit=20):
    whole = pl.BlockSpec(memory_space=pltpu.VMEM)
    return pl.pallas_call(
        kernel,
        out_shape=[jax.ShapeDtypeStruct(shape, kind) for shape, kind in outs],
        in_specs=[whole] * len(args),
        out_specs=[whole] * len(outs),
        scratch_shapes=[pltpu.VMEM(shape, kind) for shape, kind in scratch],
        compiler_params=pltpu.CompilerParams(vmem_limit_bytes=limit * MB),
        cost_estimate=pl.CostEstimate(flops=flops // 20, bytes_accessed=0, transcendentals=0),
        name=name,
    )(*args)


def pack_kernel(rows, *refs):
    w_qkv, b_qv, w_out, b_out, w_in, b_in, w_back, b_back, segs, x, first = refs[:11]
    later, two, biases = refs[11:-2], refs[-2], refs[-1]
    biases[...] = jnp.zeros(biases.shape, F32)
    biases[0:1, :] = b_out[...].astype(F32).reshape(1, -1)
    biases[1:2, :] = b_back[...].astype(F32).reshape(1, -1)
    width, model = w_qkv.shape[1:]
    units = w_in.shape[1]
    half = model // 2
    here = x.shape[1]
    for r in range(rows):
        out = later[0] if r else first
        at = (r - 1) * (here + 16) if r else 0
        out[at : at + here, :] = x[r]
        at += here
        out[at : at + 16, :] = jnp.zeros((16, model), BF)
        seg = segs[r : r + 1, :]
        for digit in (jnp.bitwise_and(seg, 31), jnp.right_shift(seg, 5)):
            digit = digit.astype(F32).astype(BF)
            for start in range(0, here, model):
                out[at : at + 1, :] = digit[:, start : start + model]
                at += 1
    at = here + 16
    for c in range(3):
        first[at : at + width, :] = w_qkv[c]
        at += width
    first[at : at + 16, :] = jnp.zeros((16, model), BF)
    first[at : at + 1, 0:width] = b_qv[0:1, :]
    first[at : at + 1, width : 2 * width] = b_qv[1:2, :]
    two[0:width, :] = w_out[...]
    at = width
    two[at : at + half, 0:units] = w_in[0:half, :]
    two[at : at + half, units : 2 * units] = w_in[half:, :]
    at += half
    two[at : at + units, :] = w_back[...]
    at += units
    two[at : at + 16, :] = jnp.zeros((16, model), BF)
    two[at : at + 1, 0:units] = b_in[...]


def pack(w_qkv, b_qv, w_out, b_out, w_in, b_in, w_back, b_back, segments, inputs):
    width, units, model = w_qkv.shape[2], w_in.shape[1], w_in.shape[0]
    rows, here = segments.shape
    sizes = [here + 16 + 3 * width + 16]
    if rows > 1:
        sizes.append((rows - 1) * (here + 16))
    sizes.append(width + model // 2 + units + 16)
    args = (
        w_qkv.transpose(0, 2, 1),
        b_qv,
        w_out,
        b_out,
        w_in,
        b_in.reshape(1, units),
        w_back,
        b_back,
        segments,
        inputs,
    )
    return call(
        functools.partial(pack_kernel, rows),
        "pack",
        [pltpu.with_memory_space_constraint(a, pltpu.HBM) for a in args],
        [((size, model), BF) for size in sizes] + [((8, model), F32)],
    )


def load_weights(ws, here, hd, w_q, w_kv, bias):
    at = here + 16
    for i, w in enumerate(ws):
        w_q[i * hd : (i + 1) * hd, :] = w[at : at + hd, :]
        w_kv[i * 2 * hd : (i + 1) * 2 * hd, :] = w[at + hd : at + 3 * hd, :]
        line = w[at + 3 * hd : at + 3 * hd + 1, 0 : 2 * hd].astype(F32)
        bias[i] = jnp.broadcast_to(line, (2 * hd, 2 * hd)).T


def same_cell(x, at, here, hd):
    per = here // x.shape[1]
    low = [x[at + i : at + i + 1, :].astype(F32) for i in range(per)]
    high = [x[at + per + i : at + per + i + 1, :].astype(F32) for i in range(per)]
    low, high = jnp.concatenate(low, axis=1), jnp.concatenate(high, axis=1)
    lane = lax.broadcasted_iota(jnp.int32, (hd, here), 0).astype(F32)
    return lane == jnp.where(lane < 32, low, high + 32.0)


def value_ones(hd, length, count):
    return (lax.broadcasted_iota(jnp.int32, (hd, length), 0) < count).astype(F32).astype(BF)


def attend(queries, kvs, feats, before, put):
    hd = kvs[0].shape[0] // 2
    length = kvs[0].shape[1]
    ones = value_ones(hd, length, hd)

    def score(i):
        scores = mm(queries[i], jnp.concatenate([kvs[i][:hd], feats], axis=0), NN)
        top = jnp.max(scores, axis=-1, keepdims=True)
        top = jnp.broadcast_to(top, (scores.shape[0], 2 * hd))
        if before is None:
            return scores, top, None
        steps = jnp.maximum(jnp.ceil((top - before[i]) * LOG2_E), 0.0)
        return scores, before[i] + steps * LN_2, jnp.exp2(-steps)

    later = score(0)
    for i in range(len(queries)):
        scores, top, weight = later
        if i + 1 < len(queries):
            later = score(i + 1)
        wide = jnp.concatenate([top] * (length // (2 * hd)), axis=1)
        expo = jnp.exp(scores - wide).astype(BF)
        out = mm(expo, jnp.concatenate([kvs[i][hd:], ones], axis=0), NT)
        put(i, expo, out, top, weight)


def project(x, w, bias, put):
    hd = bias.shape[1] // 2
    proj = mm(w, x, NT)
    for i in range(w.shape[0] // (2 * hd)):
        at = 2 * i * hd
        keys = proj[at : at + hd].astype(BF)
        values = (proj[at + hd : at + 2 * hd] + bias[i, hd:, 0:1]).astype(BF)
        put(i, keys, values)


def local_kernel(rows, here, hd, *refs):
    count = 2 if rows > 1 else 1
    mine, nears = refs[:count], refs[count : 2 * count]
    ws = refs[2 * count : 2 * count + 2]
    e_out, kv_out, qt_out, qa_out, o_out, top_out = refs[2 * count + 2 : 2 * count + 8]
    w_q, w_kv, bias, feats = refs[2 * count + 8 :]
    load_weights(ws, here, hd, w_q, w_kv, bias)
    for r in range(rows):
        at = (r - 1) * (here + 16) if r else 0
        pair = (mine[min(r, 1)], nears[min(r, 1)])
        for b, x in enumerate(pair):
            same = same_cell(x, at + here, here, hd)
            feats[r, :, b * here : (b + 1) * here] = jnp.where(same, 0.0, FAR).astype(BF)
            if b == 0:
                first = same.astype(F32)

        def put(i, keys, values, r=r):
            kv_out[r, i, :hd, :] = keys
            kv_out[r, i, hd:, :] = values

        block = jnp.concatenate([x[at : at + here, :] for x in pair], axis=0)
        project(block, w_kv[...], bias, put)
        proj = mm(w_q[...], pair[0][at : at + here, :], NT)
        for i in range(2):
            qt = proj[i * hd : (i + 1) * hd] + bias[i, :hd, 0:1]
            qt = qt.astype(BF).astype(F32) * (hd**-0.5)
            qt_out[r, i] = qt.astype(BF)
            qa_out[r, i] = jnp.concatenate([qt, first], axis=0).T.astype(BF)

    def one_row(r, _):
        def put(i, expo, out, top, _):
            e_out[r, i] = expo
            o_out[r, i] = out
            top_out[r, i] = top

        queries, kvs = [qa_out[r, i] for i in range(2)], [kv_out[r, i] for i in range(2)]
        attend(queries, kvs, feats[r], None, put)
        return 0

    lax.fori_loop(0, rows, one_row, 0)


def attend_local(mine, nears, ws, rows, here, hd):
    model = mine[0].shape[1]
    return call(
        functools.partial(local_kernel, rows, here, hd),
        "attend_local",
        (*mine, *nears, *ws),
        [
            ((rows, 2, here, 2 * here), BF),
            ((rows, 2, 2 * hd, 2 * here), BF),
            ((rows, 2, hd, here), BF),
            ((rows, 2, here, 2 * hd), BF),
            ((rows, 2, here, 2 * hd), F32),
            ((rows, 2, here, 2 * hd), F32),
        ],
        [
            ((2 * hd, model), BF),
            ((4 * hd, model), BF),
            ((2, 2 * hd, 2 * hd), F32),
            ((rows, hd, 2 * here), BF),
        ],
        flops=1,
        limit=LIMITS[0],
    )


def remote_kernel(rows, here, hd, *refs):
    qs, os, tops, xs, ws = refs[:2], refs[2:4], refs[4:6], refs[6:8], refs[8:12]
    e_out, kv_out, o_out, weight_out, w_q, w_kv, bias, feats = refs[12:]
    heads = len(ws)
    load_weights(ws, here, hd, w_q, w_kv, bias)
    for n, row in enumerate(rows):
        at = (row - 1) * (here + 16) if row else 0
        for b, x in enumerate(xs):
            same = same_cell(x, at + here, here, hd)
            feats[n, :, b * here : (b + 1) * here] = jnp.where(same, 0.0, FAR).astype(BF)

        def put(i, keys, values, n=n):
            kv_out[n, i, :hd, :] = keys
            kv_out[n, i, hd:, :] = values

        block = jnp.concatenate([x[at : at + here, :] for x in xs], axis=0)
        project(block, w_kv[...], bias, put)

    def one_row(n, _):
        r = rows[0] + n

        def put(h, expo, out, _, weight):
            e_out[n, h] = expo
            o_out[n, h] = out + os[h // 2][r, h % 2] * weight
            weight_out[n, h] = weight.astype(BF)

        queries = [qs[h // 2][r, h % 2] for h in range(heads)]
        before = [tops[h // 2][r, h % 2] for h in range(heads)]
        attend(queries, [kv_out[n, h] for h in range(heads)], feats[n], before, put)
        return 0

    lax.fori_loop(0, len(rows), one_row, 0)


def attend_remote(rows, queries, outs, tops, xs, ws, here, hd):
    model = xs[0].shape[1]
    heads = len(ws)
    count = len(rows)
    return call(
        functools.partial(remote_kernel, rows, here, hd),
        "attend_remote",
        (*queries, *outs, *tops, *xs, *ws),
        [
            ((count, heads, here, 2 * here), BF),
            ((count, heads, 2 * hd, 2 * here), BF),
            ((count, heads, here, 2 * hd), F32),
            ((count, heads, here, 2 * hd), BF),
        ],
        [
            ((heads * hd, model), BF),
            ((heads * 2 * hd, model), BF),
            ((heads, 2 * hd, 2 * hd), F32),
            ((count, hd, 2 * here), BF),
        ],
        flops=1,
        limit=LIMITS[0],
    )


def middle_kernel(parts, heads, rows, *refs):
    groups = min(rows, 2)
    os, xs = refs[:groups], refs[groups : 2 * groups]
    at = 2 * groups
    cot_in = refs[at]
    ws = refs[at + 1 : at + 1 + parts]
    at += 1 + parts
    g_one, e_one, g_two, e_two, biases = refs[at : at + 5]
    result_out, keep_out, send_out, dh1_out, do_out = refs[at + 5 : at + 10]
    w_out, w_pad, w_in, w_back, o_all, x_all = refs[at + 10 : at + 16]
    dw_out, dw_in, dw_back, db_in, sums = refs[at + 16 :]
    w_pad[...] = jnp.zeros(w_pad.shape, BF)
    here, model = cot_in.shape[1:]
    hd = model // heads
    per = w_out.shape[0] // parts
    units = w_back.shape[0] // parts
    half_model = model // 2
    bias = []
    for b in range(parts):
        at = 0
        w_out[b * per : (b + 1) * per, :] = ws[b][at : at + per, :]
        w_pad[b * 2 * per : b * 2 * per + per, :] = ws[b][at : at + per, :]
        at += per
        cols = slice(b * units, (b + 1) * units)
        w_in[0:half_model, cols] = ws[b][at : at + half_model, 0:units]
        w_in[half_model:, cols] = ws[b][at : at + half_model, units : 2 * units]
        at += half_model
        w_back[b * units : (b + 1) * units, :] = ws[b][at : at + units, :]
        at += units
        bias.append(ws[b][at : at + 1, 0:units].astype(F32))
    b_in = jnp.concatenate(bias, axis=1)
    lane = lax.broadcasted_iota(jnp.int32, (here, 2 * hd), 1)
    for r in range(rows):
        o_all[r] = os[min(r, 1)][max(r - 1, 0)]
        at = (r - 1) * (here + 16) if r else 0
        x_all[r] = xs[min(r, 1)][at : at + here, :]
    for total in (dw_out, dw_in, dw_back, db_in, sums):
        total[...] = jnp.zeros(total.shape, F32)

    def norm(h):
        centre = h - jnp.mean(h, axis=-1, keepdims=True)
        rstd = lax.rsqrt(jnp.mean(centre * centre, axis=-1, keepdims=True) + EPS)
        return centre * rstd, rstd

    def norm_back(dy, gain, unit, rstd):
        dn = dy * gain
        mean = jnp.mean(dn, axis=-1, keepdims=True)
        along = jnp.mean(dn * unit, axis=-1, keepdims=True)
        return rstd * (dn - mean - unit * along)

    def down(v):
        return jnp.sum(v, axis=0, keepdims=True)

    def one_row(r, _):
        o_in = [o_all[r, h] for h in range(heads)]
        inv = [1.0 / o[:, hd : hd + 1] for o in o_in]
        normal = [o * i for o, i in zip(o_in, inv)]
        tiles = [
            jnp.where(lane < hd, normal[h], pltpu.roll(normal[h + 1], hd, 1))
            for h in range(0, heads, 2)
        ]
        att = jnp.concatenate(tiles, axis=1).astype(BF)
        h1 = x_all[r].astype(F32) + mm(att, w_out[...], NN) + biases[0:1, :]
        n1, rstd1 = norm(h1)
        y1 = n1 * g_one[...] + e_one[...]
        y1b = y1.astype(BF)
        pre = mm(y1b, w_in[...], NN) + b_in
        square = pre * pre
        th = jnp.tanh(GELU_C * pre * (1.0 + GELU_A * square))
        half = 0.5 * (1.0 + th)
        act = (pre * half).astype(BF)
        slope = half + 0.5 * pre * (1.0 - th * th) * (GELU_C * (1.0 + 3.0 * GELU_A * square))
        h2 = y1 + mm(act, w_back[...], NN) + biases[1:2, :]
        n2, rstd2 = norm(h2)
        result_out[r] = (n2 * g_two[...] + e_two[...]).astype(BF)
        cot = cot_in[r].astype(F32)
        dh2 = norm_back(cot, g_two[...], n2, rstd2)
        dz = dh2.astype(BF)
        dact = mm(dz, w_back[...], NT)
        dpre = (dact * slope).astype(BF)
        dw_back[...] += mm(act, dz, TN)
        dw_in[...] += mm(y1b, dpre, TN)
        db_in[...] += down(dpre.astype(F32))
        dy1 = mm(dpre, w_in[...], NT) + dh2
        dh1 = norm_back(dy1, g_one[...], n1, rstd1)
        dh1_out[r] = dh1
        da = dh1.astype(BF)
        dw_out[...] += mm(att, da, TN)
        dwide = mm(da, w_pad[...], NT)
        for h in range(heads):
            grad = (dwide[:, 2 * hd * h : 2 * hd * (h + 1)] * inv[h]).astype(BF)
            wide = grad.astype(F32)
            inner = jnp.sum(wide * normal[h], axis=-1, keepdims=True)
            high = inner.astype(BF).astype(F32)
            rest = inner - high
            wide = jnp.where(lane == hd, -high, jnp.where(lane == hd + 1, -rest, wide))
            do_out[r, h] = wide.astype(BF)
        rows_of = [down(dh1), down(dy1 * n1), down(dy1), down(dh2), down(cot * n2), down(cot)]
        for i, row in enumerate(rows_of):
            sums[i : i + 1, :] += row
        return 0

    lax.fori_loop(0, rows, one_row, 0)
    for b in range(parts):
        out = send_out if b % 2 else keep_out
        kind = out.dtype
        c = b // 2
        cols = slice(b * units, (b + 1) * units)
        at = 0
        out[c, at : at + per, :] = dw_out[b * per : (b + 1) * per, :].astype(kind)
        at += per
        out[c, at : at + half_model, 0:units] = dw_in[0:half_model, cols].astype(kind)
        out[c, at : at + half_model, units : 2 * units] = dw_in[half_model:, cols].astype(kind)
        at += half_model
        out[c, at : at + units, :] = dw_back[b * units : (b + 1) * units, :].astype(kind)
        at += units
        out[c, at:, :] = jnp.zeros((16, model), kind)
        out[c, at : at + 1, 0:units] = db_in[:, cols].astype(kind)
        out[c, at + 1 : at + 7, :] = sums[0:6, :].astype(kind)


def middle(os, xs, cotangent, ws, vectors, heads):
    parts = len(ws)
    rows, here, model = cotangent.shape
    hd = model // heads
    width = model // parts
    size = ws[0].shape[0]
    units = size - 16 - width - model // 2
    return call(
        functools.partial(middle_kernel, parts, heads, rows),
        "middle",
        (*os, *xs, cotangent, *ws, *vectors),
        [
            (cotangent.shape, BF),
            ((parts // 2, size, model), F32),
            ((parts // 2, size, model), BF),
            ((rows, here, model), F32),
            ((rows, heads, here, 2 * hd), BF),
        ],
        [
            ((parts * width, model), BF),
            ((2 * parts * width, model), BF),
            ((model, parts * units), BF),
            ((parts * units, model), BF),
            ((rows, heads, here, 2 * hd), F32),
            ((rows, here, model), BF),
            ((parts * width, model), F32),
            ((model, parts * units), F32),
            ((parts * units, model), F32),
            ((1, parts * units), F32),
            ((8, model), F32),
        ],
        flops=rows * 6 * here * model * (2 * model + 2 * parts * units),
        limit=LIMITS[1],
    )


def heads_step(row, n, pair, ref):
    el_in, kvl_in, qt_in = ref["el", pair], ref["kvl", pair], ref["qt", pair]
    er_in, kvr_in, do_in, weight_in = ref["er"], ref["kvr"], ref["do"], ref["weight"]
    dkv, dq, ds = ref["dkv", pair], ref["dq", pair], ref["ds"]
    hd = qt_in.shape[2]
    half = kvl_in.shape[3]
    ones = value_ones(hd, half, 2)

    def one_head(i, _):
        h = 2 * pair + i
        kvs = (kvl_in[row, i], kvr_in[n, h])
        es, do = (el_in[row, i], er_in[n, h]), do_in[row, h]
        dos = (do * weight_in[n, h], do)
        for side in range(2):
            cols = slice(side * half, (side + 1) * half)
            values = jnp.concatenate([kvs[side][hd:], ones], axis=0)
            dp = mm(dos[side], values, NN)
            ds[:, cols] = (dp * es[side].astype(F32)).astype(BF)
            dkv[i, hd:, cols] = mm(dos[side], es[side], TN)[:hd].astype(BF)
        dkv[i, :hd, :] = mm(qt_in[row, i], ds[...], NN).astype(BF)
        keys = jnp.concatenate([kv[:hd] for kv in kvs], axis=1)
        dq[i] = (mm(keys, ds[...], NT) * (hd**-0.5)).astype(BF)
        return 0

    lax.fori_loop(0, 2, one_head, 0)


def joined(refs, cols):
    return jnp.concatenate([ref[h, :, cols] for ref in refs for h in range(ref.shape[0])], axis=0)


def inputs_step(row, parts, ref):
    dkvs, dqs = [[ref[name, pair] for pair in range(parts // 2)] for name in ("dkv", "dq")]
    w_q, w_kv = ref["w_q"], ref["w_kv"]
    hd = w_q.shape[0] // parts
    here = dqs[0].shape[2]
    at = here + 16
    for b in range(parts):
        w = ref["w", b]
        w_q[b * hd : (b + 1) * hd, :] = w[at : at + hd, :]
        w_kv[b * 2 * hd : (b + 1) * 2 * hd, :] = w[at + hd : at + 3 * hd, :]
    for b in range(parts):
        dx = mm(joined(dkvs, slice(b * here, (b + 1) * here)), w_kv[...], TN)
        if b == 0:
            own = mm(joined(dqs, slice(0, here)), w_q[...], TN)
            ref["dx_own"][...] = dx + own + ref["dh1"][row]
        elif b % 2:
            ref["dx_send"][b // 2] = dx.astype(BF)
        else:
            ref["dx_keep"][...] = dx


def weights_step(row, parts, last, ref):
    dkvs, dqs = [[ref[name, pair] for pair in range(parts // 2)] for name in ("dkv", "dq")]
    here = dqs[0].shape[2]
    model = ref["x", 0].shape[1]
    hd = model // parts
    length = parts * here
    at = (row - 1) * (here + 16) if row else 0
    dq = joined(dqs, slice(0, here))
    gkv = None
    for b in range(parts):
        left = joined(dkvs, slice(b * here, (b + 1) * here))
        term = mm(left, ref["x", b][at : at + here, :], NN)
        gkv = term if gkv is None else gkv + term
    gq = mm(dq, ref["x", 0][at : at + here, :], NN)
    bq = mm(jnp.ones((8, here), BF), dq, NT)[0:1]
    bkv = mm(jnp.ones((8, length), BF), joined(dkvs, slice(0, length)), NT)[0:1]
    for b in range(parts):
        pieces = [
            (slice(0, hd), slice(0, model), gq[b * hd : (b + 1) * hd]),
            (slice(hd, 3 * hd), slice(0, model), gkv[b * 2 * hd : (b + 1) * 2 * hd]),
            (slice(3 * hd, 3 * hd + 1), slice(0, hd), bq[:, b * hd : (b + 1) * hd]),
            (
                slice(3 * hd, 3 * hd + 1),
                slice(hd, 2 * hd),
                bkv[:, b * 2 * hd + hd : (b + 1) * 2 * hd],
            ),
        ]
        out, c = (ref["grads", b % 2], b // 2) if last else (ref["grads"], b)
        out[c, 3 * hd :, :] = jnp.zeros((16, model), out.dtype)
        for rows, cols, value in pieces:
            if ("grads_in",) in ref:
                value = value + ref["grads_in",][b, rows, cols]
            out[c, rows, cols] = value.astype(out.dtype)


def backward_kernel(names, row, n, pairs, parts, want, last, *refs):
    ref = {name if len(name) > 1 else name[0]: r for name, r in zip(names, refs)}
    ref.update({name: r for name, r in zip(names, refs) if len(name) == 1})
    for pair in pairs:
        heads_step(row, n, pair, ref)
    if "weights" in want:
        weights_step(row, parts, last, ref)
    if "inputs" in want:
        inputs_step(row, parts, ref)


def backward(row, n, pairs, want, last, ins):
    parts = 4
    el = ins["el", 0]
    here, half = el.shape[2:]
    length = 2 * half
    hd = ins["kvl", 0].shape[2] // 2
    model = ins["x", 0].shape[1]
    size = 3 * hd + 16
    use = set()
    outs, scratch = {}, {}
    for pair in pairs:
        use |= {("el", pair), ("kvl", pair), ("qt", pair), ("er",), ("kvr",), ("do",), ("weight",)}
        scratch["ds",] = ((here, length), BF)
    shapes = {"dkv": ((2, 2 * hd, length), BF), "dq": ((2, hd, here), BF)}
    for pair in range(parts // 2):
        for name, shape in shapes.items():
            if pair in pairs:
                (outs if len(want) < 2 else scratch)[name, pair] = shape
            elif want:
                use.add((name, pair))
    if "inputs" in want:
        use |= {("w", b) for b in range(parts)} | {("dh1",)}
        outs["dx_own",] = ((here, model), F32)
        outs["dx_keep",] = ((here, model), F32)
        outs["dx_send",] = ((parts // 2, here, model), BF)
        scratch["w_kv",] = ((2 * model, model), BF)
        scratch["w_q",] = ((model, model), BF)
    if "weights" in want:
        use |= {("x", b) for b in range(parts)}
        if ("grads_in",) in ins:
            use.add(("grads_in",))
        if last:
            outs["grads", 0] = ((parts // 2, size, model), F32)
            outs["grads", 1] = ((parts // 2, size, model), BF)
        else:
            outs["grads",] = ((parts, size, model), F32)
    order = sorted(use, key=str)
    names = tuple(order) + tuple(outs) + tuple(scratch)
    done = call(
        functools.partial(backward_kernel, names, row, n, pairs, parts, want, last),
        "backward",
        [ins[name] for name in order],
        list(outs.values()),
        list(scratch.values()),
        limit=LIMITS[2],
    )
    return dict(zip(outs, done))


def add_kernel(rows, *refs):
    owns, nears, fars, out = refs[:rows], refs[rows : 2 * rows], refs[2 * rows : -1], refs[-1]
    for r in range(rows):
        out[r] = owns[r][...] + nears[r][0].astype(F32) + fars[r][...].astype(F32)


def add_inputs(owns, nears, fars):
    rows = len(owns)
    (out,) = call(
        functools.partial(add_kernel, rows),
        "add_inputs",
        (*owns, *nears, *fars),
        [((rows,) + owns[0].shape, F32)],
        limit=LIMITS[3],
    )
    return out


def finish_one_kernel(a, b, qkv, bias):
    width = qkv.shape[1]
    total = a[...].astype(F32) + b[...].astype(F32)
    for c in range(3):
        qkv[c] = total[c * width : (c + 1) * width]
    line = total[3 * width : 3 * width + 1]
    bias[0:1, :] = line[:, 0:width]
    bias[1:2, :] = line[:, width : 2 * width]


def finish_two_kernel(a, b, w_out, w_in, b_in, w_back, *sums):
    width, model = w_out.shape
    units = w_back.shape[0]
    half = model // 2
    total = a[...].astype(F32) + b[...].astype(F32)
    w_out[...] = total[:width]
    at = width
    w_in[0:half, :] = total[at : at + half, 0:units]
    w_in[half:, :] = total[at : at + half, units : 2 * units]
    at += half
    w_back[...] = total[at : at + units]
    at += units
    b_in[...] = total[at : at + 1, 0:units]
    for i, out in enumerate(sums):
        out[...] = total[at + 1 + i : at + 2 + i]


def swap(value, axis, size, bit):
    return lax.ppermute(value, axis, [(i, i ^ bit) for i in range(size)])


def after(value, *others):
    return lax.optimization_barrier((value, *others))[0]


def layer(mesh_sizes, *args):
    (inputs, segments, w_qkv, b_qv, w_out, b_out, gain_one, shift_one) = args[:8]
    (w_in, b_in, w_back, b_back, gain_two, shift_two, cotangent) = args[8:]
    dp, mp = mesh_sizes
    rows, here, model = inputs.shape
    heads = HEADS
    width = w_qkv.shape[2]
    units = w_in.shape[1]

    def near(value):
        return swap(value, "mp", mp, 1)

    def far(value):
        return swap(value, "mp", mp, 2)

    first, *later, two, biases = pack(
        w_qkv, b_qv, w_out, b_out, w_in, b_in, w_back, b_back, segments, inputs
    )
    vectors = [v.reshape(1, model) for v in (gain_one, shift_one, gain_two, shift_two)]
    vectors.append(biases)
    hd = model // heads
    first_far = far(first)
    first_near = near(first)
    mine, nears, fars = [first], [first_near], [first_far]
    if rows > 1:
        nears.append(near(later[0]))
        fars.append(far(after(later[0], first_near)))
        mine.append(later[0])
    two_far = far(after(two, nears[-1]))
    two_near = near(after(two, nears[-1]))
    locals_of = [attend_local(mine, nears, (first, first_near), rows, here, hd)]
    first_both = near(after(first_far, locals_of[0][2]))
    boths = [first_both]
    ws = (first, first_near, first_far, first_both)
    locals_of.append(attend_local(mine, nears, ws[2:], rows, here, hd))
    queries, outs, tops = zip(*[out[3:6] for out in locals_of])
    remotes = []
    for c, rows_of in enumerate([[0], list(range(1, rows))][: min(rows, 2)]):
        if c == 1:
            boths.append(near(after(fars[1], remotes[0][2])))
        xs = [fars[c], boths[c]]
        remotes.append(attend_remote(rows_of, queries, outs, tops, xs, ws, here, hd))
    blocks = [[group[min(r, 1)] for group in (mine, nears, fars, boths)] for r in range(rows)]
    two_both = near(after(two_far, remotes[-1][2]))
    result, keep_two, send_two, dh1s, dos = middle(
        [out[2] for out in remotes],
        mine,
        cotangent,
        [two, two_near, two_far, two_both],
        vectors,
        heads,
    )

    def halved(keep, send):
        got = near(send)
        mine = keep[0] + got[0].astype(F32)
        return mine, (keep[1] + got[1].astype(F32)).astype(BF)

    def over_dp(value, bits, tied=()):
        for bit in bits:
            sent = value.astype(BF)
            if bit == bits[-1] and tied:
                sent = after(sent, *tied)
            got = swap(sent, "dp", dp, bit)
            yield sent, got
            value = sent.astype(F32) + got.astype(F32)

    bits = [1 << k for k in range(dp.bit_length() - 1)]


    def inputs_of(r, **more):
        er, kvr, _, weight = remotes[min(r, 1)]
        ins = {("er",): er, ("kvr",): kvr, ("weight",): weight, ("do",): dos, ("dh1",): dh1s}
        for pair in range(heads // 2):
            names = (("el", pair), ("kvl", pair), ("qt", pair))
            ins.update(zip(names, locals_of[pair][:3]))
        for b in range(mp):
            ins["w", b] = ws[b]
            ins["x", b] = blocks[r][b]
        return ins

    def hold(ins, *ready):
        name = next(n for n in (("er",), ("dh1",)) if n in ins)
        ins[name] = after(ins[name], *ready)
        return ins

    def run(r, pairs, want, ins, last=False):
        return backward(r, max(r - 1, 0), pairs, want, last, ins)

    got_two = near(send_two)
    other_two = steps_two = step_two = None
    grads = None
    owns, near_got, far_got = [], [], []
    ready = []
    both = tuple(range(heads // 2))
    for r in range(rows):
        last = r == rows - 1
        ins = inputs_of(r)
        if ready:
            hold(ins, *ready)
        if r == 0:
            ins.update(run(0, both[:1], (), ins))
            got_two = after(got_two, ins["dkv", 0])
            other_two = (keep_two[1] + got_two[1].astype(F32)).astype(BF)
            far_two = far(other_two)
            hold(ins, other_two)
            ins.update(run(0, both[1:], () if last else ("inputs",), ins))
        else:
            ins.update(run(r, both, (), ins))
            flag = ins["dkv", 0]
            if r > 1 or last:
                far_got[-1] = after(far_got[-1], flag)
        flag = ins["dkv", 1]
        if steps_two is None:
            value_two = keep_two[0] + got_two[0].astype(F32) + after(far_two, flag).astype(F32)
            steps_two = over_dp(value_two, bits[::-1])
            step_two = next(steps_two)
            tie = (step_two[0],)
        else:
            tie = (step_two[1], *far_got)
        if grads is not None:
            ins["grads_in",] = grads
        if last:
            break
        if r:
            ins["dh1",] = after(ins["dh1",], *tie)
            ins.update(run(r, (), ("inputs",), ins))
        got = near(ins["dx_send",] if r else after(ins["dx_send",], *tie))
        owns.append(ins["dx_own",])
        ins["x", 0] = after(ins["x", 0], ins["dx_send",])
        grads = run(r, (), ("weights",), ins)["grads",]
        got = after(got, grads)
        near_got.append(got)
        other = (ins["dx_keep",] + got[1].astype(F32)).astype(BF)
        far_got.append(far(other))
        ready = [other, step_two[0]]
    ins["x", 0] = after(ins["x", 0], *tie)
    row = run(r, (), ("weights",), ins, True)
    mine_one, other_one = halved(row["grads", 0], row["grads", 1])
    far_one = far(other_one)
    ins["dh1",] = after(ins["dh1",], other_one)
    row = run(r, (), ("inputs",), ins)
    got = near(row["dx_send",])
    owns.append(row["dx_own",])
    near_got.append(got)
    value_one = mine_one + far_one.astype(F32)
    total_one = None
    for k, total_one in enumerate(over_dp(value_one, bits)):
        if k == 0:
            other = (row["dx_keep",] + after(got[1], total_one[0]).astype(F32)).astype(BF)
            far_got.append(far(other))
    total_two = step_two
    for total_two in steps_two:
        pass
    grad_inputs = add_inputs(owns, near_got, far_got)
    grad_out, grad_in, grad_b_in, grad_back, *sums = call(
        finish_two_kernel,
        "finish_two",
        total_two,
        [
            ((width, model), F32),
            ((model, units), F32),
            ((1, units), F32),
            ((units, model), F32),
        ]
        + [((1, model), F32)] * 6,
    )
    grad_qkv, grad_bias = call(
        finish_one_kernel,
        "finish_one",
        (after(total_one[0], grad_inputs), total_one[1]),
        [((3, width, model), F32), ((2, width), F32)],
    )
    sums = [s.reshape(model) for s in sums]
    return (
        result,
        grad_inputs,
        grad_qkv.transpose(0, 2, 1),
        grad_bias,
        grad_out,
        sums[0],
        sums[1],
        sums[2],
        grad_in,
        grad_b_in.reshape(units),
        grad_back,
        sums[3],
        sums[4],
        sums[5],
    )


def solution(mesh):
    in_specs = (
        P("dp", "mp", None),
        P("dp", "mp"),
        P(None, None, "mp"),
        P(None, "mp"),
        P("mp", None),
        P(),
        P(),
        P(),
        P(None, "mp"),
        P("mp"),
        P("mp", None),
        P(),
        P(),
        P(),
        P("dp", "mp", None),
    )
    out_specs = (
        P("dp", "mp", None),
        P("dp", "mp", None),
        P(None, None, "mp"),
        P(None, "mp"),
        P("mp", None),
        P(),
        P(),
        P(),
        P(None, "mp"),
        P("mp"),
        P("mp", None),
        P(),
        P(),
        P(),
    )
    sizes = (mesh.shape["dp"], mesh.shape["mp"])
    return jax.shard_map(
        functools.partial(layer, sizes),
        mesh=mesh,
        in_specs=in_specs,
        out_specs=out_specs,
        check_vma=False,
    )
```

```python
import functools

import jax
import jax.numpy as jnp
from jax import lax
from jax.experimental import pallas as pl
from jax.experimental.pallas import tpu as pltpu
from jax.sharding import PartitionSpec as P

HEADS = 4
EPS = 1e-06
FAR = -(2.0**99)
GELU_C = 0.7978845608028654
GELU_A = 0.044715
LOG2_E = 1.4426950408889634
LN_2 = 0.6931471805599453

BF = jnp.bfloat16
F32 = jnp.float32

NN = (((1,), (0,)), ((), ()))
NT = (((1,), (1,)), ((), ()))
TN = (((0,), (0,)), ((), ()))

MB = 2**20
LIMITS = (10, 12, 8, 8)


def mm(left, right, dims):
    return lax.dot_general(left, right, dims, preferred_element_type=F32)


def call(kernel, name, args, outs, scratch=(), flops=0, limit=20):
    whole = pl.BlockSpec(memory_space=pltpu.VMEM)
    return pl.pallas_call(
        kernel,
        out_shape=[jax.ShapeDtypeStruct(shape, kind) for shape, kind in outs],
        in_specs=[whole] * len(args),
        out_specs=[whole] * len(outs),
        scratch_shapes=[pltpu.VMEM(shape, kind) for shape, kind in scratch],
        compiler_params=pltpu.CompilerParams(vmem_limit_bytes=limit * MB),
        cost_estimate=pl.CostEstimate(flops=flops // 20, bytes_accessed=0, transcendentals=0),
        name=name,
    )(*args)


def pack_kernel(rows, *refs):
    w_qkv, b_qv, w_out, b_out, w_in, b_in, w_back, b_back, segs, x, first = refs[:11]
    later, two, biases = refs[11:-2], refs[-2], refs[-1]
    biases[...] = jnp.zeros(biases.shape, F32)
    biases[0:1, :] = b_out[...].astype(F32).reshape(1, -1)
    biases[1:2, :] = b_back[...].astype(F32).reshape(1, -1)
    width, model = w_qkv.shape[1:]
    units = w_in.shape[1]
    half = model // 2
    here = x.shape[1]
    for r in range(rows):
        out = later[0] if r else first
        at = (r - 1) * (here + 16) if r else 0
        out[at : at + here, :] = x[r]
        at += here
        out[at : at + 16, :] = jnp.zeros((16, model), BF)
        seg = segs[r : r + 1, :]
        for digit in (jnp.bitwise_and(seg, 31), jnp.right_shift(seg, 5)):
            digit = digit.astype(F32).astype(BF)
            for start in range(0, here, model):
                out[at : at + 1, :] = digit[:, start : start + model]
                at += 1
    at = here + 16
    for c in range(3):
        first[at : at + width, :] = w_qkv[c]
        at += width
    first[at : at + 16, :] = jnp.zeros((16, model), BF)
    first[at : at + 1, 0:width] = b_qv[0:1, :]
    first[at : at + 1, width : 2 * width] = b_qv[1:2, :]
    two[0:width, :] = w_out[...]
    at = width
    two[at : at + half, 0:units] = w_in[0:half, :]
    two[at : at + half, units : 2 * units] = w_in[half:, :]
    at += half
    two[at : at + units, :] = w_back[...]
    at += units
    two[at : at + 16, :] = jnp.zeros((16, model), BF)
    two[at : at + 1, 0:units] = b_in[...]


def pack(w_qkv, b_qv, w_out, b_out, w_in, b_in, w_back, b_back, segments, inputs):
    width, units, model = w_qkv.shape[2], w_in.shape[1], w_in.shape[0]
    rows, here = segments.shape
    sizes = [here + 16 + 3 * width + 16]
    if rows > 1:
        sizes.append((rows - 1) * (here + 16))
    sizes.append(width + model // 2 + units + 16)
    args = (
        w_qkv.transpose(0, 2, 1),
        b_qv,
        w_out,
        b_out,
        w_in,
        b_in.reshape(1, units),
        w_back,
        b_back,
        segments,
        inputs,
    )
    return call(
        functools.partial(pack_kernel, rows),
        "pack",
        [pltpu.with_memory_space_constraint(a, pltpu.HBM) for a in args],
        [((size, model), BF) for size in sizes] + [((8, model), F32)],
    )


def load_weights(ws, here, hd, w_q, w_kv, bias):
    at = here + 16
    for i, w in enumerate(ws):
        w_q[i * hd : (i + 1) * hd, :] = w[at : at + hd, :]
        w_kv[i * 2 * hd : (i + 1) * 2 * hd, :] = w[at + hd : at + 3 * hd, :]
        line = w[at + 3 * hd : at + 3 * hd + 1, 0 : 2 * hd].astype(F32)
        bias[i] = jnp.broadcast_to(line, (2 * hd, 2 * hd)).T


def same_cell(x, at, here, hd):
    per = here // x.shape[1]
    low = [x[at + i : at + i + 1, :].astype(F32) for i in range(per)]
    high = [x[at + per + i : at + per + i + 1, :].astype(F32) for i in range(per)]
    low, high = jnp.concatenate(low, axis=1), jnp.concatenate(high, axis=1)
    lane = lax.broadcasted_iota(jnp.int32, (hd, here), 0).astype(F32)
    return lane == jnp.where(lane < 32, low, high + 32.0)


def value_ones(hd, length, count):
    return (lax.broadcasted_iota(jnp.int32, (hd, length), 0) < count).astype(F32).astype(BF)


def attend(queries, kvs, feats, before, put):
    hd = kvs[0].shape[0] // 2
    length = kvs[0].shape[1]
    ones = value_ones(hd, length, hd)

    def score(i):
        scores = mm(queries[i], jnp.concatenate([kvs[i][:hd], feats], axis=0), NN)
        top = jnp.max(scores, axis=-1, keepdims=True)
        top = jnp.broadcast_to(top, (scores.shape[0], 2 * hd))
        if before is None:
            return scores, top, None
        steps = jnp.maximum(jnp.ceil((top - before[i]) * LOG2_E), 0.0)
        return scores, before[i] + steps * LN_2, jnp.exp2(-steps)

    later = score(0)
    for i in range(len(queries)):
        scores, top, weight = later
        if i + 1 < len(queries):
            later = score(i + 1)
        wide = jnp.concatenate([top] * (length // (2 * hd)), axis=1)
        expo = jnp.exp(scores - wide).astype(BF)
        out = mm(expo, jnp.concatenate([kvs[i][hd:], ones], axis=0), NT)
        put(i, expo, out, top, weight)


def project(x, w, bias, put):
    hd = bias.shape[1] // 2
    proj = mm(w, x, NT)
    for i in range(w.shape[0] // (2 * hd)):
        at = 2 * i * hd
        keys = proj[at : at + hd].astype(BF)
        values = (proj[at + hd : at + 2 * hd] + bias[i, hd:, 0:1]).astype(BF)
        put(i, keys, values)


def local_kernel(rows, here, hd, *refs):
    count = 2 if rows > 1 else 1
    mine, nears = refs[:count], refs[count : 2 * count]
    ws = refs[2 * count : 2 * count + 2]
    e_out, kv_out, qt_out, qa_out, o_out = refs[2 * count + 2 : 2 * count + 7]
    w_q, w_kv, bias, feats = refs[2 * count + 7 :]
    load_weights(ws, here, hd, w_q, w_kv, bias)
    for r in range(rows):
        at = (r - 1) * (here + 16) if r else 0
        pair = (mine[min(r, 1)], nears[min(r, 1)])
        for b, x in enumerate(pair):
            same = same_cell(x, at + here, here, hd)
            feats[r, :, b * here : (b + 1) * here] = jnp.where(same, 0.0, FAR).astype(BF)
            if b == 0:
                first = same.astype(F32)

        def put(i, keys, values, r=r):
            kv_out[r, i, :hd, :] = keys
            kv_out[r, i, hd:, :] = values

        block = jnp.concatenate([x[at : at + here, :] for x in pair], axis=0)
        project(block, w_kv[...], bias, put)
        proj = mm(w_q[...], pair[0][at : at + here, :], NT)
        for i in range(2):
            qt = proj[i * hd : (i + 1) * hd] + bias[i, :hd, 0:1]
            qt = qt.astype(BF).astype(F32) * (hd**-0.5)
            qt_out[r, i] = qt.astype(BF)
            qa_out[r, i] = jnp.concatenate([qt, first], axis=0).T.astype(BF)

    lane = lax.broadcasted_iota(jnp.int32, (here, 2 * hd), 1)

    def one_row(r, _):
        def put(i, expo, out, top, _):
            e_out[r, i] = expo
            o_out[r, i] = jnp.where(lane < 3 * hd // 2, out, top)

        queries, kvs = [qa_out[r, i] for i in range(2)], [kv_out[r, i] for i in range(2)]
        attend(queries, kvs, feats[r], None, put)
        return 0

    lax.fori_loop(0, rows, one_row, 0)


def attend_local(mine, nears, ws, rows, here, hd):
    model = mine[0].shape[1]
    return call(
        functools.partial(local_kernel, rows, here, hd),
        "attend_local",
        (*mine, *nears, *ws),
        [
            ((rows, 2, here, 2 * here), BF),
            ((rows, 2, 2 * hd, 2 * here), BF),
            ((rows, 2, hd, here), BF),
            ((rows, 2, here, 2 * hd), BF),
            ((rows, 2, here, 2 * hd), F32),
        ],
        [
            ((2 * hd, model), BF),
            ((4 * hd, model), BF),
            ((2, 2 * hd, 2 * hd), F32),
            ((rows, hd, 2 * here), BF),
        ],
        flops=1,
        limit=LIMITS[0],
    )


def remote_kernel(rows, here, hd, *refs):
    qs, os, xs, ws = refs[:2], refs[2:4], refs[4:6], refs[6:10]
    e_out, kv_out, o_out, weight_out, w_q, w_kv, bias, feats = refs[10:]
    heads = len(ws)
    load_weights(ws, here, hd, w_q, w_kv, bias)
    for n, row in enumerate(rows):
        at = (row - 1) * (here + 16) if row else 0
        for b, x in enumerate(xs):
            same = same_cell(x, at + here, here, hd)
            feats[n, :, b * here : (b + 1) * here] = jnp.where(same, 0.0, FAR).astype(BF)

        def put(i, keys, values, n=n):
            kv_out[n, i, :hd, :] = keys
            kv_out[n, i, hd:, :] = values

        block = jnp.concatenate([x[at : at + here, :] for x in xs], axis=0)
        project(block, w_kv[...], bias, put)

    def one_row(n, _):
        r = rows[0] + n

        def put(h, expo, out, _, weight):
            e_out[n, h] = expo
            o_out[n, h] = out + os[h // 2][r, h % 2] * weight
            weight_out[n, h] = weight.astype(BF)

        queries = [qs[h // 2][r, h % 2] for h in range(heads)]
        at = 3 * hd // 2
        before = [
            jnp.broadcast_to(os[h // 2][r, h % 2, :, at : at + 1], (here, 2 * hd))
            for h in range(heads)
        ]
        attend(queries, [kv_out[n, h] for h in range(heads)], feats[n], before, put)
        return 0

    lax.fori_loop(0, len(rows), one_row, 0)


def attend_remote(rows, queries, outs, xs, ws, here, hd):
    model = xs[0].shape[1]
    heads = len(ws)
    count = len(rows)
    return call(
        functools.partial(remote_kernel, rows, here, hd),
        "attend_remote",
        (*queries, *outs, *xs, *ws),
        [
            ((count, heads, here, 2 * here), BF),
            ((count, heads, 2 * hd, 2 * here), BF),
            ((count, heads, here, 2 * hd), F32),
            ((count, heads, here, 2 * hd), BF),
        ],
        [
            ((heads * hd, model), BF),
            ((heads * 2 * hd, model), BF),
            ((heads, 2 * hd, 2 * hd), F32),
            ((count, hd, 2 * here), BF),
        ],
        flops=1,
        limit=LIMITS[0],
    )


def middle_kernel(parts, heads, rows, *refs):
    groups = min(rows, 2)
    os, xs = refs[:groups], refs[groups : 2 * groups]
    at = 2 * groups
    cot_in = refs[at]
    ws = refs[at + 1 : at + 1 + parts]
    at += 1 + parts
    g_one, e_one, g_two, e_two, biases = refs[at : at + 5]
    result_out, keep_out, send_out, dh1_out, do_out = refs[at + 5 : at + 10]
    w_out, w_pad, w_in, w_back = refs[at + 10 : at + 14]
    dw_out, dw_in, dw_back, db_in, db_values, sums = refs[at + 14 :]
    w_pad[...] = jnp.zeros(w_pad.shape, BF)
    here, model = cot_in.shape[1:]
    hd = model // heads
    per = w_out.shape[0] // parts
    units = w_back.shape[0] // parts
    half_model = model // 2
    bias = []
    for b in range(parts):
        at = 0
        w_out[b * per : (b + 1) * per, :] = ws[b][at : at + per, :]
        w_pad[b * 2 * per : b * 2 * per + per, :] = ws[b][at : at + per, :]
        at += per
        cols = slice(b * units, (b + 1) * units)
        w_in[0:half_model, cols] = ws[b][at : at + half_model, 0:units]
        w_in[half_model:, cols] = ws[b][at : at + half_model, units : 2 * units]
        at += half_model
        w_back[b * units : (b + 1) * units, :] = ws[b][at : at + units, :]
        at += units
        bias.append(ws[b][at : at + 1, 0:units].astype(F32))
    b_in = jnp.concatenate(bias, axis=1)
    lane = lax.broadcasted_iota(jnp.int32, (here, 2 * hd), 1)

    def o_of(r, h):
        if groups == 1:
            return os[0][r, h]
        return jnp.where(r == 0, os[0][0, h], os[1][jnp.maximum(r - 1, 0), h])

    def x_of(r):
        first = xs[0][0:here, :].astype(F32)
        if groups == 1:
            return first
        at = pl.multiple_of(jnp.maximum(r - 1, 0) * (here + 16), 16)
        return jnp.where(r == 0, first, xs[1][pl.ds(at, here), :].astype(F32))

    for total in (dw_out, dw_in, dw_back, db_in, db_values, sums):
        total[...] = jnp.zeros(total.shape, F32)

    def norm(h):
        centre = h - jnp.mean(h, axis=-1, keepdims=True)
        rstd = lax.rsqrt(jnp.mean(centre * centre, axis=-1, keepdims=True) + EPS)
        return centre * rstd, rstd

    def norm_back(dy, gain, unit, rstd):
        dn = dy * gain
        mean = jnp.mean(dn, axis=-1, keepdims=True)
        along = jnp.mean(dn * unit, axis=-1, keepdims=True)
        return rstd * (dn - mean - unit * along)

    def down(v):
        return jnp.sum(v, axis=0, keepdims=True)

    def one_row(r, _):
        o_in = [o_of(r, h) for h in range(heads)]
        inv = [1.0 / o[:, hd : hd + 1] for o in o_in]
        normal = [o * i for o, i in zip(o_in, inv)]
        tiles = [
            jnp.where(lane < hd, normal[h], pltpu.roll(normal[h + 1], hd, 1))
            for h in range(0, heads, 2)
        ]
        att = jnp.concatenate(tiles, axis=1).astype(BF)
        h1 = x_of(r) + mm(att, w_out[...], NN) + biases[0:1, :]
        n1, rstd1 = norm(h1)
        y1 = n1 * g_one[...] + e_one[...]
        y1b = y1.astype(BF)
        pre = mm(y1b, w_in[...], NN) + b_in
        square = pre * pre
        half = 0.5 + 0.5 * jnp.tanh(pre * (GELU_C + GELU_C * GELU_A * square))
        full = pre * half
        act = full.astype(BF)
        slope = half + full * (1.0 - half) * (2.0 * GELU_C + 6.0 * GELU_C * GELU_A * square)
        h2 = y1 + mm(act, w_back[...], NN) + biases[1:2, :]
        n2, rstd2 = norm(h2)
        result_out[r] = (n2 * g_two[...] + e_two[...]).astype(BF)
        cot = cot_in[r].astype(F32)
        dh2 = norm_back(cot, g_two[...], n2, rstd2)
        dz = dh2.astype(BF)
        dact = mm(dz, w_back[...], NT)
        dpre = (dact * slope).astype(BF)
        dw_back[...] += mm(act, dz, TN)
        dw_in[...] += mm(y1b, dpre, TN)
        db_in[...] += down(dpre.astype(F32))
        dy1 = mm(dpre, w_in[...], NT) + dh2
        dh1 = norm_back(dy1, g_one[...], n1, rstd1)
        dh1_out[r] = dh1
        da = dh1.astype(BF)
        dw_out[...] += mm(att, da, TN)
        dwide = mm(da, w_pad[...], NT)
        for h in range(heads):
            grad = (dwide[:, 2 * hd * h : 2 * hd * (h + 1)] * inv[h]).astype(BF)
            wide = grad.astype(F32)
            inner = jnp.sum(wide * normal[h], axis=-1, keepdims=True)
            high = inner.astype(BF).astype(F32)
            rest = inner - high
            wide = jnp.where(lane == hd, -high, jnp.where(lane == hd + 1, -rest, wide))
            do_out[r, h] = wide.astype(BF)
        db_values[...] += down(dwide)
        rows_of = [down(dh1), down(dy1 * n1), down(dy1), down(dh2), down(cot * n2), down(cot)]
        for i, row in enumerate(rows_of):
            sums[i : i + 1, :] += row
        return 0

    lax.fori_loop(0, rows, one_row, 0)
    for b in range(parts):
        out = send_out if b % 2 else keep_out
        kind = out.dtype
        c = b // 2
        cols = slice(b * units, (b + 1) * units)
        at = 0
        out[c, at : at + per, :] = dw_out[b * per : (b + 1) * per, :].astype(kind)
        at += per
        out[c, at : at + half_model, 0:units] = dw_in[0:half_model, cols].astype(kind)
        out[c, at : at + half_model, units : 2 * units] = dw_in[half_model:, cols].astype(kind)
        at += half_model
        out[c, at : at + units, :] = dw_back[b * units : (b + 1) * units, :].astype(kind)
        at += units
        out[c, at:, :] = jnp.zeros((16, model), kind)
        out[c, at : at + 1, 0:units] = db_in[:, cols].astype(kind)
        out[c, at + 1 : at + 7, :] = sums[0:6, :].astype(BF).astype(kind)
        line = db_values[:, 2 * per * b : 2 * per * b + per]
        out[c, at + 7 : at + 8, 0:per] = line.astype(kind)


def middle(os, xs, cotangent, ws, vectors, heads):
    parts = len(ws)
    rows, here, model = cotangent.shape
    hd = model // heads
    width = model // parts
    size = ws[0].shape[0]
    units = size - 16 - width - model // 2
    return call(
        functools.partial(middle_kernel, parts, heads, rows),
        "middle",
        (*os, *xs, cotangent, *ws, *vectors),
        [
            (cotangent.shape, BF),
            ((parts // 2, size, model), F32),
            ((parts // 2, size, model), BF),
            ((rows, here, model), F32),
            ((rows, heads, here, 2 * hd), BF),
        ],
        [
            ((parts * width, model), BF),
            ((2 * parts * width, model), BF),
            ((model, parts * units), BF),
            ((parts * units, model), BF),
            ((parts * width, model), F32),
            ((model, parts * units), F32),
            ((parts * units, model), F32),
            ((1, parts * units), F32),
            ((1, 2 * model), F32),
            ((8, model), F32),
        ],
        flops=rows * 6 * here * model * (2 * model + 2 * parts * units),
        limit=LIMITS[1],
    )


def heads_step(row, n, pair, ref):
    el_in, kvl_in, qt_in = ref["el", pair], ref["kvl", pair], ref["qt", pair]
    er_in, kvr_in, do_in, weight_in = ref["er"], ref["kvr"], ref["do"], ref["weight"]
    dkv, dq, ds = ref["dkv", pair], ref["dq", pair], ref["ds"]
    hd = qt_in.shape[2]
    half = kvl_in.shape[3]
    ones = value_ones(hd, half, 2)

    def one_head(i, _):
        h = 2 * pair + i
        kvs = (kvl_in[row, i], kvr_in[n, h])
        es, do = (el_in[row, i], er_in[n, h]), do_in[row, h]
        dos = (do * weight_in[n, h], do)
        for side in range(2):
            cols = slice(side * half, (side + 1) * half)
            values = jnp.concatenate([kvs[side][hd:], ones], axis=0)
            dp = mm(dos[side], values, NN)
            ds[:, cols] = (dp * es[side].astype(F32)).astype(BF)
            dkv[i, hd:, cols] = mm(dos[side], es[side], TN)[:hd].astype(BF)
        dkv[i, :hd, :] = mm(qt_in[row, i], ds[...], NN).astype(BF)
        keys = jnp.concatenate([kv[:hd] for kv in kvs], axis=1)
        dq[i] = (mm(keys, ds[...], NT) * (hd**-0.5)).astype(BF)
        return 0

    lax.fori_loop(0, 2, one_head, 0)


def joined(refs, cols):
    return jnp.concatenate([ref[h, :, cols] for ref in refs for h in range(ref.shape[0])], axis=0)


def inputs_step(row, parts, ref):
    dkvs, dqs = [[ref[name, pair] for pair in range(parts // 2)] for name in ("dkv", "dq")]
    w_q, w_kv = ref["w_q"], ref["w_kv"]
    hd = w_q.shape[0] // parts
    here = dqs[0].shape[2]
    at = here + 16
    for b in range(parts):
        w = ref["w", b]
        w_q[b * hd : (b + 1) * hd, :] = w[at : at + hd, :]
        w_kv[b * 2 * hd : (b + 1) * 2 * hd, :] = w[at + hd : at + 3 * hd, :]
    for b in range(parts):
        dx = mm(joined(dkvs, slice(b * here, (b + 1) * here)), w_kv[...], TN)
        if b == 0:
            own = mm(joined(dqs, slice(0, here)), w_q[...], TN)
            ref["dx_own"][...] = dx + own + ref["dh1"][row]
        elif b % 2:
            ref["dx_send"][b // 2] = dx.astype(BF)
        else:
            ref["dx_keep"][...] = dx


def weights_step(row, heads, parts, ref):
    dkvs = [ref["dkv", h // 2][h % 2] for h in heads]
    dq = jnp.concatenate([ref["dq", h // 2][h % 2] for h in heads], axis=0)
    here = dq.shape[1]
    model = ref["x", 0].shape[1]
    hd = model // parts
    at = (row - 1) * (here + 16) if row else 0
    gkv = None
    for b in range(parts):
        left = jnp.concatenate([d[:, b * here : (b + 1) * here] for d in dkvs], axis=0)
        term = mm(left, ref["x", b][at : at + here, :], NN)
        gkv = term if gkv is None else gkv + term
    gq = mm(dq, ref["x", 0][at : at + here, :], NN)
    bq = mm(jnp.ones((8, here), BF), dq, NT)[0:1]
    out = ref["grads",]
    for c, h in enumerate(heads):
        pieces = [
            (slice(0, hd), slice(0, model), gq[c * hd : (c + 1) * hd]),
            (slice(hd, 3 * hd), slice(0, model), gkv[c * 2 * hd : (c + 1) * 2 * hd]),
            (slice(3 * hd, 3 * hd + 1), slice(0, hd), bq[:, c * hd : (c + 1) * hd]),
        ]
        out[c, 3 * hd :, :] = jnp.zeros((16, model), out.dtype)
        for rows, cols, value in pieces:
            if ("grads_in",) in ref:
                value = value + ref["grads_in",][h, rows, cols]
            out[c, rows, cols] = value.astype(out.dtype)


def backward_kernel(names, row, n, pairs, parts, want, some, *refs):
    ref = {name if len(name) > 1 else name[0]: r for name, r in zip(names, refs)}
    ref.update({name: r for name, r in zip(names, refs) if len(name) == 1})
    for pair in pairs:
        heads_step(row, n, pair, ref)
    if "weights" in want:
        weights_step(row, some, parts, ref)
    if "inputs" in want:
        inputs_step(row, parts, ref)


def backward(row, n, pairs, want, ins, some=(0, 1, 2, 3), kind=F32):
    parts = 4
    el = ins["el", 0]
    here, half = el.shape[2:]
    length = 2 * half
    hd = ins["kvl", 0].shape[2] // 2
    model = ins["x", 0].shape[1]
    size = 3 * hd + 16
    use = set()
    outs, scratch = {}, {}
    for pair in pairs:
        use |= {("el", pair), ("kvl", pair), ("qt", pair), ("er",), ("kvr",), ("do",), ("weight",)}
        scratch["ds",] = ((here, length), BF)
    shapes = {"dkv": ((2, 2 * hd, length), BF), "dq": ((2, hd, here), BF)}
    for pair in range(parts // 2):
        for name, shape in shapes.items():
            if pair in pairs:
                (outs if len(want) < 2 else scratch)[name, pair] = shape
            elif want:
                use.add((name, pair))
    if "inputs" in want:
        use |= {("w", b) for b in range(parts)} | {("dh1",)}
        outs["dx_own",] = ((here, model), F32)
        outs["dx_keep",] = ((here, model), F32)
        outs["dx_send",] = ((parts // 2, here, model), BF)
        scratch["w_kv",] = ((2 * model, model), BF)
        scratch["w_q",] = ((model, model), BF)
    if "weights" in want:
        use |= {("x", b) for b in range(parts)}
        if ("grads_in",) in ins:
            use.add(("grads_in",))
        outs["grads",] = ((len(some), size, model), kind)
    order = sorted(use, key=str)
    names = tuple(order) + tuple(outs) + tuple(scratch)
    done = call(
        functools.partial(backward_kernel, names, row, n, pairs, parts, want, some),
        "backward",
        [ins[name] for name in order],
        list(outs.values()),
        list(scratch.values()),
        limit=LIMITS[2],
    )
    return dict(zip(outs, done))


def add_kernel(rows, *refs):
    owns, nears, fars, out = refs[:rows], refs[rows : 2 * rows], refs[2 * rows : -1], refs[-1]
    for r in range(rows):
        out[r] = owns[r][...] + nears[r][0].astype(F32) + fars[r][...].astype(F32)


def add_inputs(owns, nears, fars):
    rows = len(owns)
    (out,) = call(
        functools.partial(add_kernel, rows),
        "add_inputs",
        (*owns, *nears, *fars),
        [((rows,) + owns[0].shape, F32)],
        limit=LIMITS[3],
    )
    return out


def finish_one_kernel(a, b, values, qkv, bias):
    width = qkv.shape[1]
    total = a[...].astype(F32) + b[...].astype(F32)
    for c in range(3):
        qkv[c] = total[c * width : (c + 1) * width]
    bias[0:1, :] = total[3 * width : 3 * width + 1, 0:width]
    bias[1:2, :] = values[:, 0:width]


def finish_two_kernel(a, b, w_out, w_in, b_in, w_back, values, *sums):
    width, model = w_out.shape
    units = w_back.shape[0]
    half = model // 2
    total = a[...].astype(F32) + b[...].astype(F32)
    w_out[...] = total[:width]
    at = width
    w_in[0:half, :] = total[at : at + half, 0:units]
    w_in[half:, :] = total[at : at + half, units : 2 * units]
    at += half
    w_back[...] = total[at : at + units]
    at += units
    b_in[...] = total[at : at + 1, 0:units]
    values[...] = total[at + 7 : at + 8]
    for i, out in enumerate(sums):
        out[...] = total[at + 1 + i : at + 2 + i]


def swap(value, axis, size, bit):
    return lax.ppermute(value, axis, [(i, i ^ bit) for i in range(size)])


def after(value, *others):
    return lax.optimization_barrier((value, *others))[0]


def layer(mesh_sizes, *args):
    (inputs, segments, w_qkv, b_qv, w_out, b_out, gain_one, shift_one) = args[:8]
    (w_in, b_in, w_back, b_back, gain_two, shift_two, cotangent) = args[8:]
    dp, mp = mesh_sizes
    rows, here, model = inputs.shape
    heads = HEADS
    width = w_qkv.shape[2]
    units = w_in.shape[1]

    def near(value):
        return swap(value, "mp", mp, 1)

    def far(value):
        return swap(value, "mp", mp, 2)

    first, *later, two, biases = pack(
        w_qkv, b_qv, w_out, b_out, w_in, b_in, w_back, b_back, segments, inputs
    )
    vectors = [v.reshape(1, model) for v in (gain_one, shift_one, gain_two, shift_two)]
    vectors.append(biases)
    hd = model // heads
    first_far = far(first)
    first_near = near(first)
    mine, nears, fars = [first], [first_near], [first_far]
    if rows > 1:
        nears.append(near(later[0]))
        fars.append(far(after(later[0], first_near)))
        mine.append(later[0])
    two_far = far(after(two, nears[-1]))
    two_near = near(after(two, nears[-1]))
    locals_of = [attend_local(mine, nears, (first, first_near), rows, here, hd)]
    first_both = near(after(first_far, locals_of[0][2]))
    boths = [first_both]
    ws = (first, first_near, first_far, first_both)
    locals_of.append(attend_local(mine, nears, ws[2:], rows, here, hd))
    queries, outs = zip(*[out[3:5] for out in locals_of])
    remotes = []
    for c, rows_of in enumerate([[0], list(range(1, rows))][: min(rows, 2)]):
        if c == 1:
            boths.append(near(after(fars[1], remotes[0][2])))
        xs = [fars[c], boths[c]]
        remotes.append(attend_remote(rows_of, queries, outs, xs, ws, here, hd))
    blocks = [[group[min(r, 1)] for group in (mine, nears, fars, boths)] for r in range(rows)]
    two_both = near(after(two_far, remotes[-1][2]))
    result, keep_two, send_two, dh1s, dos = middle(
        [out[2] for out in remotes],
        mine,
        cotangent,
        [two, two_near, two_far, two_both],
        vectors,
        heads,
    )

    def over_dp(value, even, odd):
        for bits in zip(even, odd):
            pairs = []
            for d in range(dp):
                for m in range(mp):
                    pairs.append((d * mp + m, (d ^ bits[m % 2]) * mp + m))
            sent = value.astype(BF)
            got = lax.ppermute(sent, ("dp", "mp"), pairs)
            yield sent, got
            value = sent.astype(F32) + got.astype(F32)

    bits = [1 << k for k in range(dp.bit_length() - 1)]


    def inputs_of(r, **more):
        er, kvr, _, weight = remotes[min(r, 1)]
        ins = {("er",): er, ("kvr",): kvr, ("weight",): weight, ("do",): dos, ("dh1",): dh1s}
        for pair in range(heads // 2):
            names = (("el", pair), ("kvl", pair), ("qt", pair))
            ins.update(zip(names, locals_of[pair][:3]))
        for b in range(mp):
            ins["w", b] = ws[b]
            ins["x", b] = blocks[r][b]
        return ins

    def hold(ins, *ready):
        name = next(n for n in (("er",), ("dh1",)) if n in ins)
        ins[name] = after(ins[name], *ready)
        return ins

    def run(r, pairs, want, ins, **more):
        return backward(r, max(r - 1, 0), pairs, want, ins, **more)

    got_two = near(send_two)
    other_two = steps_two = step_two = None
    grads = None
    owns, near_got, far_got = [], [], []
    ready = []
    both = tuple(range(heads // 2))
    for r in range(rows):
        last = r == rows - 1
        ins = inputs_of(r)
        if ready:
            hold(ins, *ready)
        if r == 0:
            ins.update(run(0, both[:1], (), ins))
            got_two = after(got_two, ins["dkv", 0])
            other_two = (keep_two[1] + got_two[1].astype(F32)).astype(BF)
            far_two = far(other_two)
            hold(ins, other_two)
            ins.update(run(0, both[1:], () if last else ("inputs",), ins))
        else:
            ins.update(run(r, both, (), ins))
            flag = ins["dkv", 0]
            if r > 1 or last:
                far_got[-1] = after(far_got[-1], flag)
        flag = ins["dkv", 1]
        if steps_two is None:
            value_two = (keep_two[0] + got_two[0].astype(F32)).astype(BF).astype(F32)
            value_two = value_two + after(far_two, flag).astype(F32)
            steps_two = over_dp(value_two, bits[::-1], bits[::-1])
            step_two = next(steps_two)
            tie = (step_two[0],)
        else:
            tie = (step_two[1], *far_got)
        if grads is not None:
            ins["grads_in",] = grads
        if last:
            break
        if r:
            ins["dh1",] = after(ins["dh1",], *tie)
            ins.update(run(r, (), ("inputs",), ins))
        got = near(ins["dx_send",] if r else after(ins["dx_send",], *tie))
        owns.append(ins["dx_own",])
        ins["x", 0] = after(ins["x", 0], ins["dx_send",])
        grads = run(r, (), ("weights",), ins)["grads",]
        got = after(got, grads)
        near_got.append(got)
        other = (ins["dx_keep",] + got[1].astype(F32)).astype(BF)
        far_got.append(far(other))
        ready = [other, step_two[0]]
    ins["x", 0] = after(ins["x", 0], *tie)
    send = run(r, (), ("weights",), ins, some=(1, 3), kind=BF)["grads",]
    got = near(send)
    ins["x", 0] = after(ins["x", 0], send)
    keep = run(r, (), ("weights",), ins, some=(0, 2))["grads",]
    mine_one = keep[0] + got[0].astype(F32)
    other_one = (keep[1] + got[1].astype(F32)).astype(BF)
    far_one = far(other_one)
    ins["dh1",] = after(ins["dh1",], other_one)
    row = run(r, (), ("inputs",), ins)
    got = near(row["dx_send",])
    owns.append(row["dx_own",])
    near_got.append(got)
    value_one = mine_one + far_one.astype(F32)
    total_one = None
    for k, total_one in enumerate(over_dp(value_one, bits, bits)):
        if k == 0:
            other = (row["dx_keep",] + after(got[1], total_one[0]).astype(F32)).astype(BF)
            far_got.append(far(other))
    total_two = step_two
    for total_two in steps_two:
        pass
    grad_inputs = add_inputs(owns, near_got, far_got)
    grad_out, grad_in, grad_b_in, grad_back, values, *sums = call(
        finish_two_kernel,
        "finish_two",
        total_two,
        [
            ((width, model), F32),
            ((model, units), F32),
            ((1, units), F32),
            ((units, model), F32),
        ]
        + [((1, model), F32)] * 7,
    )
    grad_qkv, grad_bias = call(
        finish_one_kernel,
        "finish_one",
        (after(total_one[0], grad_inputs), total_one[1], values),
        [((3, width, model), F32), ((2, width), F32)],
    )
    sums = [s.reshape(model) for s in sums]
    return (
        result,
        grad_inputs,
        grad_qkv.transpose(0, 2, 1),
        grad_bias,
        grad_out,
        sums[0],
        sums[1],
        sums[2],
        grad_in,
        grad_b_in.reshape(units),
        grad_back,
        sums[3],
        sums[4],
        sums[5],
    )


def solution(mesh):
    in_specs = (
        P("dp", "mp", None),
        P("dp", "mp"),
        P(None, None, "mp"),
        P(None, "mp"),
        P("mp", None),
        P(),
        P(),
        P(),
        P(None, "mp"),
        P("mp"),
        P("mp", None),
        P(),
        P(),
        P(),
        P("dp", "mp", None),
    )
    out_specs = (
        P("dp", "mp", None),
        P("dp", "mp", None),
        P(None, None, "mp"),
        P(None, "mp"),
        P("mp", None),
        P(),
        P(),
        P(),
        P(None, "mp"),
        P("mp"),
        P("mp", None),
        P(),
        P(),
        P(),
    )
    sizes = (mesh.shape["dp"], mesh.shape["mp"])
    return jax.shard_map(
        functools.partial(layer, sizes),
        mesh=mesh,
        in_specs=in_specs,
        out_specs=out_specs,
        check_vma=False,
    )
```

```python
import functools

import jax
import jax.numpy as jnp
from jax import lax
from jax.experimental import pallas as pl
from jax.experimental.pallas import tpu as pltpu
from jax.sharding import PartitionSpec as P

HEADS = 4
EPS = 1e-06
FAR = -(2.0**99)
GELU_C = 0.7978845608028654
GELU_A = 0.044715
LOG2_E = 1.4426950408889634
LN_2 = 0.6931471805599453

BF = jnp.bfloat16
F32 = jnp.float32

NN = (((1,), (0,)), ((), ()))
NT = (((1,), (1,)), ((), ()))
TN = (((0,), (0,)), ((), ()))

MB = 2**20
LIMITS = (10, 12, 8, 8)


def mm(left, right, dims):
    return lax.dot_general(left, right, dims, preferred_element_type=F32)


def call(kernel, name, args, outs, scratch=(), flops=0, limit=20):
    whole = pl.BlockSpec(memory_space=pltpu.VMEM)
    return pl.pallas_call(
        kernel,
        out_shape=[jax.ShapeDtypeStruct(shape, kind) for shape, kind in outs],
        in_specs=[whole] * len(args),
        out_specs=[whole] * len(outs),
        scratch_shapes=[pltpu.VMEM(shape, kind) for shape, kind in scratch],
        compiler_params=pltpu.CompilerParams(vmem_limit_bytes=limit * MB),
        cost_estimate=pl.CostEstimate(flops=flops // 20, bytes_accessed=0, transcendentals=0),
        name=name,
    )(*args)


def pack_kernel(rows, *refs):
    w_qkv, b_qv, w_out, b_out, w_in, b_in, w_back, b_back, segs, x, first = refs[:11]
    later, two, biases = refs[11:-2], refs[-2], refs[-1]
    biases[...] = jnp.zeros(biases.shape, F32)
    biases[0:1, :] = b_out[...].astype(F32).reshape(1, -1)
    biases[1:2, :] = b_back[...].astype(F32).reshape(1, -1)
    width, model = w_qkv.shape[1:]
    units = w_in.shape[1]
    half = model // 2
    here = x.shape[1]
    for r in range(rows):
        out = later[0] if r else first
        at = (r - 1) * (here + 16) if r else 0
        out[at : at + here, :] = x[r]
        at += here
        out[at : at + 16, :] = jnp.zeros((16, model), BF)
        seg = segs[r : r + 1, :]
        for digit in (jnp.bitwise_and(seg, 31), jnp.right_shift(seg, 5)):
            digit = digit.astype(F32).astype(BF)
            for start in range(0, here, model):
                out[at : at + 1, :] = digit[:, start : start + model]
                at += 1
    at = here + 16
    for c in range(3):
        first[at : at + width, :] = w_qkv[c]
        at += width
    first[at : at + 16, :] = jnp.zeros((16, model), BF)
    first[at : at + 1, 0:width] = b_qv[0:1, :]
    first[at : at + 1, width : 2 * width] = b_qv[1:2, :]
    two[0:width, :] = w_out[...]
    at = width
    two[at : at + half, 0:units] = w_in[0:half, :]
    two[at : at + half, units : 2 * units] = w_in[half:, :]
    at += half
    two[at : at + units, :] = w_back[...]
    at += units
    two[at : at + 16, :] = jnp.zeros((16, model), BF)
    two[at : at + 1, 0:units] = b_in[...]


def pack(w_qkv, b_qv, w_out, b_out, w_in, b_in, w_back, b_back, segments, inputs):
    width, units, model = w_qkv.shape[2], w_in.shape[1], w_in.shape[0]
    rows, here = segments.shape
    sizes = [here + 16 + 3 * width + 16]
    if rows > 1:
        sizes.append((rows - 1) * (here + 16))
    sizes.append(width + model // 2 + units + 16)
    args = (
        w_qkv.transpose(0, 2, 1),
        b_qv,
        w_out,
        b_out,
        w_in,
        b_in.reshape(1, units),
        w_back,
        b_back,
        segments,
        inputs,
    )
    return call(
        functools.partial(pack_kernel, rows),
        "pack",
        [pltpu.with_memory_space_constraint(a, pltpu.HBM) for a in args],
        [((size, model), BF) for size in sizes] + [((8, model), F32)],
    )


def load_weights(ws, here, hd, w_q, w_kv, bias):
    at = here + 16
    for i, w in enumerate(ws):
        w_q[i * hd : (i + 1) * hd, :] = w[at : at + hd, :]
        w_kv[i * 2 * hd : (i + 1) * 2 * hd, :] = w[at + hd : at + 3 * hd, :]
        line = w[at + 3 * hd : at + 3 * hd + 1, 0 : 2 * hd].astype(F32)
        bias[i] = jnp.broadcast_to(line, (2 * hd, 2 * hd)).T


def same_cell(x, at, here, hd):
    per = here // x.shape[1]
    low = [x[at + i : at + i + 1, :].astype(F32) for i in range(per)]
    high = [x[at + per + i : at + per + i + 1, :].astype(F32) for i in range(per)]
    low, high = jnp.concatenate(low, axis=1), jnp.concatenate(high, axis=1)
    lane = lax.broadcasted_iota(jnp.int32, (hd, here), 0).astype(F32)
    return lane == jnp.where(lane < 32, low, high + 32.0)


def value_ones(hd, length, count):
    return (lax.broadcasted_iota(jnp.int32, (hd, length), 0) < count).astype(F32).astype(BF)


def attend(queries, kvs, feats, before, put):
    hd = kvs[0].shape[0] // 2
    length = kvs[0].shape[1]
    ones = value_ones(hd, length, hd)

    def score(i):
        scores = mm(queries[i], jnp.concatenate([kvs[i][:hd], feats[i]], axis=0), NN)
        top = jnp.max(scores, axis=-1, keepdims=True)
        top = jnp.broadcast_to(top, (scores.shape[0], 2 * hd))
        if before is None:
            return scores, top, None
        steps = jnp.maximum(jnp.ceil((top - before[i]) * LOG2_E), 0.0)
        return scores, before[i] + steps * LN_2, jnp.exp2(-steps)

    later = score(0)
    for i in range(len(queries)):
        scores, top, weight = later
        if i + 1 < len(queries):
            later = score(i + 1)
        wide = jnp.concatenate([top] * (length // (2 * hd)), axis=1)
        expo = jnp.exp(scores - wide).astype(BF)
        out = mm(expo, jnp.concatenate([kvs[i][hd:], ones], axis=0), NT)
        put(i, expo, out, top, weight)


def project(x, w, bias, put):
    hd = bias.shape[1] // 2
    proj = mm(w, x, NT)
    for i in range(w.shape[0] // (2 * hd)):
        at = 2 * i * hd
        keys = proj[at : at + hd].astype(BF)
        values = (proj[at + hd : at + 2 * hd] + bias[i, hd:, 0:1]).astype(BF)
        put(i, keys, values)


def local_kernel(rows, here, hd, *refs):
    count = 2 if rows > 1 else 1
    mine, nears = refs[:count], refs[count : 2 * count]
    ws = refs[2 * count : 2 * count + 2]
    e_out, kv_out, qt_out, qa_out, o_out = refs[2 * count + 2 : 2 * count + 7]
    w_q, w_kv, bias, feats = refs[2 * count + 7 :]
    load_weights(ws, here, hd, w_q, w_kv, bias)
    for r in range(rows):
        at = (r - 1) * (here + 16) if r else 0
        pair = (mine[min(r, 1)], nears[min(r, 1)])
        for b, x in enumerate(pair):
            same = same_cell(x, at + here, here, hd)
            feats[r, :, b * here : (b + 1) * here] = jnp.where(same, 0.0, FAR).astype(BF)
            if b == 0:
                first = same.astype(F32)

        def put(i, keys, values, r=r):
            kv_out[r, i, :hd, :] = keys
            kv_out[r, i, hd:, :] = values

        block = jnp.concatenate([x[at : at + here, :] for x in pair], axis=0)
        project(block, w_kv[...], bias, put)
        proj = mm(w_q[...], pair[0][at : at + here, :], NT)
        for i in range(2):
            qt = proj[i * hd : (i + 1) * hd] + bias[i, :hd, 0:1]
            qt = qt.astype(BF).astype(F32) * (hd**-0.5)
            qt_out[r, i] = qt.astype(BF)
            qa_out[r, i] = jnp.concatenate([qt, first], axis=0).T.astype(BF)

    lane = lax.broadcasted_iota(jnp.int32, (here, 2 * hd), 1)

    def put(k, expo, out, top, _):
        e_out[k // 2, k % 2] = expo
        o_out[k // 2, k % 2] = jnp.where(lane < 3 * hd // 2, out, top)

    queries = [qa_out[r, i] for r in range(rows) for i in range(2)]
    kvs = [kv_out[r, i] for r in range(rows) for i in range(2)]
    attend(queries, kvs, [feats[r] for r in range(rows) for i in range(2)], None, put)


def attend_local(mine, nears, ws, rows, here, hd):
    model = mine[0].shape[1]
    return call(
        functools.partial(local_kernel, rows, here, hd),
        "attend_local",
        (*mine, *nears, *ws),
        [
            ((rows, 2, here, 2 * here), BF),
            ((rows, 2, 2 * hd, 2 * here), BF),
            ((rows, 2, hd, here), BF),
            ((rows, 2, here, 2 * hd), BF),
            ((rows, 2, here, 2 * hd), F32),
        ],
        [
            ((2 * hd, model), BF),
            ((4 * hd, model), BF),
            ((2, 2 * hd, 2 * hd), F32),
            ((rows, hd, 2 * here), BF),
        ],
        flops=1,
        limit=LIMITS[0],
    )


def remote_kernel(rows, here, hd, *refs):
    qs, os, xs, ws = refs[:2], refs[2:4], refs[4:6], refs[6:10]
    e_out, kv_out, o_out, weight_out, w_q, w_kv, bias, feats = refs[10:]
    heads = len(ws)
    load_weights(ws, here, hd, w_q, w_kv, bias)
    for n, row in enumerate(rows):
        at = (row - 1) * (here + 16) if row else 0
        for b, x in enumerate(xs):
            same = same_cell(x, at + here, here, hd)
            feats[n, :, b * here : (b + 1) * here] = jnp.where(same, 0.0, FAR).astype(BF)

        def put(i, keys, values, n=n):
            kv_out[n, i, :hd, :] = keys
            kv_out[n, i, hd:, :] = values

        block = jnp.concatenate([x[at : at + here, :] for x in xs], axis=0)
        project(block, w_kv[...], bias, put)

    def one_row(n, _):
        r = rows[0] + n

        def put(h, expo, out, _, weight):
            e_out[n, h] = expo
            o_out[n, h] = out + os[h // 2][r, h % 2] * weight
            weight_out[n, h] = weight.astype(BF)

        queries = [qs[h // 2][r, h % 2] for h in range(heads)]
        at = 3 * hd // 2
        before = [
            jnp.broadcast_to(os[h // 2][r, h % 2, :, at : at + 1], (here, 2 * hd))
            for h in range(heads)
        ]
        attend(queries, [kv_out[n, h] for h in range(heads)], [feats[n]] * heads, before, put)
        return 0

    lax.fori_loop(0, len(rows), one_row, 0)


def attend_remote(rows, queries, outs, xs, ws, here, hd):
    model = xs[0].shape[1]
    heads = len(ws)
    count = len(rows)
    return call(
        functools.partial(remote_kernel, rows, here, hd),
        "attend_remote",
        (*queries, *outs, *xs, *ws),
        [
            ((count, heads, here, 2 * here), BF),
            ((count, heads, 2 * hd, 2 * here), BF),
            ((count, heads, here, 2 * hd), F32),
            ((count, heads, here, 2 * hd), BF),
        ],
        [
            ((heads * hd, model), BF),
            ((heads * 2 * hd, model), BF),
            ((heads, 2 * hd, 2 * hd), F32),
            ((count, hd, 2 * here), BF),
        ],
        flops=1,
        limit=LIMITS[0],
    )


def middle_kernel(parts, heads, rows, *refs):
    groups = min(rows, 2)
    os, xs = refs[:groups], refs[groups : 2 * groups]
    at = 2 * groups
    cot_in = refs[at]
    ws = refs[at + 1 : at + 1 + parts]
    at += 1 + parts
    g_one, e_one, g_two, e_two, biases = refs[at : at + 5]
    result_out, keep_out, send_out, dh1_out, do_out = refs[at + 5 : at + 10]
    w_out, w_pad, w_in, w_back = refs[at + 10 : at + 14]
    dw_out, dw_in, dw_back, db_in, db_values, sums = refs[at + 14 :]
    w_pad[...] = jnp.zeros(w_pad.shape, BF)
    here, model = cot_in.shape[1:]
    hd = model // heads
    per = w_out.shape[0] // parts
    units = w_back.shape[0] // parts
    half_model = model // 2
    bias = []
    for b in range(parts):
        at = 0
        w_out[b * per : (b + 1) * per, :] = ws[b][at : at + per, :]
        w_pad[b * 2 * per : b * 2 * per + per, :] = ws[b][at : at + per, :]
        at += per
        cols = slice(b * units, (b + 1) * units)
        w_in[0:half_model, cols] = ws[b][at : at + half_model, 0:units]
        w_in[half_model:, cols] = ws[b][at : at + half_model, units : 2 * units]
        at += half_model
        w_back[b * units : (b + 1) * units, :] = ws[b][at : at + units, :]
        at += units
        bias.append(ws[b][at : at + 1, 0:units].astype(F32))
    b_in = jnp.concatenate(bias, axis=1)
    lane = lax.broadcasted_iota(jnp.int32, (here, 2 * hd), 1)

    def o_of(r, h):
        if groups == 1:
            return os[0][r, h]
        return jnp.where(r == 0, os[0][0, h], os[1][jnp.maximum(r - 1, 0), h])

    def x_of(r):
        first = xs[0][0:here, :].astype(F32)
        if groups == 1:
            return first
        at = pl.multiple_of(jnp.maximum(r - 1, 0) * (here + 16), 16)
        return jnp.where(r == 0, first, xs[1][pl.ds(at, here), :].astype(F32))

    for total in (dw_out, dw_in, dw_back, db_in, db_values, sums):
        total[...] = jnp.zeros(total.shape, F32)

    def norm(h):
        centre = h - jnp.mean(h, axis=-1, keepdims=True)
        rstd = lax.rsqrt(jnp.mean(centre * centre, axis=-1, keepdims=True) + EPS)
        return centre * rstd, rstd

    def norm_back(dy, gain, unit, rstd):
        dn = dy * gain
        mean = jnp.mean(dn, axis=-1, keepdims=True)
        along = jnp.mean(dn * unit, axis=-1, keepdims=True)
        return rstd * (dn - mean - unit * along)

    def down(v):
        return jnp.sum(v, axis=0, keepdims=True)

    def one_row(r, _):
        o_in = [o_of(r, h) for h in range(heads)]
        inv = [1.0 / o[:, hd : hd + 1] for o in o_in]
        normal = [o * i for o, i in zip(o_in, inv)]
        tiles = [
            jnp.where(lane < hd, normal[h], pltpu.roll(normal[h + 1], hd, 1))
            for h in range(0, heads, 2)
        ]
        att = jnp.concatenate(tiles, axis=1).astype(BF)
        h1 = x_of(r) + mm(att, w_out[...], NN) + biases[0:1, :]
        n1, rstd1 = norm(h1)
        y1 = n1 * g_one[...] + e_one[...]
        y1b = y1.astype(BF)
        pre = mm(y1b, w_in[...], NN) + b_in
        square = pre * pre
        half = 0.5 + 0.5 * jnp.tanh(pre * (GELU_C + GELU_C * GELU_A * square))
        full = pre * half
        act = full.astype(BF)
        slope = half + full * (1.0 - half) * (2.0 * GELU_C + 6.0 * GELU_C * GELU_A * square)
        h2 = y1 + mm(act, w_back[...], NN) + biases[1:2, :]
        n2, rstd2 = norm(h2)
        result_out[r] = (n2 * g_two[...] + e_two[...]).astype(BF)
        cot = cot_in[r].astype(F32)
        dh2 = norm_back(cot, g_two[...], n2, rstd2)
        dz = dh2.astype(BF)
        dact = mm(dz, w_back[...], NT)
        dpre = (dact * slope).astype(BF)
        dw_back[...] += mm(act, dz, TN)
        dw_in[...] += mm(y1b, dpre, TN)
        db_in[...] += down(dpre.astype(F32))
        dy1 = mm(dpre, w_in[...], NT) + dh2
        dh1 = norm_back(dy1, g_one[...], n1, rstd1)
        dh1_out[r] = dh1
        da = dh1.astype(BF)
        dw_out[...] += mm(att, da, TN)
        dwide = mm(da, w_pad[...], NT)
        for h in range(heads):
            grad = (dwide[:, 2 * hd * h : 2 * hd * (h + 1)] * inv[h]).astype(BF)
            wide = grad.astype(F32)
            inner = jnp.sum(wide * normal[h], axis=-1, keepdims=True)
            high = inner.astype(BF).astype(F32)
            rest = inner - high
            wide = jnp.where(lane == hd, -high, jnp.where(lane == hd + 1, -rest, wide))
            do_out[r, h] = wide.astype(BF)
        db_values[...] += down(dwide)
        rows_of = [down(dh1), down(dy1 * n1), down(dy1), down(dh2), down(cot * n2), down(cot)]
        for i, row in enumerate(rows_of):
            sums[i : i + 1, :] += row
        return 0

    lax.fori_loop(0, rows, one_row, 0)
    for b in range(parts):
        out = send_out if b % 2 else keep_out
        kind = out.dtype
        c = b // 2
        cols = slice(b * units, (b + 1) * units)
        at = 0
        out[c, at : at + per, :] = dw_out[b * per : (b + 1) * per, :].astype(kind)
        at += per
        out[c, at : at + half_model, 0:units] = dw_in[0:half_model, cols].astype(kind)
        out[c, at : at + half_model, units : 2 * units] = dw_in[half_model:, cols].astype(kind)
        at += half_model
        out[c, at : at + units, :] = dw_back[b * units : (b + 1) * units, :].astype(kind)
        at += units
        out[c, at:, :] = jnp.zeros((16, model), kind)
        out[c, at : at + 1, 0:units] = db_in[:, cols].astype(kind)
        out[c, at + 1 : at + 7, :] = sums[0:6, :].astype(BF).astype(kind)
        line = db_values[:, 2 * per * b : 2 * per * b + per]
        out[c, at + 7 : at + 8, 0:per] = line.astype(kind)


def middle(os, xs, cotangent, ws, vectors, heads):
    parts = len(ws)
    rows, here, model = cotangent.shape
    hd = model // heads
    width = model // parts
    size = ws[0].shape[0]
    units = size - 16 - width - model // 2
    return call(
        functools.partial(middle_kernel, parts, heads, rows),
        "middle",
        (*os, *xs, cotangent, *ws, *vectors),
        [
            (cotangent.shape, BF),
            ((parts // 2, size, model), F32),
            ((parts // 2, size, model), BF),
            ((rows, here, model), F32),
            ((rows, heads, here, 2 * hd), BF),
        ],
        [
            ((parts * width, model), BF),
            ((2 * parts * width, model), BF),
            ((model, parts * units), BF),
            ((parts * units, model), BF),
            ((parts * width, model), F32),
            ((model, parts * units), F32),
            ((parts * units, model), F32),
            ((1, parts * units), F32),
            ((1, 2 * model), F32),
            ((8, model), F32),
        ],
        flops=rows * 6 * here * model * (2 * model + 2 * parts * units),
        limit=LIMITS[1],
    )


def heads_step(row, n, pairs, ref):
    er_in, kvr_in, do_in, weight_in, ds = (ref[k] for k in ("er", "kvr", "do", "weight", "ds"))
    hd = kvr_in.shape[2] // 2
    half = kvr_in.shape[3]
    ones = value_ones(hd, half, 2)

    def one_head(step, _):
        h = 2 * pairs[0] + step
        i = step % 2

        def pick(name):
            found = [ref[name, pair][row, i] for pair in pairs]
            return found[0] if len(pairs) == 1 else jnp.where(step < 2, *found)

        kvs, es, do = (pick("kvl"), kvr_in[n, h]), (pick("el"), er_in[n, h]), do_in[row, h]
        dos = (do * weight_in[n, h], do)
        for side in range(2):
            cols = slice(side * half, (side + 1) * half)
            values = jnp.concatenate([kvs[side][hd:], ones], axis=0)
            dp = mm(dos[side], values, NN)
            ds[:, cols] = (dp * es[side].astype(F32)).astype(BF)
            ref["dkv", pairs[0]][step, hd:, cols] = mm(dos[side], es[side], TN)[:hd].astype(BF)
        ref["dkv", pairs[0]][step, :hd, :] = mm(pick("qt"), ds[...], NN).astype(BF)
        keys = jnp.concatenate([kv[:hd] for kv in kvs], axis=1)
        ref["dq", pairs[0]][step] = (mm(keys, ds[...], NT) * (hd**-0.5)).astype(BF)
        return 0

    lax.fori_loop(0, 2 * len(pairs), one_head, 0)


def joined(refs, cols):
    return jnp.concatenate([ref[h, :, cols] for ref in refs for h in range(ref.shape[0])], axis=0)


def inputs_step(row, parts, ref):
    dkvs, dqs = [[ref[k] for k in ref if k[0] == name] for name in ("dkv", "dq")]
    w_q, w_kv = ref["w_q"], ref["w_kv"]
    hd = w_q.shape[0] // parts
    here = dqs[0].shape[2]
    at = here + 16
    for b in range(parts):
        w = ref["w", b]
        w_q[b * hd : (b + 1) * hd, :] = w[at : at + hd, :]
        w_kv[b * 2 * hd : (b + 1) * 2 * hd, :] = w[at + hd : at + 3 * hd, :]
    for b in range(parts):
        dx = mm(joined(dkvs, slice(b * here, (b + 1) * here)), w_kv[...], TN)
        if b == 0:
            own = mm(joined(dqs, slice(0, here)), w_q[...], TN)
            ref["dx_own"][...] = dx + own + ref["dh1"][row]
        elif b % 2:
            if ("dx_send",) in ref:
                ref["dx_send"][b // 2] = dx.astype(BF)
            else:
                ref["dx_same" if b == 1 else "dx_cross"][...] = dx.astype(BF)
        else:
            ref["dx_keep"][...] = dx


def weights_step(row, heads, parts, ref):
    all_dkv, all_dq = [
        [ref[k].at[h] for k in sorted(k for k in ref if k[0] == name) for h in range(ref[k].shape[0])]
        for name in ("dkv", "dq")
    ]
    dkvs = [all_dkv[h] for h in heads]
    dq = jnp.concatenate([all_dq[h][...] for h in heads], axis=0)
    here = dq.shape[1]
    model = ref["x", 0].shape[1]
    hd = model // parts
    at = (row - 1) * (here + 16) if row else 0
    gkv = None
    for b in range(parts):
        left = jnp.concatenate([d[:, b * here : (b + 1) * here] for d in dkvs], axis=0)
        term = mm(left, ref["x", b][at : at + here, :], NN)
        gkv = term if gkv is None else gkv + term
    gq = mm(dq, ref["x", 0][at : at + here, :], NN)
    bq = mm(jnp.ones((8, here), BF), dq, NT)[0:1]
    out = ref["grads",]
    for c, h in enumerate(heads):
        pieces = [
            (slice(0, hd), slice(0, model), gq[c * hd : (c + 1) * hd]),
            (slice(hd, 3 * hd), slice(0, model), gkv[c * 2 * hd : (c + 1) * 2 * hd]),
            (slice(3 * hd, 3 * hd + 1), slice(0, hd), bq[:, c * hd : (c + 1) * hd]),
        ]
        out[c, 3 * hd :, :] = jnp.zeros((16, model), out.dtype)
        for rows, cols, value in pieces:
            if ("grads_in",) in ref:
                value = value + ref["grads_in",][h, rows, cols]
            out[c, rows, cols] = value.astype(out.dtype)


def backward_kernel(names, row, n, pairs, parts, want, some, *refs):
    ref = {name if len(name) > 1 else name[0]: r for name, r in zip(names, refs)}
    ref.update({name: r for name, r in zip(names, refs) if len(name) == 1})
    if pairs:
        heads_step(row, n, pairs, ref)
    if "weights" in want:
        weights_step(row, some, parts, ref)
    if "inputs" in want:
        inputs_step(row, parts, ref)


def backward(row, n, pairs, want, ins, some=(0, 1, 2, 3), kind=F32, joint=False):
    parts = 4
    el = ins["el", 0]
    here, half = el.shape[2:]
    length = 2 * half
    hd = ins["kvl", 0].shape[2] // 2
    model = ins["x", 0].shape[1]
    size = 3 * hd + 16
    use = set()
    outs, scratch = {}, {}
    for pair in pairs:
        use |= {("el", pair), ("kvl", pair), ("qt", pair), ("er",), ("kvr",), ("do",), ("weight",)}
        scratch["ds",] = ((here, length), BF)
    if pairs:
        outs["dkv", pairs[0]] = ((2 * len(pairs), 2 * hd, length), BF)
        outs["dq", pairs[0]] = ((2 * len(pairs), hd, here), BF)
    if want:
        use |= {k for k in ins if k[0] in ("dkv", "dq")}
    if "inputs" in want:
        use |= {("w", b) for b in range(parts)} | {("dh1",)}
        outs["dx_own",] = ((here, model), F32)
        outs["dx_keep",] = ((here, model), F32)
        if joint:
            outs["dx_send",] = ((parts // 2, here, model), BF)
        else:
            outs["dx_same",] = ((here, model), BF)
            outs["dx_cross",] = ((here, model), BF)
        scratch["w_kv",] = ((2 * model, model), BF)
        scratch["w_q",] = ((model, model), BF)
    if "weights" in want:
        use |= {("x", b) for b in range(parts)}
        if ("grads_in",) in ins:
            use.add(("grads_in",))
        outs["grads",] = ((len(some), size, model), kind)
    order = sorted(use, key=str)
    names = tuple(order) + tuple(outs) + tuple(scratch)
    done = call(
        functools.partial(backward_kernel, names, row, n, pairs, parts, want, some),
        "backward",
        [ins[name] for name in order],
        list(outs.values()),
        list(scratch.values()),
        limit=LIMITS[2],
    )
    return dict(zip(outs, done))


def add_kernel(rows, *refs):
    owns, nears, fars, out = refs[:rows], refs[rows : 2 * rows], refs[2 * rows : -1], refs[-1]
    for r in range(rows):
        out[r] = owns[r][...] + nears[r][...].astype(F32) + fars[r][...].astype(F32)


def add_inputs(owns, nears, fars):
    rows = len(owns)
    (out,) = call(
        functools.partial(add_kernel, rows),
        "add_inputs",
        (*owns, *nears, *fars),
        [((rows,) + owns[0].shape, F32)],
        limit=LIMITS[3],
    )
    return out


def finish_one_kernel(a, b, values, qkv, bias):
    width = qkv.shape[1]
    total = a[...].astype(F32) + b[...].astype(F32)
    for c in range(3):
        qkv[c] = total[c * width : (c + 1) * width]
    bias[0:1, :] = total[3 * width : 3 * width + 1, 0:width]
    bias[1:2, :] = values[:, 0:width]


def finish_two_kernel(a, b, w_out, w_in, b_in, w_back, values, *sums):
    width, model = w_out.shape
    units = w_back.shape[0]
    half = model // 2
    total = a[...].astype(F32) + b[...].astype(F32)
    w_out[...] = total[:width]
    at = width
    w_in[0:half, :] = total[at : at + half, 0:units]
    w_in[half:, :] = total[at : at + half, units : 2 * units]
    at += half
    w_back[...] = total[at : at + units]
    at += units
    b_in[...] = total[at : at + 1, 0:units]
    values[...] = total[at + 7 : at + 8]
    for i, out in enumerate(sums):
        out[...] = total[at + 1 + i : at + 2 + i]


def swap(value, axis, size, bit):
    return lax.ppermute(value, axis, [(i, i ^ bit) for i in range(size)])


def after(value, *others):
    return lax.optimization_barrier((value, *others))[0]


def layer(mesh_sizes, *args):
    (inputs, segments, w_qkv, b_qv, w_out, b_out, gain_one, shift_one) = args[:8]
    (w_in, b_in, w_back, b_back, gain_two, shift_two, cotangent) = args[8:]
    dp, mp = mesh_sizes
    rows, here, model = inputs.shape
    heads = HEADS
    width = w_qkv.shape[2]
    units = w_in.shape[1]

    def near(value):
        return swap(value, "mp", mp, 1)

    def far(value):
        return swap(value, "mp", mp, 2)

    first, *later, two, biases = pack(
        w_qkv, b_qv, w_out, b_out, w_in, b_in, w_back, b_back, segments, inputs
    )
    vectors = [v.reshape(1, model) for v in (gain_one, shift_one, gain_two, shift_two)]
    vectors.append(biases)
    hd = model // heads
    first_far = far(first)
    first_near = near(first)
    mine, nears, fars = [first], [first_near], [first_far]
    if rows > 1:
        nears.append(near(later[0]))
        fars.append(far(after(later[0], first_near)))
        mine.append(later[0])
    two_far = far(after(two, nears[-1]))
    two_near = near(after(two, nears[-1]))
    locals_of = [attend_local(mine, nears, (first, first_near), rows, here, hd)]
    first_both = near(after(first_far, locals_of[0][2]))
    boths = [first_both]
    ws = (first, first_near, first_far, first_both)
    locals_of.append(attend_local(mine, nears, ws[2:], rows, here, hd))
    queries, outs = zip(*[out[3:5] for out in locals_of])
    remotes = []
    for c, rows_of in enumerate([[0], list(range(1, rows))][: min(rows, 2)]):
        if c == 1:
            boths.append(near(after(fars[1], remotes[0][2])))
        xs = [fars[c], boths[c]]
        remotes.append(attend_remote(rows_of, queries, outs, xs, ws, here, hd))
    blocks = [[group[min(r, 1)] for group in (mine, nears, fars, boths)] for r in range(rows)]
    two_both = near(after(two_far, remotes[-1][2]))
    result, keep_two, send_two, dh1s, dos = middle(
        [out[2] for out in remotes],
        mine,
        cotangent,
        [two, two_near, two_far, two_both],
        vectors,
        heads,
    )

    def over_dp(value, even, odd):
        for bits in zip(even, odd):
            pairs = []
            for d in range(dp):
                for m in range(mp):
                    pairs.append((d * mp + m, (d ^ bits[m % 2]) * mp + m))
            sent = value.astype(BF)
            got = lax.ppermute(sent, ("dp", "mp"), pairs)
            yield sent, got
            value = sent.astype(F32) + got.astype(F32)

    bits = [1 << k for k in range(dp.bit_length() - 1)]


    def inputs_of(r, **more):
        er, kvr, _, weight = remotes[min(r, 1)]
        ins = {("er",): er, ("kvr",): kvr, ("weight",): weight, ("do",): dos, ("dh1",): dh1s}
        for pair in range(heads // 2):
            names = (("el", pair), ("kvl", pair), ("qt", pair))
            ins.update(zip(names, locals_of[pair][:3]))
        for b in range(mp):
            ins["w", b] = ws[b]
            ins["x", b] = blocks[r][b]
        return ins

    def hold(ins, *ready):
        name = next(n for n in (("er",), ("dh1",)) if n in ins)
        ins[name] = after(ins[name], *ready)
        return ins

    def run(r, pairs, want, ins, **more):
        return backward(r, max(r - 1, 0), pairs, want, ins, **more)

    got_two = near(send_two)
    other_two = steps_two = step_two = None
    grads = None
    owns, near_got, far_got = [], [], []
    ready = []
    both = tuple(range(heads // 2))
    for r in range(rows):
        last = r == rows - 1
        ins = inputs_of(r)
        if ready:
            hold(ins, *ready)
        if r == 0:
            ins.update(run(0, both[:1], (), ins))
            got_two = after(got_two, ins["dkv", 0])
            other_two = (keep_two[1] + got_two[1].astype(F32)).astype(BF)
            far_two = far(other_two)
            hold(ins, other_two)
            ins.update(run(0, both[1:], () if last else ("inputs",), ins))
        else:
            ins.update(run(r, both, (), ins))
            flag = ins["dkv", 0]
            if r > 1 or last:
                far_got[-1] = after(far_got[-1], flag)
        flag = ins["dkv", 1] if r == 0 else ins["dkv", 0]
        if steps_two is None:
            value_two = (keep_two[0] + got_two[0].astype(F32)).astype(BF).astype(F32)
            value_two = value_two + after(far_two, flag).astype(F32)
            steps_two = over_dp(value_two, bits[::-1], bits[::-1])
            step_two = next(steps_two)
            tie = (step_two[0],)
        else:
            tie = (step_two[1], *far_got)
        if grads is not None:
            ins["grads_in",] = grads
        if last:
            break
        if r:
            ins["dh1",] = after(ins["dh1",], *tie)
            ins.update(run(r, (), ("inputs",), ins))
        got = near(ins["dx_cross",] if r else after(ins["dx_cross",], *tie))
        owns.append(ins["dx_own",])
        ins["x", 0] = after(ins["x", 0], ins["dx_cross",])
        grads = run(r, (), ("weights",), ins)["grads",]
        got = after(got, grads)
        near_got.append(near(after(ins["dx_same",], got)))
        other = (ins["dx_keep",] + got.astype(F32)).astype(BF)
        far_got.append(far(other))
        ready = [other, step_two[0]]
    ins["x", 0] = after(ins["x", 0], *tie)
    send = run(r, (), ("weights",), ins, some=(1, 3), kind=BF)["grads",]
    got = near(send)
    ins["x", 0] = after(ins["x", 0], send)
    keep = run(r, (), ("weights",), ins, some=(0, 2))["grads",]
    mine_one = keep[0] + got[0].astype(F32)
    other_one = (keep[1] + got[1].astype(F32)).astype(BF)
    far_one = far(other_one)
    ins["dh1",] = after(ins["dh1",], other_one)
    row = run(r, (), ("inputs",), ins, joint=True)
    got = near(after(row["dx_send",], other_one))
    owns.append(row["dx_own",])
    near_got.append(got[0])
    value_one = mine_one + far_one.astype(F32)
    total_one = None
    for k, total_one in enumerate(over_dp(value_one, bits, bits)):
        if k == 0:
            other = (row["dx_keep",] + after(got[1], total_one[0]).astype(F32)).astype(BF)
            far_got.append(far(other))
    total_two = step_two
    for total_two in steps_two:
        pass
    grad_inputs = add_inputs(owns, near_got, far_got)
    grad_out, grad_in, grad_b_in, grad_back, values, *sums = call(
        finish_two_kernel,
        "finish_two",
        total_two,
        [
            ((width, model), F32),
            ((model, units), F32),
            ((1, units), F32),
            ((units, model), F32),
        ]
        + [((1, model), F32)] * 7,
    )
    grad_qkv, grad_bias = call(
        finish_one_kernel,
        "finish_one",
        (after(total_one[0], grad_inputs), total_one[1], values),
        [((3, width, model), F32), ((2, width), F32)],
    )
    sums = [s.reshape(model) for s in sums]
    return (
        result,
        grad_inputs,
        grad_qkv.transpose(0, 2, 1),
        grad_bias,
        grad_out,
        sums[0],
        sums[1],
        sums[2],
        grad_in,
        grad_b_in.reshape(units),
        grad_back,
        sums[3],
        sums[4],
        sums[5],
    )


def solution(mesh):
    in_specs = (
        P("dp", "mp", None),
        P("dp", "mp"),
        P(None, None, "mp"),
        P(None, "mp"),
        P("mp", None),
        P(),
        P(),
        P(),
        P(None, "mp"),
        P("mp"),
        P("mp", None),
        P(),
        P(),
        P(),
        P("dp", "mp", None),
    )
    out_specs = (
        P("dp", "mp", None),
        P("dp", "mp", None),
        P(None, None, "mp"),
        P(None, "mp"),
        P("mp", None),
        P(),
        P(),
        P(),
        P(None, "mp"),
        P("mp"),
        P("mp", None),
        P(),
        P(),
        P(),
    )
    sizes = (mesh.shape["dp"], mesh.shape["mp"])
    return jax.shard_map(
        functools.partial(layer, sizes),
        mesh=mesh,
        in_specs=in_specs,
        out_specs=out_specs,
        check_vma=False,
    )
```

```python
import functools

import jax
import jax.numpy as jnp
from jax import lax
from jax.experimental import pallas as pl
from jax.experimental.pallas import tpu as pltpu
from jax.sharding import PartitionSpec as P

HEADS = 4
EPS = 1e-06
FAR = -(2.0**99)
GELU_C = 0.7978845608028654
GELU_A = 0.044715
LOG2_E = 1.4426950408889634
LN_2 = 0.6931471805599453

BF = jnp.bfloat16
F32 = jnp.float32

NN = (((1,), (0,)), ((), ()))
NT = (((1,), (1,)), ((), ()))
TN = (((0,), (0,)), ((), ()))

MB = 2**20
LIMITS = (10, 12, 8, 8)


def mm(left, right, dims):
    return lax.dot_general(left, right, dims, preferred_element_type=F32)


def call(kernel, name, args, outs, scratch=(), flops=0, limit=20):
    whole = pl.BlockSpec(memory_space=pltpu.VMEM)
    return pl.pallas_call(
        kernel,
        out_shape=[jax.ShapeDtypeStruct(shape, kind) for shape, kind in outs],
        in_specs=[whole] * len(args),
        out_specs=[whole] * len(outs),
        scratch_shapes=[pltpu.VMEM(shape, kind) for shape, kind in scratch],
        compiler_params=pltpu.CompilerParams(vmem_limit_bytes=limit * MB),
        cost_estimate=pl.CostEstimate(flops=flops // 20, bytes_accessed=0, transcendentals=0),
        name=name,
    )(*args)


def stacked(lines, width):
    place = lax.broadcasted_iota(jnp.int32, (16, width), 0)
    out = jnp.zeros((16, width), F32)
    for k, line in enumerate(lines):
        line = line.astype(F32)
        if line.shape[1] < width:
            fill = jnp.zeros((1, width - line.shape[1]), F32)
            line = jnp.concatenate([line, fill], axis=1)
        out = jnp.where(place == k, jnp.broadcast_to(line, (16, width)), out)
    return out


def pack_kernel(rows, *refs):
    w_qkv, b_qv, w_out, b_out, w_in, b_in, w_back, b_back, segs, x, first = refs[:11]
    later, two, biases = refs[11:-2], refs[-2], refs[-1]
    biases[...] = jnp.zeros(biases.shape, F32)
    biases[0:1, :] = b_out[...].astype(F32).reshape(1, -1)
    biases[1:2, :] = b_back[...].astype(F32).reshape(1, -1)
    width, model = w_qkv.shape[1:]
    units = w_in.shape[1]
    half = model // 2
    here = x.shape[1]
    for r in range(rows):
        out = later[0] if r else first
        at = (r - 1) * (here + 16) if r else 0
        out[at : at + here, :] = x[r]
        at += here
        seg = segs[r : r + 1, :]
        digits = [jnp.bitwise_and(seg, 31), jnp.right_shift(seg, 5)]
        lines = [d[:, k : k + model] for d in digits for k in range(0, here, model)]
        out[at : at + 16, :] = stacked(lines, model).astype(BF)
    at = here + 16
    for c in range(3):
        first[at : at + width, :] = w_qkv[c]
        at += width
    both = b_qv[...].astype(F32)
    line = jnp.concatenate([both[0:1], both[1:2]], axis=1)
    first[at : at + 16, :] = stacked([line], model).astype(BF)
    two[0:width, :] = w_out[...]
    at = width
    two[at : at + half, 0:units] = w_in[0:half, :]
    two[at : at + half, units : 2 * units] = w_in[half:, :]
    at += half
    two[at : at + units, :] = w_back[...]
    at += units
    two[at : at + 16, :] = stacked([b_in[...]], model).astype(BF)


def pack(w_qkv, b_qv, w_out, b_out, w_in, b_in, w_back, b_back, segments, inputs):
    width, units, model = w_qkv.shape[2], w_in.shape[1], w_in.shape[0]
    rows, here = segments.shape
    sizes = [here + 16 + 3 * width + 16]
    if rows > 1:
        sizes.append((rows - 1) * (here + 16))
    sizes.append(width + model // 2 + units + 16)
    args = (
        w_qkv.transpose(0, 2, 1),
        b_qv,
        w_out,
        b_out,
        w_in,
        b_in.reshape(1, units),
        w_back,
        b_back,
        segments,
        inputs,
    )
    return call(
        functools.partial(pack_kernel, rows),
        "pack",
        [pltpu.with_memory_space_constraint(a, pltpu.HBM) for a in args],
        [((size, model), BF) for size in sizes] + [((8, model), F32)],
    )


def load_weights(ws, here, hd, w_q, w_kv, bias):
    at = here + 16
    for i, w in enumerate(ws):
        w_q[i * hd : (i + 1) * hd, :] = w[at : at + hd, :]
        w_kv[i * 2 * hd : (i + 1) * 2 * hd, :] = w[at + hd : at + 3 * hd, :]
        line = w[at + 3 * hd : at + 3 * hd + 16, 0 : 2 * hd].astype(F32)[0:1]
        bias[i] = jnp.broadcast_to(line, (2 * hd, 2 * hd)).T


def same_cell(x, at, here, hd):
    per = here // x.shape[1]
    block = x[at : at + 16, :].astype(F32)
    low = [block[i : i + 1] for i in range(per)]
    high = [block[per + i : per + i + 1] for i in range(per)]
    low, high = jnp.concatenate(low, axis=1), jnp.concatenate(high, axis=1)
    lane = lax.broadcasted_iota(jnp.int32, (hd, here), 0).astype(F32)
    return lane == jnp.where(lane < 32, low, high + 32.0)


def value_ones(hd, length, count):
    return (lax.broadcasted_iota(jnp.int32, (hd, length), 0) < count).astype(F32).astype(BF)


def attend(queries, kvs, feats, before, put):
    hd = kvs[0].shape[0] // 2
    length = kvs[0].shape[1]
    ones = value_ones(hd, length, hd)

    def score(i):
        scores = mm(queries[i], jnp.concatenate([kvs[i][:hd], feats[i]], axis=0), NN)
        top = jnp.max(scores, axis=-1, keepdims=True)
        top = jnp.broadcast_to(top, (scores.shape[0], 2 * hd))
        if before is None:
            return scores, top, None
        steps = jnp.maximum(jnp.ceil((top - before[i]) * LOG2_E), 0.0)
        return scores, before[i] + steps * LN_2, jnp.exp2(-steps)

    later = score(0)
    for i in range(len(queries)):
        scores, top, weight = later
        if i + 1 < len(queries):
            later = score(i + 1)
        wide = jnp.concatenate([top] * (length // (2 * hd)), axis=1)
        expo = jnp.exp(scores - wide).astype(BF)
        out = mm(expo, jnp.concatenate([kvs[i][hd:], ones], axis=0), NT)
        put(i, expo, out, top, weight)


def project(x, w, bias, put):
    hd = bias.shape[1] // 2
    proj = mm(w, x, NT)
    for i in range(w.shape[0] // (2 * hd)):
        at = 2 * i * hd
        keys = proj[at : at + hd].astype(BF)
        values = (proj[at + hd : at + 2 * hd] + bias[i, hd:, 0:1]).astype(BF)
        put(i, keys, values)


def local_kernel(rows, here, hd, *refs):
    count = 2 if rows > 1 else 1
    mine, nears = refs[:count], refs[count : 2 * count]
    ws = refs[2 * count : 2 * count + 2]
    e_out, kv_out, qt_out, qa_out, o_out = refs[2 * count + 2 : 2 * count + 7]
    w_q, w_kv, bias, feats = refs[2 * count + 7 :]
    load_weights(ws, here, hd, w_q, w_kv, bias)
    for r in range(rows):
        at = (r - 1) * (here + 16) if r else 0
        pair = (mine[min(r, 1)], nears[min(r, 1)])
        for b, x in enumerate(pair):
            same = same_cell(x, at + here, here, hd)
            feats[r, :, b * here : (b + 1) * here] = jnp.where(same, 0.0, FAR).astype(BF)
            if b == 0:
                first = same.astype(F32)

        def put(i, keys, values, r=r):
            kv_out[r, i, :hd, :] = keys
            kv_out[r, i, hd:, :] = values

        block = jnp.concatenate([x[at : at + here, :] for x in pair], axis=0)
        project(block, w_kv[...], bias, put)
        proj = mm(w_q[...], pair[0][at : at + here, :], NT)
        for i in range(2):
            qt = proj[i * hd : (i + 1) * hd] + bias[i, :hd, 0:1]
            qt = qt.astype(BF).astype(F32) * (hd**-0.5)
            qt_out[r, i] = qt.astype(BF)
            qa_out[r, i] = jnp.concatenate([qt, first], axis=0).T.astype(BF)

    lane = lax.broadcasted_iota(jnp.int32, (here, 2 * hd), 1)

    def put(k, expo, out, top, _):
        e_out[k // 2, k % 2] = expo
        o_out[k // 2, k % 2] = jnp.where(lane < 3 * hd // 2, out, top)

    queries = [qa_out[r, i] for r in range(rows) for i in range(2)]
    kvs = [kv_out[r, i] for r in range(rows) for i in range(2)]
    attend(queries, kvs, [feats[r] for r in range(rows) for i in range(2)], None, put)


def attend_local(mine, nears, ws, rows, here, hd):
    model = mine[0].shape[1]
    return call(
        functools.partial(local_kernel, rows, here, hd),
        "attend_local",
        (*mine, *nears, *ws),
        [
            ((rows, 2, here, 2 * here), BF),
            ((rows, 2, 2 * hd, 2 * here), BF),
            ((rows, 2, hd, here), BF),
            ((rows, 2, here, 2 * hd), BF),
            ((rows, 2, here, 2 * hd), F32),
        ],
        [
            ((2 * hd, model), BF),
            ((4 * hd, model), BF),
            ((2, 2 * hd, 2 * hd), F32),
            ((rows, hd, 2 * here), BF),
        ],
        flops=1,
        limit=LIMITS[0],
    )


def remote_kernel(rows, here, hd, *refs):
    qs, os, xs, ws = refs[:2], refs[2:4], refs[4:6], refs[6:10]
    e_out, kv_out, o_out, weight_out, w_q, w_kv, bias, feats = refs[10:]
    heads = len(ws)
    load_weights(ws, here, hd, w_q, w_kv, bias)
    for n, row in enumerate(rows):
        at = (row - 1) * (here + 16) if row else 0
        for b, x in enumerate(xs):
            same = same_cell(x, at + here, here, hd)
            feats[n, :, b * here : (b + 1) * here] = jnp.where(same, 0.0, FAR).astype(BF)

        def put(i, keys, values, n=n):
            kv_out[n, i, :hd, :] = keys
            kv_out[n, i, hd:, :] = values

        block = jnp.concatenate([x[at : at + here, :] for x in xs], axis=0)
        project(block, w_kv[...], bias, put)

    def one_row(n, _):
        r = rows[0] + n

        def put(h, expo, out, _, weight):
            e_out[n, h] = expo
            o_out[n, h] = out + os[h // 2][r, h % 2] * weight
            weight_out[n, h] = weight.astype(BF)

        queries = [qs[h // 2][r, h % 2] for h in range(heads)]
        at = 3 * hd // 2
        before = [
            jnp.broadcast_to(os[h // 2][r, h % 2, :, at : at + 1], (here, 2 * hd))
            for h in range(heads)
        ]
        attend(queries, [kv_out[n, h] for h in range(heads)], [feats[n]] * heads, before, put)
        return 0

    lax.fori_loop(0, len(rows), one_row, 0)


def attend_remote(rows, queries, outs, xs, ws, here, hd):
    model = xs[0].shape[1]
    heads = len(ws)
    count = len(rows)
    return call(
        functools.partial(remote_kernel, rows, here, hd),
        "attend_remote",
        (*queries, *outs, *xs, *ws),
        [
            ((count, heads, here, 2 * here), BF),
            ((count, heads, 2 * hd, 2 * here), BF),
            ((count, heads, here, 2 * hd), F32),
            ((count, heads, here, 2 * hd), BF),
        ],
        [
            ((heads * hd, model), BF),
            ((heads * 2 * hd, model), BF),
            ((heads, 2 * hd, 2 * hd), F32),
            ((count, hd, 2 * here), BF),
        ],
        flops=1,
        limit=LIMITS[0],
    )


def middle_kernel(parts, heads, rows, *refs):
    groups = min(rows, 2)
    os, xs = refs[:groups], refs[groups : 2 * groups]
    at = 2 * groups
    cot_in = refs[at]
    ws = refs[at + 1 : at + 1 + parts]
    at += 1 + parts
    g_one, e_one, g_two, e_two, biases = refs[at : at + 5]
    result_out, keep_out, send_out, dh1_out, do_out = refs[at + 5 : at + 10]
    w_out, w_pad, w_in, w_back = refs[at + 10 : at + 14]
    dw_out, dw_in, dw_back, db_in, db_values, sums = refs[at + 14 :]
    w_pad[...] = jnp.zeros(w_pad.shape, BF)
    here, model = cot_in.shape[1:]
    hd = model // heads
    per = w_out.shape[0] // parts
    units = w_back.shape[0] // parts
    half_model = model // 2
    bias = []
    for b in range(parts):
        at = 0
        w_out[b * per : (b + 1) * per, :] = ws[b][at : at + per, :]
        w_pad[b * 2 * per : b * 2 * per + per, :] = ws[b][at : at + per, :]
        at += per
        cols = slice(b * units, (b + 1) * units)
        w_in[0:half_model, cols] = ws[b][at : at + half_model, 0:units]
        w_in[half_model:, cols] = ws[b][at : at + half_model, units : 2 * units]
        at += half_model
        w_back[b * units : (b + 1) * units, :] = ws[b][at : at + units, :]
        at += units
        bias.append(ws[b][at : at + 16, 0:units].astype(F32)[0:1])
    b_in = jnp.concatenate(bias, axis=1)
    lane = lax.broadcasted_iota(jnp.int32, (here, 2 * hd), 1)

    def o_of(r, h):
        if groups == 1:
            return os[0][r, h]
        return jnp.where(r == 0, os[0][0, h], os[1][jnp.maximum(r - 1, 0), h])

    def x_of(r):
        first = xs[0][0:here, :].astype(F32)
        if groups == 1:
            return first
        at = pl.multiple_of(jnp.maximum(r - 1, 0) * (here + 16), 16)
        return jnp.where(r == 0, first, xs[1][pl.ds(at, here), :].astype(F32))

    for total in (dw_out, dw_in, dw_back, db_in, db_values, sums):
        total[...] = jnp.zeros(total.shape, F32)

    def norm(h):
        centre = h - jnp.mean(h, axis=-1, keepdims=True)
        rstd = lax.rsqrt(jnp.mean(centre * centre, axis=-1, keepdims=True) + EPS)
        return centre * rstd, rstd

    def norm_back(dy, gain, unit, rstd):
        dn = dy * gain
        mean = jnp.mean(dn, axis=-1, keepdims=True)
        along = jnp.mean(dn * unit, axis=-1, keepdims=True)
        return rstd * (dn - mean - unit * along)

    def down(v):
        return jnp.sum(v, axis=0, keepdims=True)

    def one_row(r, _):
        o_in = [o_of(r, h) for h in range(heads)]
        inv = [1.0 / o[:, hd : hd + 1] for o in o_in]
        normal = [o * i for o, i in zip(o_in, inv)]
        tiles = [
            jnp.where(lane < hd, normal[h], pltpu.roll(normal[h + 1], hd, 1))
            for h in range(0, heads, 2)
        ]
        att = jnp.concatenate(tiles, axis=1).astype(BF)
        h1 = x_of(r) + mm(att, w_out[...], NN) + biases[0:1, :]
        n1, rstd1 = norm(h1)
        y1 = n1 * g_one[...] + e_one[...]
        y1b = y1.astype(BF)
        pre = mm(y1b, w_in[...], NN) + b_in
        square = pre * pre
        half = 0.5 + 0.5 * jnp.tanh(pre * (GELU_C + GELU_C * GELU_A * square))
        full = pre * half
        act = full.astype(BF)
        slope = half + full * (1.0 - half) * (2.0 * GELU_C + 6.0 * GELU_C * GELU_A * square)
        h2 = y1 + mm(act, w_back[...], NN) + biases[1:2, :]
        n2, rstd2 = norm(h2)
        result_out[r] = (n2 * g_two[...] + e_two[...]).astype(BF)
        cot = cot_in[r].astype(F32)
        dh2 = norm_back(cot, g_two[...], n2, rstd2)
        dz = dh2.astype(BF)
        dact = mm(dz, w_back[...], NT)
        dpre = (dact * slope).astype(BF)
        dw_back[...] += mm(act, dz, TN)
        dw_in[...] += mm(y1b, dpre, TN)
        db_in[...] += down(dpre.astype(F32))
        dy1 = mm(dpre, w_in[...], NT) + dh2
        dh1 = norm_back(dy1, g_one[...], n1, rstd1)
        dh1_out[r] = dh1
        da = dh1.astype(BF)
        dw_out[...] += mm(att, da, TN)
        dwide = mm(da, w_pad[...], NT)
        for h in range(heads):
            grad = (dwide[:, 2 * hd * h : 2 * hd * (h + 1)] * inv[h]).astype(BF)
            wide = grad.astype(F32)
            inner = jnp.sum(wide * normal[h], axis=-1, keepdims=True)
            high = inner.astype(BF).astype(F32)
            rest = inner - high
            wide = jnp.where(lane == hd, -high, jnp.where(lane == hd + 1, -rest, wide))
            do_out[r, h] = wide.astype(BF)
        db_values[...] += down(dwide)
        rows_of = [down(dh1), down(dy1 * n1), down(dy1), down(dh2), down(cot * n2), down(cot)]
        for i, row in enumerate(rows_of):
            sums[i : i + 1, :] += row
        return 0

    lax.fori_loop(0, rows, one_row, 0)
    for b in range(parts):
        out = send_out if b % 2 else keep_out
        kind = out.dtype
        c = b // 2
        cols = slice(b * units, (b + 1) * units)
        at = 0
        out[c, at : at + per, :] = dw_out[b * per : (b + 1) * per, :].astype(kind)
        at += per
        out[c, at : at + half_model, 0:units] = dw_in[0:half_model, cols].astype(kind)
        out[c, at : at + half_model, units : 2 * units] = dw_in[half_model:, cols].astype(kind)
        at += half_model
        out[c, at : at + units, :] = dw_back[b * units : (b + 1) * units, :].astype(kind)
        at += units
        lines = [db_in[:, cols]] + [sums[k : k + 1, :].astype(BF) for k in range(6)]
        lines.append(db_values[:, 2 * per * b : 2 * per * b + per])
        out[c, at : at + 16, :] = stacked(lines, model).astype(kind)


def middle(os, xs, cotangent, ws, vectors, heads):
    parts = len(ws)
    rows, here, model = cotangent.shape
    hd = model // heads
    width = model // parts
    size = ws[0].shape[0]
    units = size - 16 - width - model // 2
    return call(
        functools.partial(middle_kernel, parts, heads, rows),
        "middle",
        (*os, *xs, cotangent, *ws, *vectors),
        [
            (cotangent.shape, BF),
            ((parts // 2, size, model), F32),
            ((parts // 2, size, model), BF),
            ((rows, here, model), F32),
            ((rows, heads, here, 2 * hd), BF),
        ],
        [
            ((parts * width, model), BF),
            ((2 * parts * width, model), BF),
            ((model, parts * units), BF),
            ((parts * units, model), BF),
            ((parts * width, model), F32),
            ((model, parts * units), F32),
            ((parts * units, model), F32),
            ((1, parts * units), F32),
            ((1, 2 * model), F32),
            ((8, model), F32),
        ],
        flops=rows * 6 * here * model * (2 * model + 2 * parts * units),
        limit=LIMITS[1],
    )


def heads_step(row, n, pairs, ref):
    er_in, kvr_in, do_in, weight_in, ds = (ref[k] for k in ("er", "kvr", "do", "weight", "ds"))
    hd = kvr_in.shape[2] // 2
    half = kvr_in.shape[3]
    ones = value_ones(hd, half, 2)

    def one_head(step, _):
        h = 2 * pairs[0] + step
        i = step % 2

        def pick(name):
            found = [ref[name, pair][row, i] for pair in pairs]
            return found[0] if len(pairs) == 1 else jnp.where(step < 2, *found)

        kvs, es, do = (pick("kvl"), kvr_in[n, h]), (pick("el"), er_in[n, h]), do_in[row, h]
        dos = (do * weight_in[n, h], do)
        for side in range(2):
            cols = slice(side * half, (side + 1) * half)
            values = jnp.concatenate([kvs[side][hd:], ones], axis=0)
            dp = mm(dos[side], values, NN)
            ds[:, cols] = (dp * es[side].astype(F32)).astype(BF)
            ref["dkv", pairs[0]][step, hd:, cols] = mm(dos[side], es[side], TN)[:hd].astype(BF)
        ref["dkv", pairs[0]][step, :hd, :] = mm(pick("qt"), ds[...], NN).astype(BF)
        keys = jnp.concatenate([kv[:hd] for kv in kvs], axis=1)
        ref["dq", pairs[0]][step] = (mm(keys, ds[...], NT) * (hd**-0.5)).astype(BF)
        return 0

    lax.fori_loop(0, 2 * len(pairs), one_head, 0)


def joined(refs, cols):
    return jnp.concatenate([ref[h, :, cols] for ref in refs for h in range(ref.shape[0])], axis=0)


def inputs_step(row, parts, ref):
    dkvs, dqs = [[ref[k] for k in ref if k[0] == name] for name in ("dkv", "dq")]
    w_q, w_kv = ref["w_q"], ref["w_kv"]
    hd = w_q.shape[0] // parts
    here = dqs[0].shape[2]
    at = here + 16
    for b in range(parts):
        w = ref["w", b]
        w_q[b * hd : (b + 1) * hd, :] = w[at : at + hd, :]
        w_kv[b * 2 * hd : (b + 1) * 2 * hd, :] = w[at + hd : at + 3 * hd, :]
    for b in range(parts):
        dx = mm(joined(dkvs, slice(b * here, (b + 1) * here)), w_kv[...], TN)
        if b == 0:
            own = mm(joined(dqs, slice(0, here)), w_q[...], TN)
            ref["dx_own"][...] = dx + own + ref["dh1"][row]
        elif b % 2:
            if ("dx_send",) in ref:
                ref["dx_send"][b // 2] = dx.astype(BF)
            else:
                ref["dx_same" if b == 1 else "dx_cross"][...] = dx.astype(BF)
        else:
            ref["dx_keep"][...] = dx


def weights_step(row, heads, parts, ref):
    all_dkv, all_dq = [
        [ref[k].at[h] for k in sorted(k for k in ref if k[0] == name) for h in range(ref[k].shape[0])]
        for name in ("dkv", "dq")
    ]
    dkvs = [all_dkv[h] for h in heads]
    dq = jnp.concatenate([all_dq[h][...] for h in heads], axis=0)
    here = dq.shape[1]
    model = ref["x", 0].shape[1]
    hd = model // parts
    at = (row - 1) * (here + 16) if row else 0
    gkv = None
    for b in range(parts):
        left = jnp.concatenate([d[:, b * here : (b + 1) * here] for d in dkvs], axis=0)
        term = mm(left, ref["x", b][at : at + here, :], NN)
        gkv = term if gkv is None else gkv + term
    gq = mm(dq, ref["x", 0][at : at + here, :], NN)
    bq = mm(jnp.ones((8, here), BF), dq, NT)[0:1]
    out = ref["grads",]
    for c, h in enumerate(heads):
        pieces = [
            (slice(0, hd), gq[c * hd : (c + 1) * hd]),
            (slice(hd, 3 * hd), gkv[c * 2 * hd : (c + 1) * 2 * hd]),
            (slice(3 * hd, 3 * hd + 16), stacked([bq[:, c * hd : (c + 1) * hd]], model)),
        ]
        for rows, value in pieces:
            if ("grads_in",) in ref:
                value = value + ref["grads_in",][h, rows, :]
            out[c, rows, :] = value.astype(out.dtype)


def backward_kernel(names, row, n, pairs, parts, want, some, *refs):
    ref = {name if len(name) > 1 else name[0]: r for name, r in zip(names, refs)}
    ref.update({name: r for name, r in zip(names, refs) if len(name) == 1})
    if pairs:
        heads_step(row, n, pairs, ref)
    if "weights" in want:
        weights_step(row, some, parts, ref)
    if "inputs" in want:
        inputs_step(row, parts, ref)


def backward(row, n, pairs, want, ins, some=(0, 1, 2, 3), kind=F32, joint=False):
    parts = 4
    el = ins["el", 0]
    here, half = el.shape[2:]
    length = 2 * half
    hd = ins["kvl", 0].shape[2] // 2
    model = ins["x", 0].shape[1]
    size = 3 * hd + 16
    use = set()
    outs, scratch = {}, {}
    for pair in pairs:
        use |= {("el", pair), ("kvl", pair), ("qt", pair), ("er",), ("kvr",), ("do",), ("weight",)}
        scratch["ds",] = ((here, length), BF)
    if pairs:
        outs["dkv", pairs[0]] = ((2 * len(pairs), 2 * hd, length), BF)
        outs["dq", pairs[0]] = ((2 * len(pairs), hd, here), BF)
    if want:
        use |= {k for k in ins if k[0] in ("dkv", "dq")}
    if "inputs" in want:
        use |= {("w", b) for b in range(parts)} | {("dh1",)}
        outs["dx_own",] = ((here, model), F32)
        outs["dx_keep",] = ((here, model), F32)
        if joint:
            outs["dx_send",] = ((parts // 2, here, model), BF)
        else:
            outs["dx_same",] = ((here, model), BF)
            outs["dx_cross",] = ((here, model), BF)
        scratch["w_kv",] = ((2 * model, model), BF)
        scratch["w_q",] = ((model, model), BF)
    if "weights" in want:
        use |= {("x", b) for b in range(parts)}
        if ("grads_in",) in ins:
            use.add(("grads_in",))
        outs["grads",] = ((len(some), size, model), kind)
    order = sorted(use, key=str)
    names = tuple(order) + tuple(outs) + tuple(scratch)
    done = call(
        functools.partial(backward_kernel, names, row, n, pairs, parts, want, some),
        "backward",
        [ins[name] for name in order],
        list(outs.values()),
        list(scratch.values()),
        limit=LIMITS[2],
    )
    return dict(zip(outs, done))


def add_kernel(rows, *refs):
    owns, nears, fars, out = refs[:rows], refs[rows : 2 * rows], refs[2 * rows : -1], refs[-1]
    for r in range(rows):
        out[r] = owns[r][...] + nears[r][...].astype(F32) + fars[r][...].astype(F32)


def add_inputs(owns, nears, fars):
    rows = len(owns)
    (out,) = call(
        functools.partial(add_kernel, rows),
        "add_inputs",
        (*owns, *nears, *fars),
        [((rows,) + owns[0].shape, F32)],
        limit=LIMITS[3],
    )
    return out


def finish_one_kernel(a, b, values, qkv, bias):
    width = qkv.shape[1]
    total = a[...].astype(F32) + b[...].astype(F32)
    for c in range(3):
        qkv[c] = total[c * width : (c + 1) * width]
    bias[0:1, :] = total[3 * width : 3 * width + 1, 0:width]
    bias[1:2, :] = values[:, 0:width]


def finish_two_kernel(a, b, w_out, w_in, b_in, w_back, values, *sums):
    width, model = w_out.shape
    units = w_back.shape[0]
    half = model // 2
    total = a[...].astype(F32) + b[...].astype(F32)
    w_out[...] = total[:width]
    at = width
    w_in[0:half, :] = total[at : at + half, 0:units]
    w_in[half:, :] = total[at : at + half, units : 2 * units]
    at += half
    w_back[...] = total[at : at + units]
    at += units
    b_in[...] = total[at : at + 1, 0:units]
    values[...] = total[at + 7 : at + 8]
    for i, out in enumerate(sums):
        out[...] = total[at + 1 + i : at + 2 + i]


def swap(value, axis, size, bit):
    return lax.ppermute(value, axis, [(i, i ^ bit) for i in range(size)])


def after(value, *others):
    return lax.optimization_barrier((value, *others))[0]


def layer(mesh_sizes, *args):
    (inputs, segments, w_qkv, b_qv, w_out, b_out, gain_one, shift_one) = args[:8]
    (w_in, b_in, w_back, b_back, gain_two, shift_two, cotangent) = args[8:]
    dp, mp = mesh_sizes
    rows, here, model = inputs.shape
    heads = HEADS
    width = w_qkv.shape[2]
    units = w_in.shape[1]

    def near(value):
        return swap(value, "mp", mp, 1)

    def far(value):
        return swap(value, "mp", mp, 2)

    first, *later, two, biases = pack(
        w_qkv, b_qv, w_out, b_out, w_in, b_in, w_back, b_back, segments, inputs
    )
    vectors = [v.reshape(1, model) for v in (gain_one, shift_one, gain_two, shift_two)]
    vectors.append(biases)
    hd = model // heads
    first_far = far(first)
    first_near = near(first)
    mine, nears, fars = [first], [first_near], [first_far]
    if rows > 1:
        nears.append(near(later[0]))
        fars.append(far(after(later[0], first_near)))
        mine.append(later[0])
    two_far = far(after(two, nears[-1]))
    two_near = near(after(two, nears[-1]))
    locals_of = [attend_local(mine, nears, (first, first_near), rows, here, hd)]
    first_both = near(after(first_far, locals_of[0][2]))
    boths = [first_both]
    ws = (first, first_near, first_far, first_both)
    locals_of.append(attend_local(mine, nears, ws[2:], rows, here, hd))
    queries, outs = zip(*[out[3:5] for out in locals_of])
    remotes = []
    for c, rows_of in enumerate([[0], list(range(1, rows))][: min(rows, 2)]):
        if c == 1:
            boths.append(near(after(fars[1], remotes[0][2])))
        xs = [fars[c], boths[c]]
        remotes.append(attend_remote(rows_of, queries, outs, xs, ws, here, hd))
    blocks = [[group[min(r, 1)] for group in (mine, nears, fars, boths)] for r in range(rows)]
    two_both = near(after(two_far, remotes[-1][2]))
    result, keep_two, send_two, dh1s, dos = middle(
        [out[2] for out in remotes],
        mine,
        cotangent,
        [two, two_near, two_far, two_both],
        vectors,
        heads,
    )

    def over_dp(value, even, odd):
        for bits in zip(even, odd):
            pairs = []
            for d in range(dp):
                for m in range(mp):
                    pairs.append((d * mp + m, (d ^ bits[m % 2]) * mp + m))
            sent = value.astype(BF)
            got = lax.ppermute(sent, ("dp", "mp"), pairs)
            yield sent, got
            value = sent.astype(F32) + got.astype(F32)

    bits = [1 << k for k in range(dp.bit_length() - 1)]


    def inputs_of(r, **more):
        er, kvr, _, weight = remotes[min(r, 1)]
        ins = {("er",): er, ("kvr",): kvr, ("weight",): weight, ("do",): dos, ("dh1",): dh1s}
        for pair in range(heads // 2):
            names = (("el", pair), ("kvl", pair), ("qt", pair))
            ins.update(zip(names, locals_of[pair][:3]))
        for b in range(mp):
            ins["w", b] = ws[b]
            ins["x", b] = blocks[r][b]
        return ins

    def hold(ins, *ready):
        name = next(n for n in (("er",), ("dh1",)) if n in ins)
        ins[name] = after(ins[name], *ready)
        return ins

    def run(r, pairs, want, ins, **more):
        return backward(r, max(r - 1, 0), pairs, want, ins, **more)

    got_two = near(send_two)
    other_two = steps_two = step_two = None
    grads = None
    owns, near_got, far_got = [], [], []
    ready = []
    both = tuple(range(heads // 2))
    for r in range(rows):
        last = r == rows - 1
        ins = inputs_of(r)
        if ready:
            hold(ins, *ready)
        if r == 0:
            ins.update(run(0, both[:1], (), ins))
            got_two = after(got_two, ins["dkv", 0])
            other_two = (keep_two[1] + got_two[1].astype(F32)).astype(BF)
            far_two = far(other_two)
            hold(ins, other_two)
            ins.update(run(0, both[1:], () if last else ("inputs",), ins))
        else:
            ins.update(run(r, both, (), ins))
            flag = ins["dkv", 0]
            if r > 1 or last:
                far_got[-1] = after(far_got[-1], flag)
        flag = ins["dkv", 1] if r == 0 else ins["dkv", 0]
        if steps_two is None:
            value_two = (keep_two[0] + got_two[0].astype(F32)).astype(BF).astype(F32)
            value_two = value_two + after(far_two, flag).astype(F32)
            steps_two = over_dp(value_two, bits[::-1], bits[::-1])
            step_two = next(steps_two)
            tie = (step_two[0],)
        else:
            tie = (step_two[1], *far_got)
        if grads is not None:
            ins["grads_in",] = grads
        if last:
            break
        if r:
            ins["dh1",] = after(ins["dh1",], *tie)
            ins.update(run(r, (), ("inputs",), ins))
        got = near(ins["dx_cross",] if r else after(ins["dx_cross",], *tie))
        owns.append(ins["dx_own",])
        ins["x", 0] = after(ins["x", 0], ins["dx_cross",])
        grads = run(r, (), ("weights",), ins)["grads",]
        got = after(got, grads)
        near_got.append(near(after(ins["dx_same",], got)))
        other = (ins["dx_keep",] + got.astype(F32)).astype(BF)
        far_got.append(far(other))
        ready = [other, step_two[0]]
    ins["x", 0] = after(ins["x", 0], *tie)
    send = run(r, (), ("weights",), ins, some=(1, 3), kind=BF)["grads",]
    got = near(send)
    ins["x", 0] = after(ins["x", 0], send)
    keep = run(r, (), ("weights",), ins, some=(0, 2))["grads",]
    mine_one = keep[0] + got[0].astype(F32)
    other_one = (keep[1] + got[1].astype(F32)).astype(BF)
    far_one = far(other_one)
    ins["dh1",] = after(ins["dh1",], other_one)
    row = run(r, (), ("inputs",), ins, joint=True)
    got = near(after(row["dx_send",], other_one))
    owns.append(row["dx_own",])
    near_got.append(got[0])
    value_one = mine_one + far_one.astype(F32)
    total_one = None
    for k, total_one in enumerate(over_dp(value_one, bits, bits)):
        if k == 0:
            other = (row["dx_keep",] + after(got[1], total_one[0]).astype(F32)).astype(BF)
            far_got.append(far(other))
    total_two = step_two
    for total_two in steps_two:
        pass
    grad_inputs = add_inputs(owns, near_got, far_got)
    grad_out, grad_in, grad_b_in, grad_back, values, *sums = call(
        finish_two_kernel,
        "finish_two",
        total_two,
        [
            ((width, model), F32),
            ((model, units), F32),
            ((1, units), F32),
            ((units, model), F32),
        ]
        + [((1, model), F32)] * 7,
    )
    grad_qkv, grad_bias = call(
        finish_one_kernel,
        "finish_one",
        (after(total_one[0], grad_inputs), total_one[1], values),
        [((3, width, model), F32), ((2, width), F32)],
    )
    sums = [s.reshape(model) for s in sums]
    return (
        result,
        grad_inputs,
        grad_qkv.transpose(0, 2, 1),
        grad_bias,
        grad_out,
        sums[0],
        sums[1],
        sums[2],
        grad_in,
        grad_b_in.reshape(units),
        grad_back,
        sums[3],
        sums[4],
        sums[5],
    )


def solution(mesh):
    in_specs = (
        P("dp", "mp", None),
        P("dp", "mp"),
        P(None, None, "mp"),
        P(None, "mp"),
        P("mp", None),
        P(),
        P(),
        P(),
        P(None, "mp"),
        P("mp"),
        P("mp", None),
        P(),
        P(),
        P(),
        P("dp", "mp", None),
    )
    out_specs = (
        P("dp", "mp", None),
        P("dp", "mp", None),
        P(None, None, "mp"),
        P(None, "mp"),
        P("mp", None),
        P(),
        P(),
        P(),
        P(None, "mp"),
        P("mp"),
        P("mp", None),
        P(),
        P(),
        P(),
    )
    sizes = (mesh.shape["dp"], mesh.shape["mp"])
    return jax.shard_map(
        functools.partial(layer, sizes),
        mesh=mesh,
        in_specs=in_specs,
        out_specs=out_specs,
        check_vma=False,
    )
```

```python
import functools

import jax
import jax.numpy as jnp
from jax import lax
from jax.experimental import pallas as pl
from jax.experimental.pallas import tpu as pltpu
from jax.sharding import PartitionSpec as P

HEADS = 4
EPS = 1e-06
FAR = -(2.0**99)
GELU_C = 0.7978845608028654
GELU_A = 0.044715
LOG2_E = 1.4426950408889634
LN_2 = 0.6931471805599453

BF = jnp.bfloat16
F32 = jnp.float32

NN = (((1,), (0,)), ((), ()))
NT = (((1,), (1,)), ((), ()))
TN = (((0,), (0,)), ((), ()))

MB = 2**20
LIMITS = (10, 12, 8, 8)


def mm(left, right, dims):
    return lax.dot_general(left, right, dims, preferred_element_type=F32)


def call(kernel, name, args, outs, scratch=(), flops=0, limit=20):
    whole = pl.BlockSpec(memory_space=pltpu.VMEM)
    return pl.pallas_call(
        kernel,
        out_shape=[jax.ShapeDtypeStruct(shape, kind) for shape, kind in outs],
        in_specs=[whole] * len(args),
        out_specs=[whole] * len(outs),
        scratch_shapes=[pltpu.VMEM(shape, kind) for shape, kind in scratch],
        compiler_params=pltpu.CompilerParams(vmem_limit_bytes=limit * MB),
        cost_estimate=pl.CostEstimate(flops=flops // 20, bytes_accessed=0, transcendentals=0),
        name=name,
    )(*args)


def stacked(lines, width):
    place = lax.broadcasted_iota(jnp.int32, (16, width), 0)
    out = jnp.zeros((16, width), F32)
    for k, line in enumerate(lines):
        line = line.astype(F32)
        if line.shape[1] < width:
            fill = jnp.zeros((1, width - line.shape[1]), F32)
            line = jnp.concatenate([line, fill], axis=1)
        out = jnp.where(place == k, jnp.broadcast_to(line, (16, width)), out)
    return out


def pack_kernel(rows, *refs):
    w_qkv, b_qv, w_out, b_out, w_in, b_in, w_back, b_back, segs, x, first = refs[:11]
    later, two, biases = refs[11:-2], refs[-2], refs[-1]
    biases[...] = jnp.zeros(biases.shape, F32)
    biases[0:1, :] = b_out[...].astype(F32).reshape(1, -1)
    biases[1:2, :] = b_back[...].astype(F32).reshape(1, -1)
    width, model = w_qkv.shape[1:]
    units = w_in.shape[1]
    half = model // 2
    here = x.shape[1]
    for r in range(rows):
        out = later[0] if r else first
        at = (r - 1) * (here + 16) if r else 0
        out[at : at + here, :] = x[r]
        at += here
        seg = segs[r : r + 1, :]
        digits = [jnp.bitwise_and(seg, 31), jnp.right_shift(seg, 5)]
        lines = [d[:, k : k + model] for d in digits for k in range(0, here, model)]
        out[at : at + 16, :] = stacked(lines, model).astype(BF)
    at = here + 16
    for c in range(3):
        first[at : at + width, :] = w_qkv[c]
        at += width
    both = b_qv[...].astype(F32)
    line = jnp.concatenate([both[0:1], both[1:2]], axis=1)
    first[at : at + 16, :] = stacked([line], model).astype(BF)
    two[0:width, :] = w_out[...]
    at = width
    two[at : at + half, 0:units] = w_in[0:half, :]
    two[at : at + half, units : 2 * units] = w_in[half:, :]
    at += half
    two[at : at + units, :] = w_back[...]
    at += units
    two[at : at + 16, :] = stacked([b_in[...]], model).astype(BF)


def pack(w_qkv, b_qv, w_out, b_out, w_in, b_in, w_back, b_back, segments, inputs):
    width, units, model = w_qkv.shape[2], w_in.shape[1], w_in.shape[0]
    rows, here = segments.shape
    sizes = [here + 16 + 3 * width + 16]
    if rows > 1:
        sizes.append((rows - 1) * (here + 16))
    sizes.append(width + model // 2 + units + 16)
    args = (
        w_qkv.transpose(0, 2, 1),
        b_qv,
        w_out,
        b_out,
        w_in,
        b_in.reshape(1, units),
        w_back,
        b_back,
        segments,
        inputs,
    )
    return call(
        functools.partial(pack_kernel, rows),
        "pack",
        [pltpu.with_memory_space_constraint(a, pltpu.HBM) for a in args],
        [((size, model), BF) for size in sizes] + [((8, model), F32)],
    )


def load_weights(ws, here, hd, w_q, w_kv, bias):
    at = here + 16
    for i, w in enumerate(ws):
        w_q[i * hd : (i + 1) * hd, :] = w[at : at + hd, :]
        w_kv[i * 2 * hd : (i + 1) * 2 * hd, :] = w[at + hd : at + 3 * hd, :]
        line = w[at + 3 * hd : at + 3 * hd + 16, 0 : 2 * hd].astype(F32)[0:1]
        bias[i] = jnp.broadcast_to(line, (2 * hd, 2 * hd)).T


def same_cell(x, at, here, hd):
    per = here // x.shape[1]
    block = x[at : at + 16, :].astype(F32)
    low = [block[i : i + 1] for i in range(per)]
    high = [block[per + i : per + i + 1] for i in range(per)]
    low, high = jnp.concatenate(low, axis=1), jnp.concatenate(high, axis=1)
    lane = lax.broadcasted_iota(jnp.int32, (hd, here), 0).astype(F32)
    return lane == jnp.where(lane < 32, low, high + 32.0)


def value_ones(hd, length, count):
    return (lax.broadcasted_iota(jnp.int32, (hd, length), 0) < count).astype(F32).astype(BF)


def attend(queries, kvs, feats, before, put):
    hd = kvs[0].shape[0] // 2
    length = kvs[0].shape[1]
    ones = value_ones(hd, length, hd)

    def score(i):
        scores = mm(queries[i], jnp.concatenate([kvs[i][:hd], feats[i]], axis=0), NN)
        top = jnp.max(scores, axis=-1, keepdims=True)
        top = jnp.broadcast_to(top, (scores.shape[0], 2 * hd))
        if before is None:
            return scores, top, None
        old = before(i)
        steps = jnp.maximum(jnp.ceil((top - old) * LOG2_E), 0.0)
        return scores, old + steps * LN_2, jnp.exp2(-steps)

    later = score(0)
    for i in range(len(queries)):
        scores, top, weight = later
        if i + 1 < len(queries):
            later = score(i + 1)
        wide = jnp.concatenate([top] * (length // (2 * hd)), axis=1)
        expo = jnp.exp(scores - wide).astype(BF)
        out = mm(expo, jnp.concatenate([kvs[i][hd:], ones], axis=0), NT)
        put(i, expo, out, top, weight)


def project(x, w, bias, put):
    hd = bias.shape[1] // 2
    proj = mm(w, x, NT)
    for i in range(w.shape[0] // (2 * hd)):
        at = 2 * i * hd
        keys = proj[at : at + hd].astype(BF)
        values = (proj[at + hd : at + 2 * hd] + bias[i, hd:, 0:1]).astype(BF)
        put(i, keys, values)


def local_kernel(rows, here, hd, *refs):
    count = 2 if rows > 1 else 1
    mine, nears = refs[:count], refs[count : 2 * count]
    ws = refs[2 * count : 2 * count + 2]
    e_out, kv_out, qt_out, qa_out, o_out = refs[2 * count + 2 : 2 * count + 7]
    w_q, w_kv, bias, feats = refs[2 * count + 7 :]
    load_weights(ws, here, hd, w_q, w_kv, bias)
    for r in range(rows):
        at = (r - 1) * (here + 16) if r else 0
        pair = (mine[min(r, 1)], nears[min(r, 1)])
        for b, x in enumerate(pair):
            same = same_cell(x, at + here, here, hd)
            feats[r, :, b * here : (b + 1) * here] = jnp.where(same, 0.0, FAR).astype(BF)
            if b == 0:
                first = same.astype(F32)

        def put(i, keys, values, r=r):
            kv_out[r, i, :hd, :] = keys
            kv_out[r, i, hd:, :] = values

        block = jnp.concatenate([x[at : at + here, :] for x in pair], axis=0)
        project(block, w_kv[...], bias, put)
        proj = mm(w_q[...], pair[0][at : at + here, :], NT)
        for i in range(2):
            qt = proj[i * hd : (i + 1) * hd] + bias[i, :hd, 0:1]
            qt = qt.astype(BF).astype(F32) * (hd**-0.5)
            qt_out[r, i] = qt.astype(BF)
            qa_out[r, i] = jnp.concatenate([qt, first], axis=0).T.astype(BF)

    lane = lax.broadcasted_iota(jnp.int32, (here, 2 * hd), 1)

    def put(k, expo, out, top, _):
        e_out[k // 2, k % 2] = expo
        o_out[k // 2, k % 2] = jnp.where(lane < 3 * hd // 2, out, top)

    queries = [qa_out[r, i] for r in range(rows) for i in range(2)]
    kvs = [kv_out[r, i] for r in range(rows) for i in range(2)]
    attend(queries, kvs, [feats[r] for r in range(rows) for i in range(2)], None, put)


def attend_local(mine, nears, ws, rows, here, hd):
    model = mine[0].shape[1]
    return call(
        functools.partial(local_kernel, rows, here, hd),
        "attend_local",
        (*mine, *nears, *ws),
        [
            ((rows, 2, here, 2 * here), BF),
            ((rows, 2, 2 * hd, 2 * here), BF),
            ((rows, 2, hd, here), BF),
            ((rows, 2, here, 2 * hd), BF),
            ((rows, 2, here, 2 * hd), F32),
        ],
        [
            ((2 * hd, model), BF),
            ((4 * hd, model), BF),
            ((2, 2 * hd, 2 * hd), F32),
            ((rows, hd, 2 * here), BF),
        ],
        flops=1,
        limit=LIMITS[0],
    )


def remote_kernel(rows, here, hd, *refs):
    qs, os, xs, ws = refs[:2], refs[2:4], refs[4:6], refs[6:10]
    e_out, kv_out, o_out, weight_out, w_q, w_kv, bias, feats = refs[10:]
    heads = len(ws)
    load_weights(ws, here, hd, w_q, w_kv, bias)
    for n, row in enumerate(rows):
        at = (row - 1) * (here + 16) if row else 0
        for b, x in enumerate(xs):
            same = same_cell(x, at + here, here, hd)
            feats[n, :, b * here : (b + 1) * here] = jnp.where(same, 0.0, FAR).astype(BF)

        def put(i, keys, values, n=n):
            kv_out[n, i, :hd, :] = keys
            kv_out[n, i, hd:, :] = values

        block = jnp.concatenate([x[at : at + here, :] for x in xs], axis=0)
        project(block, w_kv[...], bias, put)

    def one_row(n, _):
        r = rows[0] + n

        def put(h, expo, out, _, weight):
            e_out[n, h] = expo
            o_out[n, h] = out + os[h // 2][r, h % 2] * weight
            weight_out[n, h] = weight.astype(BF)

        queries = [qs[h // 2][r, h % 2] for h in range(heads)]
        at = 3 * hd // 2

        def before(h):
            return jnp.broadcast_to(os[h // 2][r, h % 2, :, at : at + 1], (here, 2 * hd))

        attend(queries, [kv_out[n, h] for h in range(heads)], [feats[n]] * heads, before, put)
        return 0

    lax.fori_loop(0, len(rows), one_row, 0)


def attend_remote(rows, queries, outs, xs, ws, here, hd):
    model = xs[0].shape[1]
    heads = len(ws)
    count = len(rows)
    return call(
        functools.partial(remote_kernel, rows, here, hd),
        "attend_remote",
        (*queries, *outs, *xs, *ws),
        [
            ((count, heads, here, 2 * here), BF),
            ((count, heads, 2 * hd, 2 * here), BF),
            ((count, heads, here, 2 * hd), F32),
            ((count, heads, here, 2 * hd), BF),
        ],
        [
            ((heads * hd, model), BF),
            ((heads * 2 * hd, model), BF),
            ((heads, 2 * hd, 2 * hd), F32),
            ((count, hd, 2 * here), BF),
        ],
        flops=1,
        limit=LIMITS[0],
    )


def middle_kernel(parts, heads, rows, *refs):
    groups = min(rows, 2)
    os, xs = refs[:groups], refs[groups : 2 * groups]
    at = 2 * groups
    cot_in = refs[at]
    ws = refs[at + 1 : at + 1 + parts]
    at += 1 + parts
    g_one, e_one, g_two, e_two, biases = refs[at : at + 5]
    result_out, keep_out, send_out, dh1_out, do_out = refs[at + 5 : at + 10]
    w_out, w_pad, w_in, w_back = refs[at + 10 : at + 14]
    dw_out, dw_in, dw_back, db_in, db_values, sums = refs[at + 14 :]
    w_pad[...] = jnp.zeros(w_pad.shape, BF)
    here, model = cot_in.shape[1:]
    hd = model // heads
    per = w_out.shape[0] // parts
    units = w_back.shape[0] // parts
    half_model = model // 2
    bias = []
    for b in range(parts):
        at = 0
        w_out[b * per : (b + 1) * per, :] = ws[b][at : at + per, :]
        w_pad[b * 2 * per : b * 2 * per + per, :] = ws[b][at : at + per, :]
        at += per
        cols = slice(b * units, (b + 1) * units)
        w_in[0:half_model, cols] = ws[b][at : at + half_model, 0:units]
        w_in[half_model:, cols] = ws[b][at : at + half_model, units : 2 * units]
        at += half_model
        w_back[b * units : (b + 1) * units, :] = ws[b][at : at + units, :]
        at += units
        bias.append(ws[b][at : at + 16, 0:units].astype(F32)[0:1])
    b_in = jnp.concatenate(bias, axis=1)
    lane = lax.broadcasted_iota(jnp.int32, (here, 2 * hd), 1)

    def o_of(r, h):
        if groups == 1:
            return os[0][r, h]
        return jnp.where(r == 0, os[0][0, h], os[1][jnp.maximum(r - 1, 0), h])

    def x_of(r):
        first = xs[0][0:here, :].astype(F32)
        if groups == 1:
            return first
        at = pl.multiple_of(jnp.maximum(r - 1, 0) * (here + 16), 16)
        return jnp.where(r == 0, first, xs[1][pl.ds(at, here), :].astype(F32))

    for total in (dw_out, dw_in, dw_back, db_in, db_values, sums):
        total[...] = jnp.zeros(total.shape, F32)

    def norm(h):
        centre = h - jnp.mean(h, axis=-1, keepdims=True)
        rstd = lax.rsqrt(jnp.mean(centre * centre, axis=-1, keepdims=True) + EPS)
        return centre * rstd, rstd

    def norm_back(dy, gain, unit, rstd):
        dn = dy * gain
        mean = jnp.mean(dn, axis=-1, keepdims=True)
        along = jnp.mean(dn * unit, axis=-1, keepdims=True)
        return rstd * (dn - mean - unit * along)

    def down(v):
        return jnp.sum(v, axis=0, keepdims=True)

    def one_row(r, _):
        o_in = [o_of(r, h) for h in range(heads)]
        inv = [1.0 / o[:, hd : hd + 1] for o in o_in]
        normal = [o * i for o, i in zip(o_in, inv)]
        tiles = [
            jnp.where(lane < hd, normal[h], pltpu.roll(normal[h + 1], hd, 1))
            for h in range(0, heads, 2)
        ]
        att = jnp.concatenate(tiles, axis=1).astype(BF)
        h1 = x_of(r) + mm(att, w_out[...], NN) + biases[0:1, :]
        n1, rstd1 = norm(h1)
        y1 = n1 * g_one[...] + e_one[...]
        y1b = y1.astype(BF)
        pre = mm(y1b, w_in[...], NN) + b_in
        square = pre * pre
        half = 0.5 + 0.5 * jnp.tanh(pre * (GELU_C + GELU_C * GELU_A * square))
        full = pre * half
        act = full.astype(BF)
        slope = half + full * (1.0 - half) * (2.0 * GELU_C + 6.0 * GELU_C * GELU_A * square)
        h2 = y1 + mm(act, w_back[...], NN) + biases[1:2, :]
        n2, rstd2 = norm(h2)
        result_out[r] = (n2 * g_two[...] + e_two[...]).astype(BF)
        cot = cot_in[r].astype(F32)
        dh2 = norm_back(cot, g_two[...], n2, rstd2)
        dz = dh2.astype(BF)
        dact = mm(dz, w_back[...], NT)
        dpre = (dact * slope).astype(BF)
        dw_back[...] += mm(act, dz, TN)
        dw_in[...] += mm(y1b, dpre, TN)
        db_in[...] += down(dpre.astype(F32))
        dy1 = mm(dpre, w_in[...], NT) + dh2
        dh1 = norm_back(dy1, g_one[...], n1, rstd1)
        dh1_out[r] = dh1
        da = dh1.astype(BF)
        dw_out[...] += mm(att, da, TN)
        dwide = mm(da, w_pad[...], NT)
        for h in range(heads):
            grad = (dwide[:, 2 * hd * h : 2 * hd * (h + 1)] * inv[h]).astype(BF)
            wide = grad.astype(F32)
            inner = jnp.sum(wide * normal[h], axis=-1, keepdims=True)
            high = inner.astype(BF).astype(F32)
            rest = inner - high
            wide = jnp.where(lane == hd, -high, jnp.where(lane == hd + 1, -rest, wide))
            do_out[r, h] = wide.astype(BF)
        db_values[...] += down(dwide)
        rows_of = [down(dh1), down(dy1 * n1), down(dy1), down(dh2), down(cot * n2), down(cot)]
        for i, row in enumerate(rows_of):
            sums[i : i + 1, :] += row
        return 0

    lax.fori_loop(0, rows, one_row, 0)
    for b in range(parts):
        out = send_out if b % 2 else keep_out
        kind = out.dtype
        c = b // 2
        cols = slice(b * units, (b + 1) * units)
        at = 0
        out[c, at : at + per, :] = dw_out[b * per : (b + 1) * per, :].astype(kind)
        at += per
        out[c, at : at + half_model, 0:units] = dw_in[0:half_model, cols].astype(kind)
        out[c, at : at + half_model, units : 2 * units] = dw_in[half_model:, cols].astype(kind)
        at += half_model
        out[c, at : at + units, :] = dw_back[b * units : (b + 1) * units, :].astype(kind)
        at += units
        lines = [db_in[:, cols]] + [sums[k : k + 1, :].astype(BF) for k in range(6)]
        lines.append(db_values[:, 2 * per * b : 2 * per * b + per])
        out[c, at : at + 16, :] = stacked(lines, model).astype(kind)


def middle(os, xs, cotangent, ws, vectors, heads):
    parts = len(ws)
    rows, here, model = cotangent.shape
    hd = model // heads
    width = model // parts
    size = ws[0].shape[0]
    units = size - 16 - width - model // 2
    return call(
        functools.partial(middle_kernel, parts, heads, rows),
        "middle",
        (*os, *xs, cotangent, *ws, *vectors),
        [
            (cotangent.shape, BF),
            ((parts // 2, size, model), F32),
            ((parts // 2, size, model), BF),
            ((rows, here, model), F32),
            ((rows, heads, here, 2 * hd), BF),
        ],
        [
            ((parts * width, model), BF),
            ((2 * parts * width, model), BF),
            ((model, parts * units), BF),
            ((parts * units, model), BF),
            ((parts * width, model), F32),
            ((model, parts * units), F32),
            ((parts * units, model), F32),
            ((1, parts * units), F32),
            ((1, 2 * model), F32),
            ((8, model), F32),
        ],
        flops=rows * 6 * here * model * (2 * model + 2 * parts * units),
        limit=LIMITS[1],
    )


def heads_step(row, n, pairs, ref):
    er_in, kvr_in, do_in, weight_in, ds = (ref[k] for k in ("er", "kvr", "do", "weight", "ds"))
    hd = kvr_in.shape[2] // 2
    half = kvr_in.shape[3]
    ones = value_ones(hd, half, 2)

    def one_head(step, _):
        h = 2 * pairs[0] + step
        i = step % 2

        def pick(name):
            found = [ref[name, pair][row, i] for pair in pairs]
            return found[0] if len(pairs) == 1 else jnp.where(step < 2, *found)

        kvs, es, do = (pick("kvl"), kvr_in[n, h]), (pick("el"), er_in[n, h]), do_in[row, h]
        dos = (do * weight_in[n, h], do)
        for side in range(2):
            cols = slice(side * half, (side + 1) * half)
            values = jnp.concatenate([kvs[side][hd:], ones], axis=0)
            dp = mm(dos[side], values, NN)
            ds[:, cols] = (dp * es[side].astype(F32)).astype(BF)
            ref["dkv", pairs[0]][step, hd:, cols] = mm(dos[side], es[side], TN)[:hd].astype(BF)
        ref["dkv", pairs[0]][step, :hd, :] = mm(pick("qt"), ds[...], NN).astype(BF)
        keys = jnp.concatenate([kv[:hd] for kv in kvs], axis=1)
        ref["dq", pairs[0]][step] = (mm(keys, ds[...], NT) * (hd**-0.5)).astype(BF)
        return 0

    lax.fori_loop(0, 2 * len(pairs), one_head, 0)


def joined(refs, cols):
    return jnp.concatenate([ref[h, :, cols] for ref in refs for h in range(ref.shape[0])], axis=0)


def inputs_step(row, parts, ref):
    dkvs, dqs = [[ref[k] for k in ref if k[0] == name] for name in ("dkv", "dq")]
    w_q, w_kv = ref["w_q"], ref["w_kv"]
    hd = w_q.shape[0] // parts
    here = dqs[0].shape[2]
    at = here + 16
    for b in range(parts):
        w = ref["w", b]
        w_q[b * hd : (b + 1) * hd, :] = w[at : at + hd, :]
        w_kv[b * 2 * hd : (b + 1) * 2 * hd, :] = w[at + hd : at + 3 * hd, :]
    for b in range(parts):
        dx = mm(joined(dkvs, slice(b * here, (b + 1) * here)), w_kv[...], TN)
        if b == 0:
            own = mm(joined(dqs, slice(0, here)), w_q[...], TN)
            ref["dx_own"][...] = dx + own + ref["dh1"][row]
        elif b % 2:
            if ("dx_send",) in ref:
                ref["dx_send"][b // 2] = dx.astype(BF)
            else:
                ref["dx_same" if b == 1 else "dx_cross"][...] = dx.astype(BF)
        else:
            ref["dx_keep"][...] = dx


def weights_step(row, heads, parts, ref):
    all_dkv, all_dq = [
        [ref[k].at[h] for k in sorted(k for k in ref if k[0] == name) for h in range(ref[k].shape[0])]
        for name in ("dkv", "dq")
    ]
    dkvs = [all_dkv[h] for h in heads]
    dq = jnp.concatenate([all_dq[h][...] for h in heads], axis=0)
    here = dq.shape[1]
    model = ref["x", 0].shape[1]
    hd = model // parts
    at = (row - 1) * (here + 16) if row else 0
    gkv = None
    for b in range(parts):
        left = jnp.concatenate([d[:, b * here : (b + 1) * here] for d in dkvs], axis=0)
        term = mm(left, ref["x", b][at : at + here, :], NN)
        gkv = term if gkv is None else gkv + term
    gq = mm(dq, ref["x", 0][at : at + here, :], NN)
    bq = mm(jnp.ones((8, here), BF), dq, NT)[0:1]
    out = ref["grads",]
    for c, h in enumerate(heads):
        pieces = [
            (slice(0, hd), gq[c * hd : (c + 1) * hd]),
            (slice(hd, 3 * hd), gkv[c * 2 * hd : (c + 1) * 2 * hd]),
            (slice(3 * hd, 3 * hd + 16), stacked([bq[:, c * hd : (c + 1) * hd]], model)),
        ]
        for rows, value in pieces:
            if ("grads_in",) in ref:
                value = value + ref["grads_in",][h, rows, :]
            out[c, rows, :] = value.astype(out.dtype)


def backward_kernel(names, row, n, pairs, parts, want, some, *refs):
    ref = {name if len(name) > 1 else name[0]: r for name, r in zip(names, refs)}
    ref.update({name: r for name, r in zip(names, refs) if len(name) == 1})
    if pairs:
        heads_step(row, n, pairs, ref)
    if "weights" in want:
        weights_step(row, some, parts, ref)
    if "inputs" in want:
        inputs_step(row, parts, ref)


def backward(row, n, pairs, want, ins, some=(0, 1, 2, 3), kind=F32, joint=False):
    parts = 4
    el = ins["el", 0]
    here, half = el.shape[2:]
    length = 2 * half
    hd = ins["kvl", 0].shape[2] // 2
    model = ins["x", 0].shape[1]
    size = 3 * hd + 16
    use = set()
    outs, scratch = {}, {}
    for pair in pairs:
        use |= {("el", pair), ("kvl", pair), ("qt", pair), ("er",), ("kvr",), ("do",), ("weight",)}
        scratch["ds",] = ((here, length), BF)
    if pairs:
        outs["dkv", pairs[0]] = ((2 * len(pairs), 2 * hd, length), BF)
        outs["dq", pairs[0]] = ((2 * len(pairs), hd, here), BF)
    if want:
        use |= {k for k in ins if k[0] in ("dkv", "dq")}
    if "inputs" in want:
        use |= {("w", b) for b in range(parts)} | {("dh1",)}
        outs["dx_own",] = ((here, model), F32)
        outs["dx_keep",] = ((here, model), F32)
        if joint:
            outs["dx_send",] = ((parts // 2, here, model), BF)
        else:
            outs["dx_same",] = ((here, model), BF)
            outs["dx_cross",] = ((here, model), BF)
        scratch["w_kv",] = ((2 * model, model), BF)
        scratch["w_q",] = ((model, model), BF)
    if "weights" in want:
        use |= {("x", b) for b in range(parts)}
        if ("grads_in",) in ins:
            use.add(("grads_in",))
        outs["grads",] = ((len(some), size, model), kind)
    order = sorted(use, key=str)
    names = tuple(order) + tuple(outs) + tuple(scratch)
    done = call(
        functools.partial(backward_kernel, names, row, n, pairs, parts, want, some),
        "backward",
        [ins[name] for name in order],
        list(outs.values()),
        list(scratch.values()),
        limit=LIMITS[2],
    )
    return dict(zip(outs, done))


def add_kernel(rows, *refs):
    owns, nears, fars, out = refs[:rows], refs[rows : 2 * rows], refs[2 * rows : -1], refs[-1]
    for r in range(rows):
        out[r] = owns[r][...] + nears[r][...].astype(F32) + fars[r][...].astype(F32)


def add_inputs(owns, nears, fars):
    rows = len(owns)
    (out,) = call(
        functools.partial(add_kernel, rows),
        "add_inputs",
        (*owns, *nears, *fars),
        [((rows,) + owns[0].shape, F32)],
        limit=LIMITS[3],
    )
    return out


def finish_one_kernel(a, b, values, qkv, bias):
    width = qkv.shape[1]
    total = a[...].astype(F32) + b[...].astype(F32)
    for c in range(3):
        qkv[c] = total[c * width : (c + 1) * width]
    bias[0:1, :] = total[3 * width : 3 * width + 1, 0:width]
    bias[1:2, :] = values[:, 0:width]


def finish_two_kernel(a, b, w_out, w_in, b_in, w_back, values, *sums):
    width, model = w_out.shape
    units = w_back.shape[0]
    half = model // 2
    total = a[...].astype(F32) + b[...].astype(F32)
    w_out[...] = total[:width]
    at = width
    w_in[0:half, :] = total[at : at + half, 0:units]
    w_in[half:, :] = total[at : at + half, units : 2 * units]
    at += half
    w_back[...] = total[at : at + units]
    at += units
    b_in[...] = total[at : at + 1, 0:units]
    values[...] = total[at + 7 : at + 8]
    for i, out in enumerate(sums):
        out[...] = total[at + 1 + i : at + 2 + i]


def swap(value, axis, size, bit):
    return lax.ppermute(value, axis, [(i, i ^ bit) for i in range(size)])


def after(value, *others):
    return lax.optimization_barrier((value, *others))[0]


def layer(mesh_sizes, *args):
    (inputs, segments, w_qkv, b_qv, w_out, b_out, gain_one, shift_one) = args[:8]
    (w_in, b_in, w_back, b_back, gain_two, shift_two, cotangent) = args[8:]
    dp, mp = mesh_sizes
    rows, here, model = inputs.shape
    heads = HEADS
    width = w_qkv.shape[2]
    units = w_in.shape[1]

    def near(value):
        return swap(value, "mp", mp, 1)

    def far(value):
        return swap(value, "mp", mp, 2)

    first, *later, two, biases = pack(
        w_qkv, b_qv, w_out, b_out, w_in, b_in, w_back, b_back, segments, inputs
    )
    vectors = [v.reshape(1, model) for v in (gain_one, shift_one, gain_two, shift_two)]
    vectors.append(biases)
    hd = model // heads
    first_far = far(first)
    first_near = near(first)
    mine, nears, fars = [first], [first_near], [first_far]
    if rows > 1:
        nears.append(near(later[0]))
        fars.append(far(after(later[0], first_near)))
        mine.append(later[0])
    two_far = far(after(two, nears[-1]))
    two_near = near(after(two, nears[-1]))
    locals_of = [attend_local(mine, nears, (first, first_near), rows, here, hd)]
    first_both = near(after(first_far, locals_of[0][2]))
    boths = [first_both]
    ws = (first, first_near, first_far, first_both)
    locals_of.append(attend_local(mine, nears, ws[2:], rows, here, hd))
    queries, outs = zip(*[out[3:5] for out in locals_of])
    remotes = []
    for c, rows_of in enumerate([[0], list(range(1, rows))][: min(rows, 2)]):
        if c == 1:
            boths.append(near(after(fars[1], remotes[0][2])))
        xs = [fars[c], boths[c]]
        remotes.append(attend_remote(rows_of, queries, outs, xs, ws, here, hd))
    blocks = [[group[min(r, 1)] for group in (mine, nears, fars, boths)] for r in range(rows)]
    two_both = near(after(two_far, remotes[-1][2]))
    result, keep_two, send_two, dh1s, dos = middle(
        [out[2] for out in remotes],
        mine,
        cotangent,
        [two, two_near, two_far, two_both],
        vectors,
        heads,
    )

    def over_dp(value, even, odd):
        for bits in zip(even, odd):
            pairs = []
            for d in range(dp):
                for m in range(mp):
                    pairs.append((d * mp + m, (d ^ bits[m % 2]) * mp + m))
            sent = value.astype(BF)
            got = lax.ppermute(sent, ("dp", "mp"), pairs)
            yield sent, got
            value = sent.astype(F32) + got.astype(F32)

    bits = [1 << k for k in range(dp.bit_length() - 1)]


    def inputs_of(r, **more):
        er, kvr, _, weight = remotes[min(r, 1)]
        ins = {("er",): er, ("kvr",): kvr, ("weight",): weight, ("do",): dos, ("dh1",): dh1s}
        for pair in range(heads // 2):
            names = (("el", pair), ("kvl", pair), ("qt", pair))
            ins.update(zip(names, locals_of[pair][:3]))
        for b in range(mp):
            ins["w", b] = ws[b]
            ins["x", b] = blocks[r][b]
        return ins

    def hold(ins, *ready):
        name = next(n for n in (("er",), ("dh1",)) if n in ins)
        ins[name] = after(ins[name], *ready)
        return ins

    def run(r, pairs, want, ins, **more):
        return backward(r, max(r - 1, 0), pairs, want, ins, **more)

    got_two = near(send_two)
    other_two = steps_two = step_two = None
    grads = None
    owns, near_got, far_got = [], [], []
    ready = []
    both = tuple(range(heads // 2))
    for r in range(rows):
        last = r == rows - 1
        ins = inputs_of(r)
        if ready:
            hold(ins, *ready)
        if r == 0:
            ins.update(run(0, both[:1], (), ins))
            got_two = after(got_two, ins["dkv", 0])
            other_two = (keep_two[1] + got_two[1].astype(F32)).astype(BF)
            far_two = far(other_two)
            hold(ins, other_two)
            ins.update(run(0, both[1:], () if last else ("inputs",), ins))
        else:
            ins.update(run(r, both, (), ins))
            flag = ins["dkv", 0]
            if r > 1 or last:
                far_got[-1] = after(far_got[-1], flag)
        flag = ins["dkv", 1] if r == 0 else ins["dkv", 0]
        if steps_two is None:
            value_two = (keep_two[0] + got_two[0].astype(F32)).astype(BF).astype(F32)
            value_two = value_two + after(far_two, flag).astype(F32)
            steps_two = over_dp(value_two, bits[::-1], bits[::-1])
            step_two = next(steps_two)
            tie = (step_two[0],)
        else:
            tie = (step_two[1], *far_got)
        if grads is not None:
            ins["grads_in",] = grads
        if last:
            break
        if r:
            ins["dh1",] = after(ins["dh1",], *tie)
            ins.update(run(r, (), ("inputs",), ins))
        got = near(ins["dx_cross",] if r else after(ins["dx_cross",], *tie))
        owns.append(ins["dx_own",])
        ins["x", 0] = after(ins["x", 0], ins["dx_cross",])
        grads = run(r, (), ("weights",), ins)["grads",]
        got = after(got, grads)
        near_got.append(near(after(ins["dx_same",], got)))
        other = (ins["dx_keep",] + got.astype(F32)).astype(BF)
        far_got.append(far(other))
        ready = [other, step_two[0]]
    ins["x", 0] = after(ins["x", 0], *tie)
    send = run(r, (), ("weights",), ins, some=(1, 3), kind=BF)["grads",]
    got = near(send)
    ins["x", 0] = after(ins["x", 0], send)
    keep = run(r, (), ("weights",), ins, some=(0, 2))["grads",]
    mine_one = keep[0] + got[0].astype(F32)
    other_one = (keep[1] + got[1].astype(F32)).astype(BF)
    far_one = far(other_one)
    ins["dh1",] = after(ins["dh1",], other_one)
    row = run(r, (), ("inputs",), ins, joint=True)
    got = near(after(row["dx_send",], other_one))
    owns.append(row["dx_own",])
    near_got.append(got[0])
    value_one = mine_one + far_one.astype(F32)
    total_one = None
    for k, total_one in enumerate(over_dp(value_one, bits, bits)):
        if k == 0:
            other = (row["dx_keep",] + after(got[1], total_one[0]).astype(F32)).astype(BF)
            far_got.append(far(other))
    total_two = step_two
    for total_two in steps_two:
        pass
    grad_inputs = add_inputs(owns, near_got, far_got)
    grad_out, grad_in, grad_b_in, grad_back, values, *sums = call(
        finish_two_kernel,
        "finish_two",
        total_two,
        [
            ((width, model), F32),
            ((model, units), F32),
            ((1, units), F32),
            ((units, model), F32),
        ]
        + [((1, model), F32)] * 7,
    )
    grad_qkv, grad_bias = call(
        finish_one_kernel,
        "finish_one",
        (after(total_one[0], grad_inputs), total_one[1], values),
        [((3, width, model), F32), ((2, width), F32)],
    )
    sums = [s.reshape(model) for s in sums]
    return (
        result,
        grad_inputs,
        grad_qkv.transpose(0, 2, 1),
        grad_bias,
        grad_out,
        sums[0],
        sums[1],
        sums[2],
        grad_in,
        grad_b_in.reshape(units),
        grad_back,
        sums[3],
        sums[4],
        sums[5],
    )


def solution(mesh):
    in_specs = (
        P("dp", "mp", None),
        P("dp", "mp"),
        P(None, None, "mp"),
        P(None, "mp"),
        P("mp", None),
        P(),
        P(),
        P(),
        P(None, "mp"),
        P("mp"),
        P("mp", None),
        P(),
        P(),
        P(),
        P("dp", "mp", None),
    )
    out_specs = (
        P("dp", "mp", None),
        P("dp", "mp", None),
        P(None, None, "mp"),
        P(None, "mp"),
        P("mp", None),
        P(),
        P(),
        P(),
        P(None, "mp"),
        P("mp"),
        P("mp", None),
        P(),
        P(),
        P(),
    )
    sizes = (mesh.shape["dp"], mesh.shape["mp"])
    return jax.shard_map(
        functools.partial(layer, sizes),
        mesh=mesh,
        in_specs=in_specs,
        out_specs=out_specs,
        check_vma=False,
    )
```
